32 devices in a mesh: dp: 8 (over z, x), mp: 4 (over y, core).
Axes of the slice: x: 2, y: 2, z: 4, core: 2. Of those that a mesh axis runs over, the one named last changes fastest.
Arguments:
- block_in: bfloat16 [2, 1024, 16, 768], P(None, ('dp', 'mp')), may hold values from -6 to 6
- seq_lengths: int32 [2, 1024], P(None, ('dp', 'mp')), may hold values from 1 to 16, as said below
- image_embed: bfloat16 [2, 1024, 768], P(None, ('dp', 'mp')), may hold values from -6 to 6
- w_qkv: float32 [768, 3, 768], P('dp', None, 'mp'), may hold values from -0.21875 to 0.21875
- w_out: float32 [768, 768], P('dp', 'mp'), may hold values from -0.4375 to 0.4375
- w_up: float32 [768, 3072], P('dp', 'mp'), may hold values from -0.21875 to 0.21875
- w_down: float32 [768, 3072], P('dp', 'mp'), may hold values from -0.109375 to 0.109375
- norm_params: float32 [768, 4], replicated, as said below
- norm_second: float32 [768, 4], P('dp'), may hold values from 16384 to 65536
- qkv_left: float32 [8, 4, 96, 96], P('dp', 'mp'), as said below
- qkv_right: float32 [8, 4, 576, 576], P('dp', 'mp'), as said below
- qkv_left_root: float32 [8, 4, 96, 96], P('dp', 'mp'), as said below
- qkv_right_root: float32 [8, 4, 576, 576], P('dp', 'mp'), as said below
- out_left: float32 [8, 4, 96, 96], P('dp', 'mp'), as said below
- out_right: float32 [8, 4, 192, 192], P('dp', 'mp'), as said below
- out_left_root: float32 [8, 4, 96, 96], P('dp', 'mp'), as said below
- out_right_root: float32 [8, 4, 192, 192], P('dp', 'mp'), as said below
- up_left: float32 [8, 4, 96, 96], P('dp', 'mp'), as said below
- up_right: float32 [8, 4, 768, 768], P('dp', 'mp'), as said below
- up_left_root: float32 [8, 4, 96, 96], P('dp', 'mp'), as said below
- up_right_root: float32 [8, 4, 768, 768], P('dp', 'mp'), as said below
- down_left: float32 [8, 4, 96, 96], P('dp', 'mp'), as said below
- down_right: float32 [8, 4, 768, 768], P('dp', 'mp'), as said below
- down_left_root: float32 [8, 4, 96, 96], P('dp', 'mp'), as said below
- down_right_root: float32 [8, 4, 768, 768], P('dp', 'mp'), as said below
Outputs:
- block_out: bfloat16 [2, 1024, 16, 768], P(None, ('dp', 'mp'))
- input_grad: float32 [2, 1024, 16, 768], P(None, ('dp', 'mp'))
- text_loss: float32 [2, 1024], P(None, ('dp', 'mp'))
- qkv_grad: float32 [768, 3, 768], P('dp', None, 'mp')
- qkv_left_new: float32 [8, 4, 96, 96], P('dp', 'mp')
- qkv_right_new: float32 [8, 4, 576, 576], P('dp', 'mp')
- qkv_new: float32 [768, 3, 768], P('dp', None, 'mp')
- out_grad: float32 [768, 768], P('dp', 'mp')
- out_left_new: float32 [8, 4, 96, 96], P('dp', 'mp')
- out_right_new: float32 [8, 4, 192, 192], P('dp', 'mp')
- out_new: float32 [768, 768], P('dp', 'mp')
- up_grad: float32 [768, 3072], P('dp', 'mp')
- up_left_new: float32 [8, 4, 96, 96], P('dp', 'mp')
- up_right_new: float32 [8, 4, 768, 768], P('dp', 'mp')
- up_new: float32 [768, 3072], P('dp', 'mp')
- down_grad: float32 [768, 3072], P('dp', 'mp')
- down_left_new: float32 [8, 4, 96, 96], P('dp', 'mp')
- down_right_new: float32 [8, 4, 768, 768], P('dp', 'mp')
- down_new: float32 [768, 3072], P('dp', 'mp')
- norm_grad: float32 [768, 4], P('dp')
- norm_second_new: float32 [768, 4], P('dp')
- norm_new: float32 [768, 4], P('dp')
The draws below stay inside these ranges and needn't reach their ends.
Inputs may be any that keep to these rules, and one draw needn't show every extreme that they name: seq_lengths[m, 1023] = 16 in every micro-batch. `qkv_left`: symmetric positive definite blocks. `qkv_right`: symmetric positive definite blocks. `qkv_left_root`: symmetric positive definite blocks. `qkv_right_root`: symmetric positive definite blocks. `out_left`: symmetric positive definite blocks. `out_right`: symmetric positive definite blocks. `out_left_root`: symmetric positive definite blocks. `out_right_root`: symmetric positive definite blocks. `up_left`: symmetric positive definite blocks. `up_right`: symmetric positive definite blocks. `up_left_root`: symmetric positive definite blocks. `up_right_root`: symmetric positive definite blocks. `down_left`: symmetric positive definite blocks. `down_right`: symmetric positive definite blocks. `down_left_root`: symmetric positive definite blocks. `down_right_root`: symmetric positive definite blocks. `norm_params`: gains (columns 0 and 2) are positive.
All inputs are finite; a program needn't handle non-finite values.
Results may differ from the reference program's by a relative error of at most 0.022.
Values may be sent and summed in bfloat16 or wider, within the bound.
No kernel may reach another device: no remote copies, remote signals or barrier semaphores. Data moves between devices by JAX's collectives and lax.ppermute only.
A program may use at most 256 MiB of HBM per device.

```python
import math
import jax
import jax.numpy as jnp
from jax import lax

MODEL_DIM = 768
HD = 64
FF = 3072
LEN = 16
MB = 2
NSEQ = 1024
TOKENS = 32768
HL = 3
ATD = 192
QKC = 576
FFD = 768
RB = 96
DPN = 8
MPN = 4
N_DP = 8
N_MP = 4


def stat_matrix(key, size, scale):
    diag_key, off_key = jax.random.split(key)
    diagonal = scale * jnp.exp(jax.random.uniform(diag_key, (DPN, MPN, size), jnp.float32, 0.0, math.log(4.0)))
    mixing = jax.random.uniform(off_key, (DPN, MPN, size, size), jnp.float32, -1.0, 1.0) * (0.3 * scale / size)
    mixing = 0.5 * (mixing + jnp.swapaxes(mixing, -1, -2))
    identity = jnp.eye(size, dtype=jnp.float32)
    return mixing * (1.0 - identity) + diagonal[..., :, None] * identity


def root_matrix(key, size, scale):
    diag_key, off_key = jax.random.split(key)
    diagonal = scale * jnp.exp(jax.random.uniform(diag_key, (DPN, MPN, size), jnp.float32, 0.0, math.log(2.0)))
    mixing = jax.random.uniform(off_key, (DPN, MPN, size, size), jnp.float32, -1.0, 1.0) * (0.5 * scale / size)
    mixing = 0.5 * (mixing + jnp.swapaxes(mixing, -1, -2))
    identity = jnp.eye(size, dtype=jnp.float32)
    return mixing * (1.0 - identity) + diagonal[..., :, None] * identity


def grad_power():
    return 160.0 * TOKENS / MODEL_DIM


def root_power():
    return TOKENS / 8.0


def draw_seq_lengths(key, part):
    key = jax.random.fold_in(key, 11)
    positions = jnp.arange(NSEQ, dtype=jnp.int32)
    ceiling = jnp.minimum(LEN * (NSEQ + 2 * positions) // (3 * NSEQ) + 1, LEN)
    drawn = jax.random.randint(key, (MB, NSEQ), 1, ceiling[None, :] + 1)
    return jnp.where(positions[None, :] == NSEQ - 1, LEN, drawn).astype(jnp.int32)


def draw_norm_params(key, part):
    key = jax.random.fold_in(key, 12)
    gain_key, shift_key = jax.random.split(key)
    gains = jnp.exp(jax.random.uniform(gain_key, (MODEL_DIM, 4), jnp.float32, math.log(0.5), math.log(2.0)))
    shifts = 0.5 * jax.random.normal(shift_key, (MODEL_DIM, 4), jnp.float32)
    columns = jnp.arange(4)[None, :]
    return jnp.where(columns % 2 == 0, gains, shifts)


def draw_qkv_left(key, part):
    key = jax.random.fold_in(key, 21)
    return stat_matrix(key, RB, QKC * grad_power())


def draw_qkv_right(key, part):
    key = jax.random.fold_in(key, 22)
    return stat_matrix(key, QKC, RB * grad_power())


def draw_qkv_left_root(key, part):
    key = jax.random.fold_in(key, 23)
    return root_matrix(key, RB, (QKC * root_power()) ** (-0.25))


def draw_qkv_right_root(key, part):
    key = jax.random.fold_in(key, 24)
    return root_matrix(key, QKC, (RB * root_power()) ** (-0.25))


def draw_out_left(key, part):
    key = jax.random.fold_in(key, 31)
    return stat_matrix(key, RB, ATD * grad_power())


def draw_out_right(key, part):
    key = jax.random.fold_in(key, 32)
    return stat_matrix(key, ATD, RB * grad_power())


def draw_out_left_root(key, part):
    key = jax.random.fold_in(key, 33)
    return root_matrix(key, RB, (ATD * root_power()) ** (-0.25))


def draw_out_right_root(key, part):
    key = jax.random.fold_in(key, 34)
    return root_matrix(key, ATD, (RB * root_power()) ** (-0.25))


def draw_up_left(key, part):
    key = jax.random.fold_in(key, 41)
    return stat_matrix(key, RB, FFD * grad_power())


def draw_up_right(key, part):
    key = jax.random.fold_in(key, 42)
    return stat_matrix(key, FFD, RB * grad_power())


def draw_up_left_root(key, part):
    key = jax.random.fold_in(key, 43)
    return root_matrix(key, RB, (FFD * root_power()) ** (-0.25))


def draw_up_right_root(key, part):
    key = jax.random.fold_in(key, 44)
    return root_matrix(key, FFD, (RB * root_power()) ** (-0.25))


def draw_down_left(key, part):
    key = jax.random.fold_in(key, 51)
    return stat_matrix(key, RB, FFD * grad_power())


def draw_down_right(key, part):
    key = jax.random.fold_in(key, 52)
    return stat_matrix(key, FFD, RB * grad_power())


def draw_down_left_root(key, part):
    key = jax.random.fold_in(key, 53)
    return root_matrix(key, RB, (FFD * root_power()) ** (-0.25))


def draw_down_right_root(key, part):
    key = jax.random.fold_in(key, 54)
    return root_matrix(key, FFD, (RB * root_power()) ** (-0.25))


def block_scale(rng, extent, cuts, low, top_value):
    loudness, own = 1.0, jax.random.fold_in(rng, 6)
    for axis_at, blocks in cuts:
        heights = jnp.exp(jax.random.uniform(jax.random.fold_in(own, axis_at), (blocks,), jnp.float32, low / len(cuts), top_value / len(cuts)))
        loudness = loudness * jnp.repeat(heights, extent[axis_at] // blocks).reshape([-1 if axis == axis_at else 1 for axis in range(len(extent))])
    return loudness


def scatter_about(key, dims, scale, bound, cuts=(), held_as=jnp.bfloat16):
    factor_of = block_scale(key, dims, cuts, -0.22, 0.18) if cuts else 1.0
    values = jax.random.normal(key, dims, jnp.float32) * scale * factor_of
    return jnp.minimum(jnp.maximum(values, -bound), bound).astype(held_as)


def setup_inputs(seed: int = 0) -> dict:
    key_list = jax.random.split(jax.random.key(seed), 26)
    block_in = scatter_about(key_list[0], (MB, NSEQ, LEN, MODEL_DIM), 1.0, 6.0, ((1, 32),))
    seq_lengths = draw_seq_lengths(jax.random.fold_in(key_list[25], 71), 0)
    image_embed = scatter_about(key_list[2], (MB, NSEQ, MODEL_DIM), 1.0, 6.0, ((1, 32),))
    w_qkv = scatter_about(key_list[3], (MODEL_DIM, 3, MODEL_DIM), MODEL_DIM ** -0.5, 0.21875, ((0, 8), (2, 4)), jnp.float32)
    w_out = scatter_about(key_list[4], (MODEL_DIM, MODEL_DIM), (MODEL_DIM // 4) ** -0.5, 0.4375, ((0, 8), (1, 4)), jnp.float32)
    w_up = scatter_about(key_list[5], (MODEL_DIM, FF), MODEL_DIM ** -0.5, 0.21875, ((0, 8), (1, 4)), jnp.float32)
    w_down = scatter_about(key_list[6], (MODEL_DIM, FF), FF ** -0.5, 0.109375, ((0, 8), (1, 4)), jnp.float32)
    norm_params = draw_norm_params(jax.random.fold_in(key_list[25], 71), 0)
    norm_second = jnp.clip(jnp.exp(math.log(65536.0) - 1.3862944 * jax.random.uniform(key_list[8], (MODEL_DIM, 4), jnp.float32) ** block_scale(key_list[8], (MODEL_DIM, 4), ((0, 8),), -0.2, 0.2)), 16384.0, 65536.0)
    qkv_left = draw_qkv_left(jax.random.fold_in(key_list[25], 71), 0)
    qkv_right = draw_qkv_right(jax.random.fold_in(key_list[25], 71), 0)
    qkv_left_root = draw_qkv_left_root(jax.random.fold_in(key_list[25], 71), 0)
    qkv_right_root = draw_qkv_right_root(jax.random.fold_in(key_list[25], 71), 0)
    out_left = draw_out_left(jax.random.fold_in(key_list[25], 71), 0)
    out_right = draw_out_right(jax.random.fold_in(key_list[25], 71), 0)
    out_left_root = draw_out_left_root(jax.random.fold_in(key_list[25], 71), 0)
    out_right_root = draw_out_right_root(jax.random.fold_in(key_list[25], 71), 0)
    up_left = draw_up_left(jax.random.fold_in(key_list[25], 71), 0)
    up_right = draw_up_right(jax.random.fold_in(key_list[25], 71), 0)
    up_left_root = draw_up_left_root(jax.random.fold_in(key_list[25], 71), 0)
    up_right_root = draw_up_right_root(jax.random.fold_in(key_list[25], 71), 0)
    down_left = draw_down_left(jax.random.fold_in(key_list[25], 71), 0)
    down_right = draw_down_right(jax.random.fold_in(key_list[25], 71), 0)
    down_left_root = draw_down_left_root(jax.random.fold_in(key_list[25], 71), 0)
    down_right_root = draw_down_right_root(jax.random.fold_in(key_list[25], 71), 0)
    return dict(block_in=block_in, seq_lengths=seq_lengths, image_embed=image_embed, w_qkv=w_qkv, w_out=w_out, w_up=w_up, w_down=w_down, norm_params=norm_params, norm_second=norm_second, qkv_left=qkv_left, qkv_right=qkv_right, qkv_left_root=qkv_left_root, qkv_right_root=qkv_right_root, out_left=out_left, out_right=out_right, out_left_root=out_left_root, out_right_root=out_right_root, up_left=up_left, up_right=up_right, up_left_root=up_left_root, up_right_root=up_right_root, down_left=down_left, down_right=down_right, down_left_root=down_left_root, down_right_root=down_right_root)


@jax.custom_vjp
def low(v):
    return lax.optimization_barrier(v.astype(jnp.bfloat16)).astype(jnp.float32)

@jax.custom_vjp
def lower_backward(v):
    return v

def low_keep(v):
    return (low(v), None)

def low_pass(kept, grad):
    return (grad,)

def back_keep(v):
    return (v, None)

def back_low(kept, grad):
    return (low(grad),)
low.defvjp(low_keep, low_pass)
lower_backward.defvjp(back_keep, back_low)
FULL_PRECISION = lax.Precision.HIGHEST
EPSILON = 1e-06
SOFTMAX_TEMP = 2.0
LOSS_SCALE = 32.0
STAT_DECAY = 0.5
SHAMPOO_RATE = 0.3
NORM_RATE = 0.5

def round_both(values):
    return low(lower_backward(values))

def layer_norm(values, norm_gain, norm_shift):
    center = values - lax.optimization_barrier(jnp.mean(values, axis=-1, keepdims=True))
    spread = lax.optimization_barrier(jnp.mean(center * center, axis=-1, keepdims=True))
    return center * lax.rsqrt(spread + EPSILON) * norm_gain + norm_shift

def shard_columns(weight, group_width):
    return weight.reshape(MODEL_DIM, N_MP, group_width).transpose(1, 0, 2)

def block_loss(params, block_rows, block_lengths, image_vectors, targets):
    w_qkv, w_out, w_up, w_down, norm_cols = params
    seq_count = block_rows.shape[0]
    token_count = seq_count * LEN
    inputs = block_rows.reshape(token_count, MODEL_DIM)
    qkv_cols = low(w_qkv).reshape(MODEL_DIM, 3, N_MP, ATD).transpose(2, 0, 1, 3).reshape(N_MP, MODEL_DIM, QKC)
    out_cols = shard_columns(low(w_out), ATD)
    up_cols = shard_columns(low(w_up), FFD)
    down_cols = shard_columns(low(w_down), FFD)
    normed = low(layer_norm(inputs, norm_cols[:, 0], norm_cols[:, 1]))
    normed_copies = lower_backward(jnp.broadcast_to(normed, (N_MP, token_count, MODEL_DIM)))
    projected = round_both(jnp.einsum('jtd,jdc->jtc', normed_copies, qkv_cols, precision=FULL_PRECISION))
    projected = projected.reshape(N_MP, seq_count, LEN, 3, HL, HD)
    queries = projected[:, :, :, 0]
    key_vecs = projected[:, :, :, 1]
    value_vecs = projected[:, :, :, 2]
    scores = lower_backward(jnp.einsum('jsqhe,jskhe->jshqk', queries, key_vecs, precision=FULL_PRECISION) * HD ** (-0.5))
    key_live = jnp.arange(LEN)[None, :] < block_lengths[:, None]
    scores = jnp.where(key_live[None, :, None, None, :], scores, -1e+30)
    attn_probs = low(jax.nn.softmax(scores, axis=-1))
    head_rows = round_both(jnp.einsum('jshqk,jskhe->jsqhe', attn_probs, value_vecs, precision=FULL_PRECISION))
    head_rows = head_rows.reshape(N_MP, token_count, ATD)
    attended = lax.optimization_barrier(jnp.sum(round_both(jnp.einsum('jtc,jdc->jtd', head_rows, out_cols, precision=FULL_PRECISION)), axis=0))
    middle = inputs + attended
    normed_two = low(layer_norm(middle, norm_cols[:, 2], norm_cols[:, 3]))
    normed_two_copies = lower_backward(jnp.broadcast_to(normed_two, (N_MP, token_count, MODEL_DIM)))
    up_rows = lower_backward(jnp.einsum('jtd,jdf->jtf', normed_two_copies, up_cols, precision=FULL_PRECISION))
    hidden = low(jax.nn.gelu(up_rows, approximate=False))
    mlp_result = lax.optimization_barrier(jnp.sum(round_both(jnp.einsum('jtf,jdf->jtd', hidden, down_cols, precision=FULL_PRECISION)), axis=0))
    outputs = (middle + mlp_result).reshape(seq_count, LEN, MODEL_DIM)
    live_mask = key_live.astype(jnp.float32)
    pooled = lax.optimization_barrier(jnp.sum(outputs * live_mask[:, :, None], axis=1)) / lax.optimization_barrier(jnp.sum(live_mask, axis=1))[:, None]
    text_vector = low(pooled * lax.rsqrt(lax.optimization_barrier(jnp.mean(pooled * pooled, axis=-1, keepdims=True)) + EPSILON))
    pair_logits = lower_backward(jnp.dot(text_vector, image_vectors.T, precision=FULL_PRECISION) * (SOFTMAX_TEMP / math.sqrt(MODEL_DIM)))
    totals = jax.scipy.special.logsumexp(pair_logits, axis=-1)
    positive = jnp.take_along_axis(pair_logits, targets[:, None], axis=1)[:, 0]
    losses = totals - positive
    return (LOSS_SCALE * jnp.sum(losses), (outputs, losses))

def owner_blocks(gradient, group_width):
    return gradient.reshape(N_DP, RB, N_MP, group_width).transpose(0, 2, 1, 3)

def from_blocks(blocks, group_width):
    return blocks.transpose(0, 2, 1, 3).reshape(MODEL_DIM, N_MP * group_width)

def qkv_blocks(weight):
    return weight.reshape(N_DP, RB, 3, N_MP, ATD).transpose(0, 3, 1, 2, 4).reshape(N_DP, N_MP, RB, QKC)

def qkv_unblock(blocks):
    return blocks.reshape(N_DP, N_MP, RB, 3, ATD).transpose(0, 2, 3, 1, 4).reshape(MODEL_DIM, 3, MODEL_DIM)

def shampoo(gradient, left_stat, right_stat, left_root, right_root, master):
    left_new = STAT_DECAY * left_stat + (1.0 - STAT_DECAY) * jnp.einsum('pjrc,pjsc->pjrs', gradient, gradient, precision=FULL_PRECISION)
    right_new = STAT_DECAY * right_stat + (1.0 - STAT_DECAY) * jnp.einsum('pjrc,pjrd->pjcd', gradient, gradient, precision=FULL_PRECISION)
    update = jnp.einsum('pjrs,pjsc->pjrc', left_root, gradient, precision=FULL_PRECISION)
    update = jnp.einsum('pjrc,pjcd->pjrd', update, right_root, precision=FULL_PRECISION)
    return (left_new, right_new, master - SHAMPOO_RATE * update)

def reference(block_in, seq_lengths, image_embed, w_qkv, w_out, w_up, w_down, norm_params, norm_second, qkv_left, qkv_right, qkv_left_root, qkv_right_root, out_left, out_right, out_left_root, out_right_root, up_left, up_right, up_left_root, up_right_root, down_left, down_right, down_left_root, down_right_root):
    block_size = math.gcd(NSEQ, 256)
    block_count = NSEQ // block_size
    checked_block = jax.checkpoint(block_loss)

    def objective(params, inputs_all):

        def per_micro(carry, items):
            micro_rows, micro_lengths, micro_images = items
            image_vectors = micro_images.astype(jnp.float32)
            targets = jnp.arange(NSEQ, dtype=jnp.int32).reshape(block_count, block_size)

            def per_block(inner, pieces):
                block_rows, block_lengths, block_targets = pieces
                value, (outputs, losses) = checked_block(params, block_rows, block_lengths, image_vectors, block_targets)
                return (inner + value, (outputs, losses))
            summed, (outputs, losses) = lax.scan(per_block, jnp.zeros((), jnp.float32), (micro_rows.reshape(block_count, block_size, LEN, MODEL_DIM), micro_lengths.reshape(block_count, block_size), targets))
            return (carry + summed, (outputs.reshape(NSEQ, LEN, MODEL_DIM), losses.reshape(NSEQ)))
        total_value, (outputs, losses) = lax.scan(per_micro, jnp.zeros((), jnp.float32), (inputs_all, seq_lengths, image_embed))
        return (total_value, (outputs, losses))
    params = (w_qkv, w_out, w_up, w_down, norm_params)
    inputs_all = block_in.astype(jnp.float32)
    total_value, backward, (outputs, losses) = jax.vjp(objective, params, inputs_all, has_aux=True)
    grads, input_grad = backward(jnp.ones((), jnp.float32))
    grad_qkv, grad_out, grad_up, grad_down, grad_norm = grads
    qkv_left_new, qkv_right_new, qkv_moved = shampoo(qkv_blocks(grad_qkv), qkv_left, qkv_right, qkv_left_root, qkv_right_root, qkv_blocks(w_qkv))
    out_left_new, out_right_new, out_moved = shampoo(owner_blocks(grad_out, ATD), out_left, out_right, out_left_root, out_right_root, owner_blocks(w_out, ATD))
    up_left_new, up_right_new, up_moved = shampoo(owner_blocks(grad_up, FFD), up_left, up_right, up_left_root, up_right_root, owner_blocks(w_up, FFD))
    down_left_new, down_right_new, down_moved = shampoo(owner_blocks(grad_down, FFD), down_left, down_right, down_left_root, down_right_root, owner_blocks(w_down, FFD))
    norm_second_new = STAT_DECAY * norm_second + (1.0 - STAT_DECAY) * grad_norm * grad_norm
    norm_new = norm_params - NORM_RATE * grad_norm / (jnp.sqrt(norm_second_new) + 1e-08)
    return (outputs.astype(jnp.bfloat16), input_grad, losses, grad_qkv, qkv_left_new, qkv_right_new, qkv_unblock(qkv_moved), grad_out, out_left_new, out_right_new, from_blocks(out_moved, ATD), grad_up, up_left_new, up_right_new, from_blocks(up_moved, FFD), grad_down, down_left_new, down_right_new, from_blocks(down_moved, FFD), grad_norm, norm_second_new, norm_new)
```

```python
import functools
import math

import jax
import jax.numpy as jnp
import numpy as np
from jax import lax
from jax.experimental import pallas as pl
from jax.experimental.pallas import tpu as pltpu
from jax.sharding import PartitionSpec as P

AXES = ("dp", "mp")
HD = 64
LANES = 128
EPSILON = 1e-06
SOFTMAX_TEMP = 2.0
LOSS_SCALE = 32.0
STAT_DECAY = 0.5
SHAMPOO_RATE = 0.3
NORM_RATE = 0.5
TILE = 256
VMEM_BYTES = 56 * 1024 * 1024
F32 = jnp.float32
BF16 = jnp.bfloat16


def exchange_steps(count):
    steps = []
    bit = count // 2
    while bit >= 8:
        steps.append([i ^ bit for i in range(count)])
        bit //= 2
    steps.append([i ^ (4 if i % 2 == 0 else 2) for i in range(count)])
    steps.append([i ^ (2 if i % 2 == 0 else 4) for i in range(count)])
    steps.append([i ^ 1 for i in range(count)])
    return steps


def source_table(count):
    table = np.arange(count)[:, None]
    for step in exchange_steps(count):
        table = np.concatenate([table, table[np.array(step)]], axis=1)
    return table


def swap(values, step):
    return lax.ppermute(values, AXES, list(enumerate(step)))


def gather_blocks(block, count):
    steps = exchange_steps(count)
    held = block[None]
    for step in steps[:-1]:
        held = jnp.concatenate([held, swap(held, step)], axis=0)
    return held, swap(held, steps[-1])


def sum_blocks(keep, send, count):
    steps = exchange_steps(count)
    received = swap(send, steps[-1])
    for step in steps[-2::-1]:
        half = keep.shape[0] // 2
        going = (keep[half:].astype(F32) + received[half:].astype(F32)).astype(BF16)
        keep = (keep[:half].astype(F32) + received[:half].astype(F32)).astype(BF16)
        received = swap(going, step)
    return keep[0].astype(F32) + received[0].astype(F32)


def dot(left, right, left_dim, right_dim):
    return lax.dot_general(
        left, right, (((left_dim,), (right_dim,)), ((), ())), preferred_element_type=F32
    )


def load_weights(order, own, other, weights, sems):
    half, rows, _ = own.shape
    groups = weights.shape[0]

    def start(q, base, ref):
        index = order[base + q]
        group = index % groups
        place = pl.multiple_of((index // groups) * rows, 16)
        pltpu.make_async_copy(
            ref.at[q], weights.at[group, pl.ds(place, rows), :], sems.at[group]
        ).start()

    def body(q, carry):
        start(q, 0, own)
        start(q, half, other)
        return carry

    lax.fori_loop(0, half, body, 0)


def wait_weights(weights, sems, group):
    pltpu.make_async_copy(weights.at[group], weights.at[group], sems.at[group]).wait()


def normalize(values):
    center = values - jnp.mean(values, axis=-1, keepdims=True)
    spread = jnp.mean(center * center, axis=-1, keepdims=True)
    scale = lax.rsqrt(spread + EPSILON)
    return center * scale, scale


def low_lanes(dtype=BF16):
    lane = lax.broadcasted_iota(jnp.int32, (1, LANES), 1)
    return jnp.where(lane < HD, 1.0, 0.0).astype(dtype)


def masked_scores(queries, keys, allowed):
    return jnp.where(allowed, dot(queries, keys, 1, 1) * (HD**-0.5), -1e30)


def allowed_pairs(key_live, seq_len):
    rows = lax.broadcasted_iota(jnp.int32, (LANES, LANES), 0) // seq_len
    cols = lax.broadcasted_iota(jnp.int32, (LANES, LANES), 1) // seq_len
    return jnp.logical_and(rows == cols, key_live > 0.0)


def attention_forward(
    order, x_ref, live_ref, norm_ref, own_ref, other_ref,
    h1_ref, proj_ref, heads_ref, lse_ref, mid_ref, h2_ref,
    weights, sems, *, seq_len,
):
    groups = weights.shape[0]
    first = pl.program_id(0) == 0

    @pl.when(first)
    def _():
        load_weights(order, own_ref, other_ref, weights, sems)

    x = x_ref[...].astype(F32)
    rows = x.shape[0]
    n1, _ = normalize(x)
    h1 = (n1 * norm_ref[0:1, :] + norm_ref[1:2, :]).astype(BF16)
    h1_ref[...] = h1
    low = low_lanes()
    high = 1 - low
    is_low = lax.broadcasted_iota(jnp.int32, (1, LANES), 1) < HD
    lane = lax.broadcasted_iota(jnp.int32, (1, LANES), 1)
    allowed = [allowed_pairs(live_ref[t], seq_len) for t in range(rows // LANES)]
    total = x
    lse_tiles = [jnp.zeros((LANES, LANES), F32) for _ in allowed]
    for group in range(groups):

        @pl.when(first)
        def _():
            wait_weights(weights, sems, group)

        proj = dot(h1, weights[group, :, : 5 * LANES], 1, 0).astype(BF16)
        proj_ref[:, group * 5 * LANES : (group + 1) * 5 * LANES] = proj
        parts = []
        for t, pairs in enumerate(allowed):
            b = [
                proj[t * LANES : (t + 1) * LANES, i * LANES : (i + 1) * LANES]
                for i in range(5)
            ]
            outs = []
            for h, (q, k, v) in enumerate(
                ((b[0] * low, b[1], b[2]), (b[0] * high, b[1], b[2]), (b[3] * low, b[4], b[3]))
            ):
                scores = masked_scores(q, k, pairs)
                top = jnp.max(scores, axis=1, keepdims=True)
                powers = jnp.exp(scores - top)
                total_power = jnp.sum(powers, axis=1, keepdims=True)
                lse_tiles[t] = jnp.where(
                    lane == group * 3 + h, top + jnp.log(total_power), lse_tiles[t]
                )
                probs = (powers * (1.0 / total_power)).astype(BF16)
                outs.append(dot(probs, v, 1, 0))
            parts.append(
                jnp.concatenate(
                    [jnp.where(is_low, 0.0, outs[2]), jnp.where(is_low, outs[0], outs[1])],
                    axis=1,
                ).astype(BF16)
            )
        heads = jnp.concatenate(parts, axis=0)
        heads_ref[:, group * 2 * LANES : (group + 1) * 2 * LANES] = heads
        total = total + dot(heads, weights[group, :, 4 * LANES :], 1, 1)
    for t, tile in enumerate(lse_tiles):
        lse_ref[t * LANES : (t + 1) * LANES, :] = tile
    mid_ref[...] = total
    n2, _ = normalize(total)
    h2_ref[...] = (n2 * norm_ref[2:3, :] + norm_ref[3:4, :]).astype(BF16)


def up_forward(
    order, h2_ref, live_ref, own_ref, other_ref,
    hid_ref, slope_ref, pooled_ref,
    weights, sems, *, seq_len,
):
    groups, _, width = weights.shape
    first = pl.program_id(0) == 0

    @pl.when(first)
    def _():
        load_weights(order, own_ref, other_ref, weights, sems)

    h2 = h2_ref[...]
    rows = h2.shape[0]
    live = live_ref[:, 0:1]
    seqs = rows // seq_len
    member = (
        lax.broadcasted_iota(jnp.int32, (seqs, rows), 1) // seq_len
        == lax.broadcasted_iota(jnp.int32, (seqs, rows), 0)
    )
    pool = jnp.where(member, 1.0, 0.0).astype(BF16)
    for group in range(groups):

        @pl.when(first)
        def _():
            wait_weights(weights, sems, group)

        cols = slice(group * width, (group + 1) * width)
        up = dot(h2, weights[group], 1, 0)
        gate = 0.5 + 0.5 * lax.erf(up * (0.5**0.5))
        hid = (up * gate).astype(BF16)
        hid_ref[:, cols] = hid
        bell = jnp.exp(up * up * -0.5) * (1.0 / math.sqrt(2.0 * math.pi))
        slope_ref[:, cols] = ((gate + up * bell) * live).astype(BF16)
        pooled_ref[:, cols] = dot(pool, hid * live.astype(BF16), 1, 0).astype(BF16)


def down_forward(
    order, hid_ref, mid_ref, live_ref, own_ref, other_ref,
    out_ref, pooled_ref, weights, sems, *, seq_len,
):
    groups, _, width = weights.shape
    first = pl.program_id(0) == 0

    @pl.when(first)
    def _():
        load_weights(order, own_ref, other_ref, weights, sems)

    total = mid_ref[...]
    for group in range(groups):

        @pl.when(first)
        def _():
            wait_weights(weights, sems, group)

        total = total + dot(
            hid_ref[:, group * width : (group + 1) * width], weights[group], 1, 1
        )
    out_ref[...] = total.astype(BF16)
    live = live_ref[:, 0:1]
    rows, features = total.shape
    seqs = rows // seq_len
    sums = jnp.sum((total * live).reshape(seqs, seq_len, features), axis=1)
    counts = jnp.sum(jnp.broadcast_to(live, (rows, LANES)).reshape(seqs, seq_len, LANES), axis=1)
    pooled_ref[...] = sums / counts[:, 0:1]


def contrast(pooled_ref, count_ref, own_ref, other_ref, loss_ref, grad_ref, low_ref, *, micros):
    pooled = pooled_ref[...]
    seqs, width = pooled.shape
    each = seqs // micros
    scale_text = SOFTMAX_TEMP / math.sqrt(width)
    r = lax.rsqrt(jnp.mean(pooled * pooled, axis=-1, keepdims=True) + EPSILON)
    text = (pooled * r).astype(BF16)
    row_micro = lax.broadcasted_iota(jnp.int32, (seqs, 1), 0) // each
    step = min(own_ref.shape[0], 1024)
    pieces = [
        ref[i : i + step, :]
        for ref in (own_ref, other_ref)
        for i in range(0, ref.shape[0], step)
    ]
    col = lax.broadcasted_iota(jnp.int32, (1, step), 1)
    same = (col // each) % micros == row_micro
    logits = [jnp.where(same, dot(text, piece, 1, 1) * scale_text, -1e30) for piece in pieces]
    top = functools.reduce(
        jnp.maximum, [jnp.max(part, axis=1, keepdims=True) for part in logits]
    )
    powers = [jnp.exp(part - top) for part in logits]
    total = functools.reduce(jnp.add, [jnp.sum(part, axis=1, keepdims=True) for part in powers])
    log_total = top + jnp.log(total)
    positive = lax.broadcasted_iota(jnp.int32, (seqs, 1), 0) == col
    loss = log_total - jnp.sum(jnp.where(positive, logits[0], 0.0), axis=1, keepdims=True)
    loss_ref[...] = jnp.broadcast_to(loss, loss_ref.shape)
    inverse = LOSS_SCALE / total
    grad_text = jnp.zeros((seqs, width), F32)
    for i, (part, piece) in enumerate(zip(powers, pieces)):
        grad_part = part * inverse
        if i == 0:
            grad_part = grad_part - jnp.where(positive, LOSS_SCALE, 0.0)
        grad_text = grad_text + dot(grad_part.astype(BF16), piece, 1, 0)
    grad_text = grad_text * scale_text
    along = jnp.mean(grad_text * pooled, axis=-1, keepdims=True)
    grad = (r * grad_text - (r * r * r) * pooled * along) / count_ref[:, 0:1]
    grad_ref[...] = grad
    low_ref[...] = grad.astype(BF16)


def weight_gradient(
    inverse, left_ref, right_ref, keep_ref, send_ref, turned, slots, sems, *extra, shared_cols
):
    group = pl.program_id(0)
    groups = pl.num_programs(0)
    half, rows, _ = keep_ref.shape
    depth = slots.shape[1]

    @pl.when(group == 0)
    def _():
        turned[...] = left_ref[...].T

    slot = group % 2

    def drain(which):
        pltpu.make_async_copy(slots.at[which], slots.at[which], sems.at[which]).wait()

    @pl.when(group >= 2)
    def _():
        drain(slot)

    slots[slot] = dot(turned[...], right_ref[...], 1, 0).astype(BF16)

    def body(p, carry):
        position = inverse[p * groups + group]
        source = slots.at[slot, pl.ds(pl.multiple_of(p * rows, 16), rows), :]

        @pl.when(position < half)
        def _():
            pltpu.make_async_copy(source, keep_ref.at[position], sems.at[slot]).start()

        @pl.when(position >= half)
        def _():
            pltpu.make_async_copy(source, send_ref.at[position - half], sems.at[slot]).start()

        return carry

    lax.fori_loop(0, depth // rows, body, 0)

    @pl.when(group == groups - 1)
    def _():
        drain(slot)

        @pl.when(groups >= 2)
        def _():
            drain(1 - slot)


def attention_gradient(
    inverse, h1_ref, proj_ref, mid_ref, heads_ref, keep_ref, send_ref,
    turned, turned_mid, slots, sems,
):
    group = pl.program_id(0)
    groups = pl.num_programs(0)
    half, rows, _ = keep_ref.shape
    depth = slots.shape[1]

    @pl.when(group == 0)
    def _():
        turned[...] = h1_ref[...].T
        turned_mid[...] = mid_ref[...].T

    slot = group % 2

    def drain(which):
        pltpu.make_async_copy(slots.at[which], slots.at[which], sems.at[which]).wait()

    @pl.when(group >= 2)
    def _():
        drain(slot)

    slots[slot, :, : 4 * LANES] = dot(turned[...], proj_ref[:, : 4 * LANES], 1, 0).astype(BF16)
    tail = dot(turned_mid[...], heads_ref[...], 1, 0)
    keys = dot(turned[...], proj_ref[:, 4 * LANES :], 1, 0)
    slots[slot, :, 4 * LANES : 5 * LANES] = (keys + tail[:, :LANES]).astype(BF16)
    slots[slot, :, 5 * LANES :] = tail[:, LANES:].astype(BF16)

    def body(p, carry):
        position = inverse[p * groups + group]
        source = slots.at[slot, pl.ds(pl.multiple_of(p * rows, 16), rows), :]

        @pl.when(position < half)
        def _():
            pltpu.make_async_copy(source, keep_ref.at[position], sems.at[slot]).start()

        @pl.when(position >= half)
        def _():
            pltpu.make_async_copy(source, send_ref.at[position - half], sems.at[slot]).start()

        return carry

    lax.fori_loop(0, depth // rows, body, 0)

    @pl.when(group == groups - 1)
    def _():
        drain(slot)

        @pl.when(groups >= 2)
        def _():
            drain(1 - slot)


def norm_back(grad, gain, values):
    n, scale = normalize(values)
    scaled = grad * gain
    moved = scale * (
        scaled
        - jnp.mean(scaled, axis=-1, keepdims=True)
        - n * jnp.mean(scaled * n, axis=-1, keepdims=True)
    )
    gain_grad = jnp.sum(grad * n, axis=0, keepdims=True)
    shift_grad = jnp.sum(grad, axis=0, keepdims=True)
    return moved, gain_grad, shift_grad


def mlp_backward(
    order, grad_ref, low_ref, slope_ref, live_ref, mid_ref, norm_ref,
    up_own, up_other, down_own, down_other,
    dup_ref, dmid_ref, dmid_low_ref, sums_ref,
    up_w, down_w, up_sems, down_sems, *, seq_len,
):
    groups, _, width = up_w.shape
    first = pl.program_id(0) == 0

    @pl.when(first)
    def _():
        load_weights(order, down_own, down_other, down_w, down_sems)
        load_weights(order, up_own, up_other, up_w, up_sems)
        sums_ref[...] = jnp.zeros_like(sums_ref)

    grad = grad_ref[...]
    low = low_ref[...]
    mid = mid_ref[...]
    rows, features = mid.shape
    seqs = rows // seq_len

    def spread(values):
        return jnp.broadcast_to(
            values[:, None, :], (seqs, seq_len, values.shape[1])
        ).reshape(rows, values.shape[1])

    total = jnp.zeros((rows, features), F32)
    for group in range(groups):

        @pl.when(first)
        def _():
            wait_weights(down_w, down_sems, group)
            wait_weights(up_w, up_sems, group)

        cols = slice(group * width, (group + 1) * width)
        by_seq = dot(low, down_w[group], 1, 0)
        dup = (slope_ref[:, cols].astype(F32) * spread(by_seq)).astype(BF16)
        dup_ref[:, cols] = dup
        total = total + dot(dup, up_w[group], 1, 1)
    moved, gain_grad, shift_grad = norm_back(total, norm_ref[2:3, :], mid)
    dmid = spread(grad) * live_ref[:, 0:1] + moved
    dmid_ref[...] = dmid
    dmid_low_ref[...] = dmid.astype(BF16)
    sums_ref[0:1, :] += gain_grad
    sums_ref[1:2, :] += shift_grad


def attention_backward(
    order, x_ref, live_ref, norm_ref, proj_ref, lse_ref, dmid_ref, dmid_low_ref,
    own_ref, other_ref,
    dproj_ref, dx_ref, sums_ref,
    weights, sems, *, seq_len,
):
    groups = weights.shape[0]
    first = pl.program_id(0) == 0

    @pl.when(first)
    def _():
        load_weights(order, own_ref, other_ref, weights, sems)
        sums_ref[...] = jnp.zeros_like(sums_ref)

    x = x_ref[...].astype(F32)
    rows = x.shape[0]
    dmid_low = dmid_low_ref[...]
    low = low_lanes()
    high = 1 - low
    is_low = lax.broadcasted_iota(jnp.int32, (1, LANES), 1) < HD
    allowed = [allowed_pairs(live_ref[t], seq_len) for t in range(rows // LANES)]
    score_scale = HD**-0.5
    total = jnp.zeros(x.shape, F32)
    for group in range(groups):

        @pl.when(first)
        def _():
            wait_weights(weights, sems, group)

        dheads = dot(dmid_low, weights[group, :, 4 * LANES :], 1, 0).astype(BF16)
        parts = []
        for t, pairs in enumerate(allowed):
            span = slice(t * LANES, (t + 1) * LANES)
            base = group * 5 * LANES
            b = [proj_ref[span, base + i * LANES : base + (i + 1) * LANES] for i in range(5)]
            d0 = dheads[span, :LANES]
            d1 = dheads[span, LANES:]
            grads = []
            for h, (q_sel, q, k, d_sel, v) in enumerate(
                (
                    (low, b[0], b[1], d1 * low, b[2]),
                    (high, b[0], b[1], d1 * high, b[2]),
                    (low, b[3], b[4], d0 * high, b[3]),
                )
            ):
                scores = masked_scores(q * q_sel, k, pairs)
                column = group * 3 + h
                probs = jnp.exp(scores - lse_ref[span, column : column + 1])
                dprobs = dot(d_sel, v, 1, 1)
                inner = jnp.sum(probs * dprobs, axis=1, keepdims=True)
                dscores = (probs * (dprobs - inner) * score_scale).astype(BF16)
                d_full = d0 if h == 2 else d1
                grads.append(
                    (
                        dot(dscores, k, 1, 0),
                        dot(dscores, q, 0, 0),
                        dot(probs.astype(BF16), d_full, 0, 0),
                    )
                )
            blocks = (
                jnp.where(is_low, grads[0][0], grads[1][0]),
                jnp.where(is_low, grads[0][1], grads[1][1]),
                jnp.where(is_low, grads[0][2], grads[1][2]),
                jnp.where(is_low, grads[2][0], grads[2][2]),
                jnp.where(is_low, grads[2][1], 0.0),
            )
            parts.append(jnp.concatenate(blocks, axis=1).astype(BF16))
        dproj = jnp.concatenate(parts, axis=0)
        dproj_ref[:, group * 5 * LANES : (group + 1) * 5 * LANES] = dproj
        total = total + dot(dproj, weights[group, :, : 5 * LANES], 1, 1)
    moved, gain_grad, shift_grad = norm_back(total, norm_ref[0:1, :], x)
    dx_ref[...] = dmid_ref[...] + moved
    sums_ref[0:1, :] += gain_grad
    sums_ref[1:2, :] += shift_grad


def shampoo_kernel(
    grad_ref, left_ref, right_ref, left_root_ref, right_root_ref, master_ref,
    left_new_ref, right_new_ref, new_ref,
):
    grad = grad_ref[...]
    low = grad.astype(BF16)
    keep = 1.0 - STAT_DECAY
    left_new_ref[...] = STAT_DECAY * left_ref[...] + keep * dot(low, low, 1, 1)
    right_new_ref[...] = STAT_DECAY * right_ref[...] + keep * dot(low, low, 0, 0)
    half = dot(left_root_ref[...].astype(BF16), low, 1, 0).astype(BF16)
    update = dot(half, right_root_ref[...].astype(BF16), 1, 0)
    new_ref[...] = master_ref[...] - SHAMPOO_RATE * update


ANY = pl.BlockSpec(memory_space=pl.ANY)
SMEM = pl.BlockSpec(memory_space=pltpu.SMEM)
WHOLE = pl.BlockSpec(memory_space=pltpu.VMEM)


def rows_of(width, height=TILE):
    return pl.BlockSpec((height, width), lambda i: (i, 0))


def fixed(shape):
    return pl.BlockSpec(shape, lambda i: (0,) * len(shape))


def params():
    return pltpu.CompilerParams(vmem_limit_bytes=VMEM_BYTES)


def cost(flops, bytes_accessed):
    return pl.CostEstimate(flops=int(flops), bytes_accessed=int(bytes_accessed), transcendentals=0)


def shape_of(*dims, dtype=BF16):
    return jax.ShapeDtypeStruct(dims, dtype)


def shampoo(gradient, left_stat, right_stat, left_root, right_root, master):
    rows, cols = gradient.shape
    left_new, right_new, new = pl.pallas_call(
        shampoo_kernel,
        out_shape=(
            shape_of(rows, rows, dtype=F32),
            shape_of(cols, cols, dtype=F32),
            shape_of(rows, cols, dtype=F32),
        ),
        in_specs=[WHOLE] * 6,
        out_specs=(WHOLE,) * 3,
        compiler_params=params(),
        cost_estimate=cost(4 * rows * cols * cols, 12 * cols * cols),
        name="shampoo",
    )(gradient, left_stat[0, 0], right_stat[0, 0], left_root[0, 0], right_root[0, 0], master)
    return left_new[None, None], right_new[None, None], new


def pack_attention(qkv, out):
    q, k, v = (qkv[:, i] for i in range(3))
    a, b = 2 * HD, 3 * HD
    return jnp.concatenate(
        [q[:, :a], k[:, :a], v[:, :a], q[:, a:b], v[:, a:b], k[:, a:b], out[:, a:b], out[:, :a]],
        axis=1,
    )


def unpack_attention(packed):
    c = [packed[:, i * HD : (i + 1) * HD] for i in range(12)]
    qkv = jnp.concatenate([c[0], c[1], c[6], c[2], c[3], c[8], c[4], c[5], c[7]], axis=1)
    return qkv, jnp.concatenate([c[10], c[11], c[9]], axis=1)


def per_device(
    block_in, seq_lengths, image_embed, w_qkv, w_out, w_up, w_down, norm_params, norm_second,
    qkv_left, qkv_right, qkv_left_root, qkv_right_root,
    out_left, out_right, out_left_root, out_right_root,
    up_left, up_right, up_left_root, up_right_root,
    down_left, down_right, down_left_root, down_right_root,
):
    micros, seqs, seq_len, width = block_in.shape
    dp_count, groups = lax.axis_size("dp"), lax.axis_size("mp")
    count = dp_count * groups
    dp_index = lax.axis_index("dp")
    me = dp_index * groups + lax.axis_index("mp")
    owned = w_up.shape[0]
    ff = w_up.shape[1]
    all_seqs = micros * seqs
    rows = all_seqs * seq_len
    tiles = rows // TILE
    seq_tile = TILE // seq_len
    direct = owned % 16 == 0

    table = source_table(count)
    order = jnp.asarray(table, jnp.int32)[me]
    inverse = jnp.asarray(np.argsort(table, axis=1), jnp.int32)[me]

    def gathered(block):
        own, other = gather_blocks(block, count)
        if direct:
            return own, other
        whole = jnp.concatenate([own, other], axis=0)[inverse]
        whole = whole.reshape(dp_count, groups, owned, block.shape[1])
        whole = whole.transpose(1, 0, 2, 3).reshape(groups, width, block.shape[1])
        return whole[: groups // 2], whole[groups // 2 :]

    kernel_order = order if direct else jnp.arange(groups, dtype=jnp.int32)
    kernel_inverse = inverse if direct else jnp.arange(groups, dtype=jnp.int32)
    block_rows = owned if direct else width
    block_half = (count if direct else groups) // 2

    def summed(keep, send):
        if not direct:
            whole = jnp.concatenate([keep, send], axis=0)
            whole = whole.reshape(groups, dp_count, owned, whole.shape[2])
            whole = whole.transpose(1, 0, 2, 3).reshape(count, owned, whole.shape[3])[order]
            keep, send = whole[: count // 2], whole[count // 2 :]
        return sum_blocks(keep, send, count)

    attention_w = gathered(pack_attention(w_qkv.astype(BF16), w_out.astype(BF16)))
    up_w = gathered(w_up.astype(BF16))
    down_w = gathered(w_down.astype(BF16))
    images = gather_blocks(image_embed.reshape(all_seqs, width), count)
    images = [part.reshape(-1, width) for part in images]

    x = block_in.reshape(rows, width)
    norms = norm_params.T
    lengths = seq_lengths.reshape(all_seqs)
    live = (jnp.arange(seq_len)[None, :] < lengths[:, None]).astype(F32).reshape(rows)
    live_cols = jnp.broadcast_to(live[:, None], (rows, LANES))
    live_keys = live.reshape(rows // LANES, 1, LANES)
    counts = jnp.broadcast_to(lengths.astype(F32)[:, None], (all_seqs, LANES))

    live_spec = rows_of(LANES)
    keys_spec = pl.BlockSpec((TILE // LANES, 1, LANES), lambda i: (i, 0, 0))
    norm_spec = fixed((4, width))

    def weight_scratch(cols):
        return [pltpu.VMEM((groups, width, cols), BF16), pltpu.SemaphoreType.DMA((groups,))]

    packed = 6 * LANES
    h1, proj, heads, lse, mid, h2 = pl.pallas_call(
        functools.partial(attention_forward, seq_len=seq_len),
        grid=(tiles,),
        in_specs=[SMEM, rows_of(width), keys_spec, norm_spec, ANY, ANY],
        out_specs=(
            rows_of(width), rows_of(groups * 5 * LANES), rows_of(groups * 2 * LANES),
            rows_of(LANES), rows_of(width), rows_of(width),
        ),
        out_shape=(
            shape_of(rows, width), shape_of(rows, groups * 5 * LANES),
            shape_of(rows, groups * 2 * LANES), shape_of(rows, LANES, dtype=F32),
            shape_of(rows, width, dtype=F32), shape_of(rows, width),
        ),
        scratch_shapes=weight_scratch(packed),
        compiler_params=params(),
        cost_estimate=cost(2 * rows * width * groups * 900, 12e6),
        name="attention_forward",
    )(kernel_order, x, live_keys, norms, *attention_w)

    hid, slope, pooled_hid = pl.pallas_call(
        functools.partial(up_forward, seq_len=seq_len),
        grid=(tiles,),
        in_specs=[SMEM, rows_of(width), live_spec, ANY, ANY],
        out_specs=(rows_of(groups * ff), rows_of(groups * ff), rows_of(groups * ff, seq_tile)),
        out_shape=(
            shape_of(rows, groups * ff), shape_of(rows, groups * ff), shape_of(all_seqs, groups * ff),
        ),
        scratch_shapes=weight_scratch(ff),
        compiler_params=params(),
        cost_estimate=cost(2 * rows * width * groups * ff, 20e6),
        name="up_forward",
    )(kernel_order, h2, live_cols, *up_w)

    block_out, pooled = pl.pallas_call(
        functools.partial(down_forward, seq_len=seq_len),
        grid=(tiles,),
        in_specs=[SMEM, rows_of(groups * ff), rows_of(width), live_spec, ANY, ANY],
        out_specs=(rows_of(width), rows_of(width, seq_tile)),
        out_shape=(shape_of(rows, width), shape_of(all_seqs, width, dtype=F32)),
        scratch_shapes=weight_scratch(ff),
        compiler_params=params(),
        cost_estimate=cost(2 * rows * width * groups * ff, 20e6),
        name="down_forward",
    )(kernel_order, hid, mid, live_cols, *down_w)

    loss, grad_seq, grad_low = pl.pallas_call(
        functools.partial(contrast, micros=micros),
        in_specs=[WHOLE] * 4,
        out_specs=(WHOLE,) * 3,
        out_shape=(
            shape_of(all_seqs, LANES, dtype=F32), shape_of(all_seqs, width, dtype=F32),
            shape_of(all_seqs, width),
        ),
        compiler_params=params(),
        cost_estimate=cost(4 * all_seqs * width * images[0].shape[0] * 2, 4e6),
        name="contrast",
    )(pooled, counts, *images)

    gradient_out = (shape_of(block_half, block_rows, packed),) * 2

    def gradient(left, right):
        depth = left.shape[0]
        return pl.pallas_call(
            functools.partial(weight_gradient, shared_cols=0),
            grid=(groups,),
            in_specs=[SMEM, fixed((depth, width)), pl.BlockSpec((depth, ff), lambda i: (0, i))],
            out_specs=(ANY, ANY),
            out_shape=gradient_out,
            scratch_shapes=[
                pltpu.VMEM((width, depth), BF16),
                pltpu.VMEM((2, width, ff), BF16),
                pltpu.SemaphoreType.DMA((2,)),
            ],
            compiler_params=params(),
            cost_estimate=cost(2 * depth * width * groups * ff, 12e6),
            name="weight_gradient",
        )(kernel_inverse, left, right)

    down_parts = gradient(grad_low, pooled_hid)
    grad_down = summed(*down_parts)

    dup, dmid, dmid_low, sums_two = pl.pallas_call(
        functools.partial(mlp_backward, seq_len=seq_len),
        grid=(tiles,),
        in_specs=[
            SMEM, rows_of(width, seq_tile), rows_of(width, seq_tile), rows_of(groups * ff),
            live_spec, rows_of(width), norm_spec, ANY, ANY, ANY, ANY,
        ],
        out_specs=(rows_of(groups * ff), rows_of(width), rows_of(width), fixed((8, width))),
        out_shape=(
            shape_of(rows, groups * ff), shape_of(rows, width, dtype=F32), shape_of(rows, width),
            shape_of(8, width, dtype=F32),
        ),
        scratch_shapes=[
            pltpu.VMEM((groups, width, ff), BF16), pltpu.VMEM((groups, width, ff), BF16),
            pltpu.SemaphoreType.DMA((groups,)), pltpu.SemaphoreType.DMA((groups,)),
        ],
        compiler_params=params(),
        cost_estimate=cost(2 * rows * width * groups * ff, 25e6),
        name="mlp_backward",
    )(kernel_order, grad_seq, grad_low, slope, live_cols, mid, norms, *up_w, *down_w)

    up_parts = gradient(h2, dup)
    grad_up = summed(*up_parts)

    dproj, input_grad, sums_one = pl.pallas_call(
        functools.partial(attention_backward, seq_len=seq_len),
        grid=(tiles,),
        in_specs=[
            SMEM, rows_of(width), keys_spec, norm_spec, rows_of(groups * 5 * LANES),
            rows_of(LANES), rows_of(width), rows_of(width), ANY, ANY,
        ],
        out_specs=(rows_of(groups * 5 * LANES), rows_of(width), fixed((8, width))),
        out_shape=(
            shape_of(rows, groups * 5 * LANES), shape_of(rows, width, dtype=F32),
            shape_of(8, width, dtype=F32),
        ),
        scratch_shapes=weight_scratch(packed),
        compiler_params=params(),
        cost_estimate=cost(2 * rows * width * groups * 1300, 20e6),
        name="attention_backward",
    )(kernel_order, x, live_keys, norms, proj, lse, dmid, dmid_low, *attention_w)

    attention_parts = pl.pallas_call(
        attention_gradient,
        grid=(groups,),
        in_specs=[
            SMEM, fixed((rows, width)), pl.BlockSpec((rows, 5 * LANES), lambda i: (0, i)),
            fixed((rows, width)), pl.BlockSpec((rows, 2 * LANES), lambda i: (0, i)),
        ],
        out_specs=(ANY, ANY),
        out_shape=gradient_out,
        scratch_shapes=[
            pltpu.VMEM((width, rows), BF16),
            pltpu.VMEM((width, rows), BF16),
            pltpu.VMEM((2, width, packed), BF16),
            pltpu.SemaphoreType.DMA((2,)),
        ],
        compiler_params=params(),
        cost_estimate=cost(2 * rows * width * groups * 900, 12e6),
        name="attention_gradient",
    )(kernel_inverse, h1, dproj, dmid_low, heads)
    grad_attention = summed(*attention_parts)

    norm_sum = jnp.concatenate([sums_one[:2], sums_two[:2]], axis=0)
    bit = 1
    while bit < count:
        norm_sum = norm_sum + swap(norm_sum, [i ^ bit for i in range(count)])
        bit *= 2
    grad_norm = lax.dynamic_slice_in_dim(norm_sum, dp_index * owned, owned, 1).T

    down_left_new, down_right_new, down_new = shampoo(
        grad_down, down_left, down_right, down_left_root, down_right_root, w_down
    )
    up_left_new, up_right_new, up_new = shampoo(
        grad_up, up_left, up_right, up_left_root, up_right_root, w_up
    )
    grad_qkv, grad_out = unpack_attention(grad_attention)
    qkv_left_new, qkv_right_new, qkv_new = shampoo(
        grad_qkv, qkv_left, qkv_right, qkv_left_root, qkv_right_root, w_qkv.reshape(owned, -1)
    )
    out_left_new, out_right_new, out_new = shampoo(
        grad_out, out_left, out_right, out_left_root, out_right_root, w_out
    )
    norm_second_new = STAT_DECAY * norm_second + (1.0 - STAT_DECAY) * grad_norm * grad_norm
    own_params = lax.dynamic_slice_in_dim(norm_params, dp_index * owned, owned, 0)
    norm_new = own_params - NORM_RATE * grad_norm / (jnp.sqrt(norm_second_new) + 1e-08)
    return (
        block_out.reshape(block_in.shape),
        input_grad.reshape(block_in.shape),
        loss[:, 0].reshape(micros, seqs),
        grad_qkv.reshape(w_qkv.shape), qkv_left_new, qkv_right_new, qkv_new.reshape(w_qkv.shape),
        grad_out, out_left_new, out_right_new, out_new,
        grad_up, up_left_new, up_right_new, up_new,
        grad_down, down_left_new, down_right_new, down_new,
        grad_norm, norm_second_new, norm_new,
    )


def solution(mesh):
    sequence = P(None, AXES)
    stat = P("dp", "mp", None, None)
    weight = P("dp", "mp")
    qkv = P("dp", None, "mp")
    norm = P("dp", None)
    in_specs = (sequence, sequence, sequence, qkv, weight, weight, weight, P(), norm) + (stat,) * 16
    out_specs = (
        (sequence, sequence, sequence)
        + (qkv, stat, stat, qkv)
        + (weight, stat, stat, weight) * 3
        + (norm, norm, norm)
    )
    return jax.shard_map(
        per_device, mesh=mesh, in_specs=in_specs, out_specs=out_specs, check_vma=False
    )
```

```python
import functools
import math

import jax
import jax.numpy as jnp
import numpy as np
from jax import lax
from jax.experimental import pallas as pl
from jax.experimental.pallas import tpu as pltpu
from jax.sharding import PartitionSpec as P

AXES = ("dp", "mp")
HD = 64
LANES = 128
EPSILON = 1e-06
SOFTMAX_TEMP = 2.0
LOSS_SCALE = 32.0
STAT_DECAY = 0.5
SHAMPOO_RATE = 0.3
NORM_RATE = 0.5
TILE = 256
VMEM_BYTES = 56 * 1024 * 1024
F32 = jnp.float32
BF16 = jnp.bfloat16


def far_digits(count):
    digits = []
    weight = 8
    while weight < count:
        size = min(4, count // weight)
        digits.append((weight, size))
        weight *= size
    return digits


def near_steps(count):
    return (
        [i ^ (4 if i % 2 == 0 else 2) for i in range(count)],
        [i ^ (2 if i % 2 == 0 else 4) for i in range(count)],
        [i ^ 1 for i in range(count)],
    )


def far_steps(count, weight, size):
    return [[i ^ (weight * m) for i in range(count)] for m in range(1, size)]


def source_table(count, near_first):
    first, second, third = near_steps(count)
    far = [far_steps(count, weight, size) for weight, size in far_digits(count)]
    rounds = [[first]] + far if near_first else far + [[first]]
    table = np.arange(count)[:, None]
    for steps in rounds + [[second], [third]]:
        table = np.concatenate([table] + [table[np.array(step)] for step in steps], axis=1)
    return table


def swap(values, step):
    return lax.ppermute(values, AXES, list(enumerate(step)))


class Gather:
    def __init__(self, block, count):
        self.count = count
        self.near = near_steps(count)
        self.held = block[None]
        self.received = []

    def keep(self, *earlier):
        if self.received:
            self.received = after(self.received, *earlier)
            self.held = jnp.concatenate([self.held] + self.received, axis=0)
            self.received = []

    def far(self, *earlier):
        (self.held,) = after([self.held], *earlier)
        for weight, size in far_digits(self.count):
            self.keep()
            steps = far_steps(self.count, weight, size)
            self.received = [swap(self.held, step) for step in steps]

    def first(self, *earlier):
        (self.held,) = after([self.held], *earlier)
        self.received = [swap(self.held, self.near[0])]

    def second(self, *earlier):
        (self.held,) = after([self.held], *earlier)
        self.across = swap(self.held, self.near[1])

    def third(self, *earlier):
        (self.held,) = after([self.held], *earlier)
        self.held_other = swap(self.held, self.near[2])

    def last(self, *earlier):
        (self.across,) = after([self.across], *earlier)
        self.across_other = swap(self.across, self.near[2])

    def quarters(self):
        return self.held, self.across, self.held_other, self.across_other


def join(*values):
    return lax.optimization_barrier(values)


def after(values, *earlier, keep=None):
    if not earlier:
        return list(values)
    return list(lax.optimization_barrier((*values, *earlier)))[: keep or len(values)]


def add_low(*terms):
    return sum(term.astype(F32) for term in terms).astype(BF16)


class Sum:
    def __init__(self, quarters, count):
        self.count = count
        self.near = near_steps(count)
        self.held, self.across, held_other, across_other = quarters
        self.from_across = swap(across_other, self.near[2])
        self.from_held = swap(held_other, self.near[2])

    def second(self, *earlier):
        (received,) = after([self.from_across], *earlier)
        self.going = add_low(self.across, received)
        self.received = swap(self.going, self.near[1])

    def first(self, *earlier):
        (received,) = after([self.received], *earlier)
        half = self.held.shape[0] // 2
        terms = self.held, self.from_held, received
        self.going = add_low(*(term[half:] for term in terms))
        self.keep = add_low(*(term[:half] for term in terms))
        self.received = swap(self.going, self.near[0])

    def far(self, *earlier):
        (received,) = after([self.received], *earlier)
        keep = [self.keep, received]
        for weight, size in far_digits(self.count)[::-1]:
            step_size = keep[0].shape[0] // size
            parts = [
                add_low(*(term[m * step_size : (m + 1) * step_size] for term in keep))
                for m in range(1, size)
            ]
            keep = [term[:step_size] if step_size > 1 else term for term in keep] + [
                swap(part, step)
                for part, step in zip(parts, far_steps(self.count, weight, size))
            ]
        self.going = parts[-1]
        self.keep = keep


def dot(left, right, left_dim, right_dim):
    return lax.dot_general(
        left, right, (((left_dim,), (right_dim,)), ((), ())), preferred_element_type=F32
    )


def load_weights(order, parts, weights, sems):
    size, rows, _ = parts[0].shape
    groups = weights.shape[0]

    def body(q, carry):
        for i, part in enumerate(parts):
            index = order[i * size + q]
            group = index % groups
            place = pl.multiple_of((index // groups) * rows, 16)
            pltpu.make_async_copy(
                part.at[q], weights.at[group, pl.ds(place, rows), :], sems.at[group]
            ).start()
        return carry

    lax.fori_loop(0, size, body, 0)


def store_blocks(inverse, source, group, groups, parts, sem):
    size, rows, _ = parts[0].shape

    def body(p, carry):
        position = inverse[p * groups + group]
        block = source.at[pl.ds(pl.multiple_of(p * rows, 16), rows), :]
        for i, part in enumerate(parts):

            @pl.when(jnp.logical_and(position >= i * size, position < (i + 1) * size))
            def _():
                pltpu.make_async_copy(block, part.at[position - i * size], sem).start()

        return carry

    lax.fori_loop(0, source.shape[0] // rows, body, 0)


def wait_weights(weights, sems, group):
    pltpu.make_async_copy(weights.at[group], weights.at[group], sems.at[group]).wait()


def normalize(values):
    center = values - jnp.mean(values, axis=-1, keepdims=True)
    spread = jnp.mean(center * center, axis=-1, keepdims=True)
    scale = lax.rsqrt(spread + EPSILON)
    return center * scale, scale


def low_lanes(dtype=BF16):
    lane = lax.broadcasted_iota(jnp.int32, (1, LANES), 1)
    return jnp.where(lane < HD, 1.0, 0.0).astype(dtype)


def pairs_of(blocks, low):
    first, second = blocks

    def join(left, right, high_half):
        if high_half:
            return jnp.where(low, turn(left), right)
        return jnp.where(low, left, turn(right))

    return (
        (first[0], first[1], first[2]),
        (second[0], second[1], second[2]),
        (
            join(first[3], second[3], False),
            join(first[4], second[4], False),
            join(first[3], second[3], True),
        ),
    )


def turn(values):
    return jnp.concatenate([values[:, HD:], values[:, :HD]], axis=1)


def both_heads(values, low_mask, high_mask):
    return jnp.concatenate([values * low_mask, values * high_mask], axis=0)


def diagonal(full, seq_len, own_cols):
    picked = full[:seq_len]
    for i, own in enumerate(own_cols):
        if i:
            picked = jnp.where(own, full[i * seq_len : (i + 1) * seq_len], picked)
    return picked


def undiagonal(compact, own_cols):
    return jnp.concatenate(
        [jnp.where(own, compact, jnp.zeros_like(compact)) for own in own_cols], axis=0
    )


def sequence_columns(seq_len):
    lane = lax.broadcasted_iota(jnp.int32, (seq_len, 2 * LANES), 1) % LANES
    return [lane // seq_len == i for i in range(LANES // seq_len)]


def stack_heads(values):
    return jnp.concatenate([values[:, :LANES], values[:, LANES:]], axis=0)


def first_norm(x_ref, norm_ref, h1_ref):
    n1, _ = normalize(x_ref[...].astype(F32))
    h1_ref[...] = (n1 * norm_ref[0:1, :] + norm_ref[1:2, :]).astype(BF16)


def attention_forward(
    order, x_ref, h1_ref, live_ref, norm_ref, w0, w1, w2, w3,
    proj_ref, heads_ref, lse_ref, mid_ref, h2_ref,
    weights, sems, *, seq_len,
):
    groups = weights.shape[0]
    first = pl.program_id(0) == 0

    @pl.when(first)
    def _():
        load_weights(order, (w0, w1, w2, w3), weights, sems)
        for group in range(weights.shape[0]):
            wait_weights(weights, sems, group)

    x = x_ref[...].astype(F32)
    rows = x.shape[0]
    h1 = h1_ref[...]
    low_mask = low_lanes()
    high_mask = 1 - low_mask
    low = lax.broadcasted_iota(jnp.int32, (1, LANES), 1) < HD
    own_cols = sequence_columns(seq_len)
    count = rows // LANES
    duos = groups // 2
    projected = [
        dot(h1, weights[group, :, : 5 * LANES], 1, 0).astype(BF16) for group in range(groups)
    ]
    chains = []
    for duo in range(duos):
        for t in range(count):
            span = slice(t * LANES, (t + 1) * LANES)
            blocks = [
                [proj[span, i * LANES : (i + 1) * LANES] for i in range(5)]
                for proj in projected[2 * duo : 2 * duo + 2]
            ]
            for i, (q, k, v) in enumerate(pairs_of(blocks, low)):
                for which, part in enumerate((q, k, v)):
                    at = ((duo * 3 + i) * 3 + which) * LANES
                    proj_ref[span, at : at + LANES] = part
                chains.append((t, duo * 3 + i, q, k, v))
    scores = [dot(k, both_heads(q, low_mask, high_mask), 1, 1) for t, i, q, k, v in chains]
    probs = []
    for (t, i, *_), full in zip(chains, scores):
        compact = diagonal(full, seq_len, own_cols) * (HD**-0.5)
        compact = jnp.where(live_ref[t] > 0.0, compact, -1e30)
        top = jnp.max(compact, axis=0, keepdims=True)
        powers = jnp.exp(compact - top)
        power = jnp.sum(powers, axis=0, keepdims=True)
        lse_ref[t, i : i + 1, :] = top + jnp.log(power)
        probs.append(undiagonal((powers * (1.0 / power)).astype(BF16), own_cols))
    outs = [
        dot(stack_heads(part), both_heads(v, low_mask, high_mask), 0, 0)
        for part, (t, i, q, k, v) in zip(probs, chains)
    ]
    total = x
    for duo in range(duos):
        heads = [[], []]
        for t in range(count):
            at = 3 * (duo * count + t)
            one, two, third = outs[at : at + 3]
            heads[0].append(
                jnp.concatenate([jnp.where(low, 0.0, turn(third)), one], axis=1).astype(BF16)
            )
            heads[1].append(
                jnp.concatenate([jnp.where(low, 0.0, third), two], axis=1).astype(BF16)
            )
        for side, group in enumerate((2 * duo, 2 * duo + 1)):
            joined = jnp.concatenate(heads[side], axis=0)
            heads_ref[:, group * 2 * LANES : (group + 1) * 2 * LANES] = joined
            total = total + dot(joined, weights[group, :, 4 * LANES :], 1, 1)
    mid_ref[...] = total
    n2, _ = normalize(total)
    h2_ref[...] = (n2 * norm_ref[2:3, :] + norm_ref[3:4, :]).astype(BF16)


def up_forward(
    order, h2_ref, live_ref, w0, w1, w2, w3,
    hid_ref, slope_ref, pooled_ref,
    weights, sems, *, seq_len,
):
    groups, _, width = weights.shape
    first = pl.program_id(0) == 0

    @pl.when(first)
    def _():
        load_weights(order, (w0, w1, w2, w3), weights, sems)
        for group in range(weights.shape[0]):
            wait_weights(weights, sems, group)

    h2 = h2_ref[...]
    rows = h2.shape[0]
    live = live_ref[:, 0:1]
    seqs = rows // seq_len
    member = (
        lax.broadcasted_iota(jnp.int32, (seqs, rows), 1) // seq_len
        == lax.broadcasted_iota(jnp.int32, (seqs, rows), 0)
    )
    pool = jnp.where(member, 1.0, 0.0).astype(BF16)
    for group in range(groups):


        cols = slice(group * width, (group + 1) * width)
        up = dot(h2, weights[group], 1, 0)
        gate = 0.5 + 0.5 * lax.erf(up * (0.5**0.5))
        hid = (up * gate).astype(BF16)
        hid_ref[:, cols] = hid
        bell = jnp.exp(up * up * -0.5) * (1.0 / math.sqrt(2.0 * math.pi))
        slope_ref[:, cols] = ((gate + up * bell) * live).astype(BF16)
        pooled_ref[:, cols] = dot(pool, hid * live.astype(BF16), 1, 0).astype(BF16)


def down_forward(
    order, hid_ref, mid_ref, live_ref, w0, w1, w2, w3,
    out_ref, pooled_ref, weights, sems, *, seq_len,
):
    groups, _, width = weights.shape
    first = pl.program_id(0) == 0

    @pl.when(first)
    def _():
        load_weights(order, (w0, w1, w2, w3), weights, sems)
        for group in range(weights.shape[0]):
            wait_weights(weights, sems, group)

    total = mid_ref[...]
    for group in range(groups):


        total = total + dot(
            hid_ref[:, group * width : (group + 1) * width], weights[group], 1, 1
        )
    out_ref[...] = total.astype(BF16)
    live = live_ref[:, 0:1]
    rows, features = total.shape
    seqs = rows // seq_len
    sums = jnp.sum((total * live).reshape(seqs, seq_len, features), axis=1)
    counts = jnp.sum(jnp.broadcast_to(live, (rows, LANES)).reshape(seqs, seq_len, LANES), axis=1)
    pooled_ref[...] = sums / counts[:, 0:1]


def contrast(pooled_ref, count_ref, m0, m1, m2, m3, loss_ref, grad_ref, low_ref, *, micros):
    pooled = pooled_ref[...]
    seqs, width = pooled.shape
    each = seqs // micros
    scale_text = SOFTMAX_TEMP / math.sqrt(width)
    r = lax.rsqrt(jnp.mean(pooled * pooled, axis=-1, keepdims=True) + EPSILON)
    text = (pooled * r).astype(BF16)
    row_micro = lax.broadcasted_iota(jnp.int32, (seqs, 1), 0) // each
    step = min(m0.shape[0], 1024)
    pieces = [
        ref[i : i + step, :]
        for ref in (m0, m1, m2, m3)
        for i in range(0, ref.shape[0], step)
    ]
    col = lax.broadcasted_iota(jnp.int32, (1, step), 1)
    same = (col // each) % micros == row_micro
    logits = [jnp.where(same, dot(text, piece, 1, 1) * scale_text, -1e30) for piece in pieces]
    top = functools.reduce(
        jnp.maximum, [jnp.max(part, axis=1, keepdims=True) for part in logits]
    )
    powers = [jnp.exp(part - top) for part in logits]
    total = functools.reduce(jnp.add, [jnp.sum(part, axis=1, keepdims=True) for part in powers])
    log_total = top + jnp.log(total)
    positive = lax.broadcasted_iota(jnp.int32, (seqs, 1), 0) == col
    loss = log_total - jnp.sum(jnp.where(positive, logits[0], 0.0), axis=1, keepdims=True)
    loss_ref[...] = jnp.broadcast_to(loss, loss_ref.shape)
    inverse = LOSS_SCALE / total
    grad_text = jnp.zeros((seqs, width), F32)
    for i, (part, piece) in enumerate(zip(powers, pieces)):
        grad_part = part * inverse
        if i == 0:
            grad_part = grad_part - jnp.where(positive, LOSS_SCALE, 0.0)
        grad_text = grad_text + dot(grad_part.astype(BF16), piece, 1, 0)
    grad_text = grad_text * scale_text
    along = jnp.mean(grad_text * pooled, axis=-1, keepdims=True)
    grad = (r * grad_text - (r * r * r) * pooled * along) / count_ref[:, 0:1]
    grad_ref[...] = grad
    low_ref[...] = grad.astype(BF16)


def drain(slots, sems, which):
    pltpu.make_async_copy(slots.at[which], slots.at[which], sems.at[which]).wait()


def finish_blocks(slots, sems, group, groups, slot):
    @pl.when(group == groups - 1)
    def _():
        drain(slots, sems, slot)

        @pl.when(groups >= 2)
        def _():
            drain(slots, sems, 1 - slot)


def weight_gradient(
    inverse, left_ref, right_ref, g0, g1, g2, g3, turned, slots, sems
):
    group = pl.program_id(0)
    groups = pl.num_programs(0)
    slot = group % 2

    @pl.when(group == 0)
    def _():
        turned[...] = left_ref[...].T

    @pl.when(group >= 2)
    def _():
        drain(slots, sems, slot)

    slots[slot] = dot(turned[...], right_ref[...], 1, 0).astype(BF16)
    store_blocks(inverse, slots.at[slot], group, groups, (g0, g1, g2, g3), sems.at[slot])
    finish_blocks(slots, sems, group, groups, slot)


def attention_gradient(
    inverse, h1_ref, proj_ref, mid_ref, heads_ref, g0, g1, g2, g3,
    turned, turned_mid, slots, sems,
):
    group = pl.program_id(0)
    groups = pl.num_programs(0)
    slot = group % 2

    @pl.when(group == 0)
    def _():
        turned[...] = h1_ref[...].T
        turned_mid[...] = mid_ref[...].T

    @pl.when(group >= 2)
    def _():
        drain(slots, sems, slot)

    slots[slot, :, : 4 * LANES] = dot(turned[...], proj_ref[:, : 4 * LANES], 1, 0).astype(BF16)
    tail = dot(turned_mid[...], heads_ref[...], 1, 0)
    keys = dot(turned[...], proj_ref[:, 4 * LANES :], 1, 0)
    slots[slot, :, 4 * LANES : 5 * LANES] = (keys + tail[:, :LANES]).astype(BF16)
    slots[slot, :, 5 * LANES :] = tail[:, LANES:].astype(BF16)
    store_blocks(inverse, slots.at[slot], group, groups, (g0, g1, g2, g3), sems.at[slot])
    finish_blocks(slots, sems, group, groups, slot)


def norm_back(grad, gain, values):
    n, scale = normalize(values)
    scaled = grad * gain
    moved = scale * (
        scaled
        - jnp.mean(scaled, axis=-1, keepdims=True)
        - n * jnp.mean(scaled * n, axis=-1, keepdims=True)
    )
    gain_grad = jnp.sum(grad * n, axis=0, keepdims=True)
    shift_grad = jnp.sum(grad, axis=0, keepdims=True)
    return moved, gain_grad, shift_grad


def down_backward(order, low_ref, w0, w1, w2, w3, by_seq_ref, weights, sems):
    groups, _, width = weights.shape
    load_weights(order, (w0, w1, w2, w3), weights, sems)
    for group in range(groups):
        wait_weights(weights, sems, group)
        by_seq_ref[:, group * width : (group + 1) * width] = dot(
            low_ref[...], weights[group], 1, 0
        )


def mlp_backward(
    order, grad_ref, by_seq_ref, slope_ref, live_ref, mid_ref, norm_ref,
    w0, w1, w2, w3,
    dup_ref, dmid_ref, dmid_low_ref, sums_ref,
    weights, sems, *, seq_len,
):
    groups, _, width = weights.shape

    @pl.when(pl.program_id(0) == 0)
    def _():
        load_weights(order, (w0, w1, w2, w3), weights, sems)
        sums_ref[...] = jnp.zeros_like(sums_ref)
        for group in range(groups):
            wait_weights(weights, sems, group)

    grad = grad_ref[...]
    mid = mid_ref[...]
    rows, features = mid.shape
    seqs = rows // seq_len

    def spread(values):
        return jnp.broadcast_to(
            values[:, None, :], (seqs, seq_len, values.shape[1])
        ).reshape(rows, values.shape[1])

    total = jnp.zeros((rows, features), F32)
    for group in range(groups):


        cols = slice(group * width, (group + 1) * width)
        dup = (slope_ref[:, cols].astype(F32) * spread(by_seq_ref[:, cols])).astype(BF16)
        dup_ref[:, cols] = dup
        total = total + dot(dup, weights[group], 1, 1)
    moved, gain_grad, shift_grad = norm_back(total, norm_ref[2:3, :], mid)
    dmid = spread(grad) * live_ref[:, 0:1] + moved
    dmid_ref[...] = dmid
    dmid_low_ref[...] = dmid.astype(BF16)
    sums_ref[0:1, :] += gain_grad
    sums_ref[1:2, :] += shift_grad


def attention_backward(
    order, x_ref, live_ref, norm_ref, proj_ref, lse_ref, dmid_ref, dmid_low_ref,
    w0, w1, w2, w3, *rest, seq_len,
):
    dproj_ref, dx_ref, sums_ref, weights, sems = rest[-5:]
    groups = weights.shape[0]
    first = pl.program_id(0) == 0

    @pl.when(first)
    def _():
        load_weights(order, (w0, w1, w2, w3), weights, sems)
        for group in range(weights.shape[0]):
            wait_weights(weights, sems, group)
        sums_ref[...] = jnp.zeros_like(sums_ref)

    x = x_ref[...].astype(F32)
    rows = x.shape[0]
    dmid_low = dmid_low_ref[...]
    low_mask = low_lanes()
    high_mask = 1 - low_mask
    low = lax.broadcasted_iota(jnp.int32, (1, LANES), 1) < HD
    own_cols = sequence_columns(seq_len)
    score_scale = HD**-0.5
    count = rows // LANES
    duos = groups // 2
    dheads = [
        dot(dmid_low, weights[group, :, 4 * LANES :], 1, 0).astype(BF16) for group in range(groups)
    ]
    chains = []
    for duo in range(duos):
        first_d, second_d = dheads[2 * duo : 2 * duo + 2]
        for t in range(count):
            span = slice(t * LANES, (t + 1) * LANES)
            for i, d in enumerate(
                (
                    first_d[span, LANES:],
                    second_d[span, LANES:],
                    jnp.where(low, turn(first_d[span, :LANES]), second_d[span, :LANES]),
                )
            ):
                at = (duo * 3 + i) * 3 * LANES
                q, k, v = (
                    proj_ref[span, at + j * LANES : at + (j + 1) * LANES] for j in range(3)
                )
                qq, kk, dd = (both_heads(part, low_mask, high_mask) for part in (q, k, d))
                chains.append((t, duo * 3 + i, k, v, qq, kk, dd))
    scores = [dot(k, qq, 1, 1) for t, i, k, v, qq, kk, dd in chains]
    powers = [dot(v, dd, 1, 1) for t, i, k, v, qq, kk, dd in chains]
    wide = []
    for (t, i, *_), full, power in zip(chains, scores, powers):
        live = live_ref[t] > 0.0
        compact = diagonal(full, seq_len, own_cols) * score_scale
        lse = lse_ref[t, i : i + 1, :]
        probs = jnp.where(live, jnp.exp(jnp.where(live, compact - lse, 0.0)), 0.0)
        dprobs = diagonal(power, seq_len, own_cols)
        inner = jnp.sum(probs * dprobs, axis=0, keepdims=True)
        dscores = probs * (dprobs - inner) * score_scale
        wide.append(
            (
                undiagonal(dscores.astype(BF16), own_cols),
                undiagonal(probs.astype(BF16), own_cols),
            )
        )
    outs = [
        (dot(stack_heads(ds), kk, 0, 0), dot(ds, qq, 1, 0), dot(p, dd, 1, 0))
        for (ds, p), (t, i, k, v, qq, kk, dd) in zip(wide, chains)
    ]
    total = jnp.zeros(x.shape, F32)
    for duo in range(duos):
        grads = [[], []]
        for t in range(count):
            at = 3 * (duo * count + t)
            one, two, third = outs[at : at + 3]
            grads[0].append(
                jnp.concatenate(
                    one
                    + (jnp.where(low, third[0], turn(third[2])), jnp.where(low, third[1], 0.0)),
                    axis=1,
                ).astype(BF16)
            )
            grads[1].append(
                jnp.concatenate(
                    two
                    + (jnp.where(low, turn(third[0]), third[2]), jnp.where(low, turn(third[1]), 0.0)),
                    axis=1,
                ).astype(BF16)
            )
        for side, group in enumerate((2 * duo, 2 * duo + 1)):
            dproj = jnp.concatenate(grads[side], axis=0)
            dproj_ref[:, group * 5 * LANES : (group + 1) * 5 * LANES] = dproj
            total = total + dot(dproj, weights[group, :, : 5 * LANES], 1, 1)
    moved, gain_grad, shift_grad = norm_back(total, norm_ref[0:1, :], x)
    dx_ref[...] = dmid_ref[...] + moved
    sums_ref[0:1, :] += gain_grad
    sums_ref[1:2, :] += shift_grad


def renew(grad, left, right, left_root, right_root):
    low = grad.astype(BF16)
    keep = 1.0 - STAT_DECAY
    half = dot(left_root.astype(BF16), low, 1, 0).astype(BF16)
    return (
        STAT_DECAY * left + keep * dot(low, low, 1, 1),
        STAT_DECAY * right + keep * dot(low, low, 0, 0),
        SHAMPOO_RATE * dot(half, right_root.astype(BF16), 1, 0),
    )


def shampoo_kernel(*refs):
    terms = refs[:-9]
    stats, master_ref = refs[-9:-5], refs[-5]
    grad_ref, left_new_ref, right_new_ref, new_ref = refs[-4:]
    grad = sum(term[0].astype(F32) for term in terms)
    grad_ref[...] = grad
    left_new_ref[...], right_new_ref[...], step = renew(grad, *(ref[...] for ref in stats))
    new_ref[...] = master_ref[...] - step


def attention_shampoo(*refs):
    terms = refs[:-18]
    qkv_ref, out_ref, *stats = refs[-18:-8]
    qkv_grad, qkv_left, qkv_right, qkv_new, out_grad, out_left, out_right, out_new = refs[-8:]
    packed = sum(term[0].astype(F32) for term in terms)
    qkv, out = unpack_attention(packed)
    out_grad[...] = out
    qkv_left[...], qkv_right[...], step = renew(qkv, *(ref[...] for ref in stats[:4]))
    width = qkv_ref.shape[2]
    for i in range(3):
        cols = slice(i * width, (i + 1) * width)
        qkv_grad[i] = qkv[:, cols]
        qkv_new[i] = qkv_ref[i] - step[:, cols]
    out_left[...], out_right[...], step = renew(out, *(ref[...] for ref in stats[4:]))
    out_new[...] = out_ref[...] - step


ANY = pl.BlockSpec(memory_space=pl.ANY)
SMEM = pl.BlockSpec(memory_space=pltpu.SMEM)
WHOLE = pl.BlockSpec(memory_space=pltpu.VMEM)


def rows_of(width, height=TILE, start=0):
    return pl.BlockSpec((height, width), lambda i: (i + start, 0))


def fixed(shape):
    return pl.BlockSpec(shape, lambda i: (0,) * len(shape))


def params():
    return pltpu.CompilerParams(vmem_limit_bytes=VMEM_BYTES)


def cost(flops, bytes_accessed):
    return pl.CostEstimate(flops=4 * int(flops), bytes_accessed=int(bytes_accessed), transcendentals=0)


def shape_of(*dims, dtype=BF16):
    return jax.ShapeDtypeStruct(dims, dtype)


def shampoo(terms, left_stat, right_stat, left_root, right_root, master):
    rows, cols = master.shape
    grad, left_new, right_new, new = pl.pallas_call(
        shampoo_kernel,
        grid=(1,),
        out_shape=(
            shape_of(rows, cols, dtype=F32),
            shape_of(rows, rows, dtype=F32),
            shape_of(cols, cols, dtype=F32),
            shape_of(rows, cols, dtype=F32),
        ),
        in_specs=[pl.BlockSpec((1, rows, cols), lambda i: (0, 0, 0))] * len(terms) + [WHOLE] * 5,
        out_specs=(WHOLE,) * 4,
        compiler_params=params(),
        cost_estimate=cost(4 * rows * cols * cols, 12 * cols * cols),
        name="shampoo",
    )(*terms, left_stat[0, 0], right_stat[0, 0], left_root[0, 0], right_root[0, 0], master)
    return grad, left_new[None, None], right_new[None, None], new


def pack_attention(qkv, out):
    q, k, v = (qkv[:, i] for i in range(3))
    a, b = 2 * HD, 3 * HD
    return jnp.concatenate(
        [q[:, :a], k[:, :a], v[:, :a], q[:, a:b], v[:, a:b], k[:, a:b], out[:, a:b], out[:, :a]],
        axis=1,
    )


def unpack_attention(packed):
    c = [packed[:, i * HD : (i + 1) * HD] for i in range(12)]
    qkv = jnp.concatenate([c[0], c[1], c[6], c[2], c[3], c[8], c[4], c[5], c[7]], axis=1)
    return qkv, jnp.concatenate([c[10], c[11], c[9]], axis=1)


def per_device(
    block_in, seq_lengths, image_embed, w_qkv, w_out, w_up, w_down, norm_params, norm_second,
    qkv_left, qkv_right, qkv_left_root, qkv_right_root,
    out_left, out_right, out_left_root, out_right_root,
    up_left, up_right, up_left_root, up_right_root,
    down_left, down_right, down_left_root, down_right_root,
):
    micros, seqs, seq_len, width = block_in.shape
    dp_count, groups = lax.axis_size("dp"), lax.axis_size("mp")
    count = dp_count * groups
    dp_index = lax.axis_index("dp")
    me = dp_index * groups + lax.axis_index("mp")
    owned = w_up.shape[0]
    ff = w_up.shape[1]
    all_seqs = micros * seqs
    rows = all_seqs * seq_len
    tiles = rows // TILE
    seq_tile = TILE // seq_len
    direct = owned % 16 == 0

    def places(near_first):
        table = source_table(count, near_first)
        return (
            jnp.asarray(table, jnp.int32)[me],
            jnp.asarray(np.argsort(table, axis=1), jnp.int32)[me],
        )

    order, inverse = places(False)
    near_order, near_inverse = places(True)

    def weights_of(gather, inverse):
        quarters = gather.quarters()
        if direct:
            return quarters
        whole = jnp.concatenate(quarters, axis=0)[inverse]
        whole = whole.reshape(dp_count, groups, owned, whole.shape[-1])
        whole = whole.transpose(1, 0, 2, 3).reshape(groups, width, whole.shape[-1])
        return tuple(jnp.split(whole, 4, axis=0))

    kernel_order = order if direct else jnp.arange(groups, dtype=jnp.int32)
    kernel_near_order = near_order if direct else kernel_order
    kernel_inverse = inverse if direct else jnp.arange(groups, dtype=jnp.int32)
    block_rows = owned if direct else width
    quarter = (count if direct else groups) // 4

    def sum_of(quarters):
        if not direct:
            whole = jnp.concatenate(quarters, axis=0)
            whole = whole.reshape(groups, dp_count, owned, whole.shape[2])
            whole = whole.transpose(1, 0, 2, 3).reshape(count, owned, whole.shape[3])[order]
            quarters = jnp.split(whole, 4, axis=0)
        return Sum(quarters, count)

    own_blocks = [w_up.astype(BF16), w_down.astype(BF16), image_embed.reshape(all_seqs, width)]
    gather_attention = Gather(pack_attention(w_qkv.astype(BF16), w_out.astype(BF16)), count)
    gather_up, gather_down, gather_images = (Gather(block, count) for block in own_blocks)
    gather_attention.far()
    from_near = swap(jnp.concatenate(own_blocks, axis=0), near_steps(count)[0])
    from_near = jnp.split(from_near, (owned, 2 * owned), axis=0)
    for gather, received in zip((gather_up, gather_down, gather_images), from_near):
        gather.received = [received[None]]
    gather_up.keep()
    gather_attention.keep(gather_up.held)
    gather_attention.first()
    gather_up.far(gather_attention.held)

    x = block_in.reshape(rows, width)
    norms = norm_params.T
    lengths = seq_lengths.reshape(all_seqs)
    live = (jnp.arange(seq_len)[None, :] < lengths[:, None]).astype(F32).reshape(rows)
    live_cols = jnp.broadcast_to(live[:, None], (rows, LANES))
    tile_seqs = LANES // seq_len
    live_keys = live.reshape(rows // LANES, tile_seqs, 1, seq_len)
    live_keys = jnp.broadcast_to(
        live_keys, (rows // LANES, tile_seqs, seq_len, seq_len)
    ).transpose(0, 3, 1, 2).reshape(rows // LANES, seq_len, LANES)
    live_keys = jnp.concatenate([live_keys, live_keys], axis=2)
    counts = jnp.broadcast_to(lengths.astype(F32)[:, None], (all_seqs, LANES))

    live_spec = rows_of(LANES)
    keys_spec = pl.BlockSpec((TILE // LANES, seq_len, 2 * LANES), lambda i: (i, 0, 0))
    lse_spec = pl.BlockSpec((TILE // LANES, 8, 2 * LANES), lambda i: (i, 0, 0))
    norm_spec = fixed((4, width))

    def weight_scratch(cols):
        return [pltpu.VMEM((groups, width, cols), BF16), pltpu.SemaphoreType.DMA((groups,))]

    packed = 6 * LANES
    (x_ready,) = after([x], gather_attention.held)
    h1 = pl.pallas_call(
        first_norm,
        grid=(tiles,),
        in_specs=[rows_of(width), norm_spec],
        out_specs=rows_of(width),
        out_shape=shape_of(rows, width),
        compiler_params=params(),
        cost_estimate=cost(1, 100e6),
        name="first_norm",
    )(x_ready, norms)

    gather_attention.keep(h1)
    gather_attention.held, *gather_up.received = join(
        gather_attention.held, *gather_up.received[:-1]
    ) + (gather_up.received[-1],)
    gather_attention.second()
    gather_attention.third()
    gather_attention.across, *gather_up.received = join(
        gather_attention.across, *gather_up.received
    )
    gather_attention.last()
    gather_up.keep()
    gather_up.second(gather_attention.across)
    gather_up.third()
    attention_w = weights_of(gather_attention, inverse)
    gather_down.keep()
    gather_down.far(gather_up.held)

    (h1_ready,) = after([h1], gather_up.held)
    proj, heads, lse, mid, h2 = pl.pallas_call(
        functools.partial(attention_forward, seq_len=seq_len),
        grid=(tiles,),
        in_specs=[SMEM, rows_of(width), rows_of(width), keys_spec, norm_spec, ANY, ANY, ANY, ANY],
        out_specs=(
            rows_of(3 * width), rows_of(groups * 2 * LANES), lse_spec, rows_of(width),
            rows_of(width),
        ),
        out_shape=(
            shape_of(rows, 3 * width), shape_of(rows, groups * 2 * LANES),
            shape_of(rows // LANES, 8, 2 * LANES, dtype=F32),
            shape_of(rows, width, dtype=F32), shape_of(rows, width),
        ),
        scratch_shapes=weight_scratch(packed),
        compiler_params=params(),
        cost_estimate=cost(2 * rows * width * groups * 900, 12e6),
        name="attention_forward",
    )(kernel_order, x, h1_ready, live_keys, norms, *attention_w)

    gather_down.keep(h2)
    gather_up.last(gather_down.held)
    gather_down.second()
    gather_down.third()
    gather_images.keep()
    gather_images.far(gather_down.held)
    up_w = weights_of(gather_up, near_inverse)
    (h2_ready,) = after([h2], gather_down.held)

    hid, slope, pooled_hid = pl.pallas_call(
        functools.partial(up_forward, seq_len=seq_len),
        grid=(tiles,),
        in_specs=[SMEM, rows_of(width), live_spec, ANY, ANY, ANY, ANY],
        out_specs=(rows_of(groups * ff), rows_of(groups * ff), rows_of(groups * ff, seq_tile)),
        out_shape=(
            shape_of(rows, groups * ff), shape_of(rows, groups * ff), shape_of(all_seqs, groups * ff),
        ),
        scratch_shapes=weight_scratch(ff),
        compiler_params=params(),
        cost_estimate=cost(2 * rows * width * groups * ff, 20e6),
        name="up_forward",
    )(kernel_near_order, h2_ready, live_cols, *up_w)

    gather_images.keep(hid)
    gather_down.last(hid, gather_images.held)
    gather_images.second(gather_down.across)
    gather_images.third()
    down_w = weights_of(gather_down, near_inverse)
    (hid_ready,) = after([hid], gather_images.held)

    block_out, pooled = pl.pallas_call(
        functools.partial(down_forward, seq_len=seq_len),
        grid=(tiles,),
        in_specs=[SMEM, rows_of(groups * ff), rows_of(width), live_spec, ANY, ANY, ANY, ANY],
        out_specs=(rows_of(width), rows_of(width, seq_tile)),
        out_shape=(shape_of(rows, width), shape_of(all_seqs, width, dtype=F32)),
        scratch_shapes=weight_scratch(ff),
        compiler_params=params(),
        cost_estimate=cost(2 * rows * width * groups * ff, 20e6),
        name="down_forward",
    )(kernel_near_order, hid_ready, mid, live_cols, *down_w)

    gather_images.last(pooled)
    images = gather_images.quarters()
    images = [part.reshape(-1, width) for part in images]
    loss, grad_seq, grad_low = pl.pallas_call(
        functools.partial(contrast, micros=micros),
        in_specs=[WHOLE] * 6,
        out_specs=(WHOLE,) * 3,
        out_shape=(
            shape_of(all_seqs, LANES, dtype=F32), shape_of(all_seqs, width, dtype=F32),
            shape_of(all_seqs, width),
        ),
        compiler_params=params(),
        cost_estimate=cost(4 * all_seqs * width * images[0].shape[0] * 4, 4e6),
        name="contrast",
    )(pooled, counts, *images)

    gradient_out = (shape_of(quarter, block_rows, packed),) * 4

    def gradient(kernel, lefts, rights, widths):
        depth = lefts[0].shape[0]
        specs = [
            (fixed((depth, width)), pl.BlockSpec((depth, cols), lambda i: (0, i)))
            for cols in widths
        ]
        return pl.pallas_call(
            kernel,
            grid=(groups,),
            in_specs=[SMEM] + [spec for pair in specs for spec in pair],
            out_specs=(ANY,) * 4,
            out_shape=gradient_out,
            scratch_shapes=[pltpu.VMEM((width, depth), BF16) for _ in lefts]
            + [pltpu.VMEM((2, width, packed), BF16), pltpu.SemaphoreType.DMA((2,))],
            compiler_params=params(),
            cost_estimate=cost(2 * depth * width * groups * 900, 10e6),
            name=kernel.__name__,
        )(kernel_inverse, *(part for pair in zip(lefts, rights) for part in pair))

    sum_down = sum_of(gradient(weight_gradient, (grad_low,), (pooled_hid,), (ff,)))

    by_seq = pl.pallas_call(
        down_backward,
        in_specs=[SMEM, WHOLE, ANY, ANY, ANY, ANY],
        out_specs=WHOLE,
        out_shape=shape_of(all_seqs, groups * ff, dtype=F32),
        scratch_shapes=weight_scratch(ff),
        compiler_params=params(),
        cost_estimate=cost(8 * all_seqs * width * groups * ff, 6e6),
        name="down_backward",
    )(kernel_near_order, grad_low, *down_w)

    sum_down.second(by_seq)
    (grad_ready,) = after([grad_seq], sum_down.going)
    dup, dmid, dmid_low, sums_two = pl.pallas_call(
        functools.partial(mlp_backward, seq_len=seq_len),
        grid=(tiles,),
        in_specs=[
            SMEM, rows_of(width, seq_tile), rows_of(groups * ff, seq_tile), rows_of(groups * ff),
            live_spec, rows_of(width), norm_spec, ANY, ANY, ANY, ANY,
        ],
        out_specs=(rows_of(groups * ff), rows_of(width), rows_of(width), fixed((8, width))),
        out_shape=(
            shape_of(rows, groups * ff), shape_of(rows, width, dtype=F32), shape_of(rows, width),
            shape_of(8, width, dtype=F32),
        ),
        scratch_shapes=weight_scratch(ff),
        compiler_params=params(),
        cost_estimate=cost(2 * rows * width * groups * ff, 25e6),
        name="mlp_backward",
    )(kernel_near_order, grad_ready, by_seq, slope, live_cols, mid, norms, *up_w)

    sum_down.first(dmid)
    (h2_ready,) = after([h2], sum_down.going)
    up_parts = gradient(weight_gradient, (h2_ready,), (dup,), (ff,))
    *up_parts, sum_down.received = join(*up_parts, sum_down.received)
    sum_up = sum_of(up_parts)
    sum_down.far()
    sum_up.second()

    def backward(start, ready, earlier=()):
        return pl.pallas_call(
            functools.partial(attention_backward, seq_len=seq_len),
            grid=(tiles,),
            in_specs=[
                SMEM, rows_of(width, start=start),
                pl.BlockSpec((TILE // LANES, seq_len, 2 * LANES), lambda i: (i + start, 0, 0)),
                norm_spec, rows_of(3 * width, start=start),
                pl.BlockSpec((TILE // LANES, 8, 2 * LANES), lambda i: (i + start, 0, 0)),
                rows_of(width, start=start), rows_of(width, start=start),
            ] + [ANY] * (4 + len(earlier)),
            out_specs=(
                rows_of(groups * 5 * LANES, start=start), rows_of(width, start=start),
                fixed((8, width)),
            ),
            out_shape=(
                shape_of(rows, groups * 5 * LANES), shape_of(rows, width, dtype=F32),
                shape_of(8, width, dtype=F32),
            ),
            scratch_shapes=weight_scratch(packed),
            input_output_aliases={12 + i: i for i in range(len(earlier))},
            compiler_params=params(),
            cost_estimate=cost(rows * width * groups * 1300, 20e6),
            name="attention_backward",
        )(
            kernel_order, ready, live_keys, norms, proj, lse, dmid, dmid_low, *attention_w, *earlier
        )

    (x_ready,) = after([x], sum_up.going, sum_down.going)
    dproj, input_grad, sums_one = backward(0, x_ready)
    sum_up.first(sums_one)
    norm_sum = jnp.concatenate([sums_one[:2], sums_two[:2]], axis=0)

    def exchanged(values, bit):
        return swap(values, [i ^ bit for i in range(count)])

    (h1_ready,) = after([h1], sum_up.going, *sum_down.keep)
    received = exchanged(norm_sum, 1)
    attention_parts = gradient(
        attention_gradient, (h1_ready, dmid_low), (dproj, heads), (5 * LANES, 2 * LANES)
    )
    *attention_parts, sum_up.received, received = join(
        *attention_parts, sum_up.received, received
    )
    norm_sum = norm_sum + received
    sum_attention = sum_of(attention_parts)
    sum_attention.second()
    sum_up.far()
    sum_down.keep = after(sum_down.keep, sum_attention.going)
    grad_down, down_left_new, down_right_new, down_new = shampoo(
        sum_down.keep, down_left, down_right, down_left_root, down_right_root, w_down
    )
    (norm_sum,) = after([norm_sum], sum_attention.going)
    bit = 8
    while bit < count:
        norm_sum = norm_sum + exchanged(norm_sum, bit)
        bit *= 2
    sum_attention.first(norm_sum, down_new)
    sum_up.keep = after(sum_up.keep, sum_attention.going)
    grad_up, up_left_new, up_right_new, up_new = shampoo(
        sum_up.keep, up_left, up_right, up_left_root, up_right_root, w_up
    )
    sum_attention.far(up_new)
    (norm_sum,) = after([norm_sum], sum_attention.going)
    for bit in (2, 4):
        norm_sum = norm_sum + exchanged(norm_sum, bit)
    *sum_attention.keep, norm_sum = join(*sum_attention.keep, norm_sum)
    grad_norm = lax.dynamic_slice_in_dim(norm_sum, dp_index * owned, owned, 1).T

    qkv_turned = w_qkv.transpose(1, 0, 2)
    (
        grad_qkv, qkv_left_new, qkv_right_new, qkv_new,
        grad_out, out_left_new, out_right_new, out_new,
    ) = pl.pallas_call(
        attention_shampoo,
        grid=(1,),
        in_specs=[pl.BlockSpec((1, owned, packed), lambda i: (0, 0, 0))] * len(sum_attention.keep)
        + [WHOLE] * 10,
        out_specs=(WHOLE,) * 8,
        out_shape=(
            shape_of(*qkv_turned.shape, dtype=F32), shape_of(owned, owned, dtype=F32),
            shape_of(*qkv_right.shape[2:], dtype=F32), shape_of(*qkv_turned.shape, dtype=F32),
            shape_of(*w_out.shape, dtype=F32), shape_of(owned, owned, dtype=F32),
            shape_of(*out_right.shape[2:], dtype=F32), shape_of(*w_out.shape, dtype=F32),
        ),
        compiler_params=params(),
        cost_estimate=cost(4 * owned * 576 * 576, 12 * 576 * 576),
        name="attention_shampoo",
    )(
        *sum_attention.keep, qkv_turned, w_out,
        *(
            stat[0, 0]
            for stat in (
                qkv_left, qkv_right, qkv_left_root, qkv_right_root,
                out_left, out_right, out_left_root, out_right_root,
            )
        ),
    )
    grad_qkv, qkv_new = grad_qkv.transpose(1, 0, 2), qkv_new.transpose(1, 0, 2)
    qkv_left_new, qkv_right_new, out_left_new, out_right_new = (
        stat[None, None] for stat in (qkv_left_new, qkv_right_new, out_left_new, out_right_new)
    )
    norm_second_new = STAT_DECAY * norm_second + (1.0 - STAT_DECAY) * grad_norm * grad_norm
    own_params = lax.dynamic_slice_in_dim(norm_params, dp_index * owned, owned, 0)
    norm_new = own_params - NORM_RATE * grad_norm / (jnp.sqrt(norm_second_new) + 1e-08)
    return (
        block_out.reshape(block_in.shape),
        input_grad.reshape(block_in.shape),
        loss[:, 0].reshape(micros, seqs),
        grad_qkv, qkv_left_new, qkv_right_new, qkv_new,
        grad_out, out_left_new, out_right_new, out_new,
        grad_up, up_left_new, up_right_new, up_new,
        grad_down, down_left_new, down_right_new, down_new,
        grad_norm, norm_second_new, norm_new,
    )


def solution(mesh):
    sequence = P(None, AXES)
    stat = P("dp", "mp", None, None)
    weight = P("dp", "mp")
    qkv = P("dp", None, "mp")
    norm = P("dp", None)
    in_specs = (sequence, sequence, sequence, qkv, weight, weight, weight, P(), norm) + (stat,) * 16
    out_specs = (
        (sequence, sequence, sequence)
        + (qkv, stat, stat, qkv)
        + (weight, stat, stat, weight) * 3
        + (norm, norm, norm)
    )
    return jax.shard_map(
        per_device, mesh=mesh, in_specs=in_specs, out_specs=out_specs, check_vma=False
    )
```

```python
import functools
import math

import jax
import jax.numpy as jnp
import numpy as np
from jax import lax
from jax.experimental import pallas as pl
from jax.experimental.pallas import tpu as pltpu
from jax.sharding import PartitionSpec as P

AXES = ("dp", "mp")
HD = 64
LANES = 128
EPSILON = 1e-06
SOFTMAX_TEMP = 2.0
LOSS_SCALE = 32.0
STAT_DECAY = 0.5
SHAMPOO_RATE = 0.3
NORM_RATE = 0.5
TILE = 256
VMEM_BYTES = 56 * 1024 * 1024
F32 = jnp.float32
BF16 = jnp.bfloat16


def far_digits(count):
    digits = []
    weight = 8
    while weight < count:
        size = min(4, count // weight)
        digits.append((weight, size))
        weight *= size
    return digits


def near_steps(count):
    return (
        [i ^ (4 if i % 2 == 0 else 2) for i in range(count)],
        [i ^ (2 if i % 2 == 0 else 4) for i in range(count)],
        [i ^ 1 for i in range(count)],
    )


def far_steps(count, weight, size):
    return [[i ^ (weight * m) for i in range(count)] for m in range(1, size)]


def source_table(count, near_first):
    first, second, third = near_steps(count)
    far = [far_steps(count, weight, size) for weight, size in far_digits(count)]
    rounds = [[first]] + far if near_first else far + [[first]]
    table = np.arange(count)[:, None]
    for steps in rounds + [[second], [third]]:
        table = np.concatenate([table] + [table[np.array(step)] for step in steps], axis=1)
    return table


def swap(values, step):
    return lax.ppermute(values, AXES, list(enumerate(step)))


class Gather:
    def __init__(self, block, count):
        self.count = count
        self.near = near_steps(count)
        self.held = block[None]
        self.received = []

    def keep(self, *earlier):
        if self.received:
            self.received = after(self.received, *earlier)
            self.held = jnp.concatenate([self.held] + self.received, axis=0)
            self.received = []

    def far(self, *earlier):
        (self.held,) = after([self.held], *earlier)
        for weight, size in far_digits(self.count):
            self.keep()
            steps = far_steps(self.count, weight, size)
            self.received = [swap(self.held, step) for step in steps]

    def first(self, *earlier):
        (self.held,) = after([self.held], *earlier)
        self.received = [swap(self.held, self.near[0])]

    def second(self, *earlier):
        (self.held,) = after([self.held], *earlier)
        self.across = swap(self.held, self.near[1])

    def third(self, *earlier):
        (self.held,) = after([self.held], *earlier)
        self.held_other = swap(self.held, self.near[2])

    def last(self, *earlier):
        (self.across,) = after([self.across], *earlier)
        self.across_other = swap(self.across, self.near[2])

    def quarters(self):
        return self.held, self.across, self.held_other, self.across_other


def join(*values):
    return lax.optimization_barrier(values)


def after(values, *earlier, keep=None):
    if not earlier:
        return list(values)
    return list(lax.optimization_barrier((*values, *earlier)))[: keep or len(values)]


def add_low(*terms):
    return sum(term.astype(F32) for term in terms).astype(BF16)


class Sum:
    def __init__(self, quarters, count):
        self.count = count
        self.near = near_steps(count)
        self.held, self.across, held_other, across_other = quarters
        self.from_across = swap(across_other, self.near[2])
        self.from_held = swap(held_other, self.near[2])

    def second(self, *earlier):
        (received,) = after([self.from_across], *earlier)
        self.going = add_low(self.across, received)
        self.received = swap(self.going, self.near[1])

    def first(self, *earlier):
        (received,) = after([self.received], *earlier)
        half = self.held.shape[0] // 2
        terms = self.held, self.from_held, received
        self.going = add_low(*(term[half:] for term in terms))
        self.keep = add_low(*(term[:half] for term in terms))
        self.received = swap(self.going, self.near[0])

    def far(self, *earlier):
        (received,) = after([self.received], *earlier)
        keep = [self.keep, received]
        for weight, size in far_digits(self.count)[::-1]:
            step_size = keep[0].shape[0] // size
            parts = [
                add_low(*(term[m * step_size : (m + 1) * step_size] for term in keep))
                for m in range(1, size)
            ]
            keep = [term[:step_size] if step_size > 1 else term for term in keep] + [
                swap(part, step)
                for part, step in zip(parts, far_steps(self.count, weight, size))
            ]
        self.going = parts[-1]
        self.keep = keep


def dot(left, right, left_dim, right_dim):
    return lax.dot_general(
        left, right, (((left_dim,), (right_dim,)), ((), ())), preferred_element_type=F32
    )


def load_weights(places, parts, weights, sems, first=0):
    size, rows, _ = parts[0].shape
    groups, _, cols = weights.shape
    me = places[2 * size * len(parts)]

    def body(q, carry):
        for i, part in enumerate(parts):
            index = places[i * size + q] ^ me
            group = index % groups
            place = pl.multiple_of((index // groups) * rows, 16)
            pltpu.make_async_copy(
                part.at[q, :, pl.ds(first, cols)],
                weights.at[group, pl.ds(place, rows), :],
                sems.at[group],
            ).start()
        return carry

    lax.fori_loop(0, size, body, 0)


def store_blocks(places, source, group, groups, parts, sem):
    size, rows, _ = parts[0].shape
    count = size * len(parts)
    me = places[2 * count]

    def body(p, carry):
        position = places[count + ((p * groups + group) ^ me)]
        block = source.at[pl.ds(pl.multiple_of(p * rows, 16), rows), :]
        for i, part in enumerate(parts):

            @pl.when(jnp.logical_and(position >= i * size, position < (i + 1) * size))
            def _():
                pltpu.make_async_copy(block, part.at[position - i * size], sem).start()

        return carry

    lax.fori_loop(0, source.shape[0] // rows, body, 0)


def wait_weights(weights, sems, group):
    pltpu.make_async_copy(weights.at[group], weights.at[group], sems.at[group]).wait()


def normalize(values):
    center = values - jnp.mean(values, axis=-1, keepdims=True)
    spread = jnp.mean(center * center, axis=-1, keepdims=True)
    scale = lax.rsqrt(spread + EPSILON)
    return center * scale, scale


def low_lanes(dtype=BF16):
    lane = lax.broadcasted_iota(jnp.int32, (1, LANES), 1)
    return jnp.where(lane < HD, 1.0, 0.0).astype(dtype)


def pairs_of(blocks, low):
    first, second = blocks

    def join(left, right, high_half):
        if high_half:
            return jnp.where(low, turn(left), right)
        return jnp.where(low, left, turn(right))

    return (
        (first[0], first[1], first[2]),
        (second[0], second[1], second[2]),
        (
            join(first[3], second[3], False),
            join(first[4], second[4], False),
            join(first[3], second[3], True),
        ),
    )


def turn(values):
    return jnp.concatenate([values[:, HD:], values[:, :HD]], axis=1)


def both_heads(values, low_mask, high_mask):
    return jnp.concatenate([values * low_mask, values * high_mask], axis=0)


def diagonal(full, seq_len, own_cols):
    picked = full[:seq_len]
    for i, own in enumerate(own_cols):
        if i:
            picked = jnp.where(own, full[i * seq_len : (i + 1) * seq_len], picked)
    return picked


def undiagonal(compact, own_cols):
    return jnp.concatenate(
        [jnp.where(own, compact, jnp.zeros_like(compact)) for own in own_cols], axis=0
    )


def sequence_columns(seq_len):
    lane = lax.broadcasted_iota(jnp.int32, (seq_len, 2 * LANES), 1) % LANES
    return [lane // seq_len == i for i in range(LANES // seq_len)]


def stack_heads(values):
    return jnp.concatenate([values[:, :LANES], values[:, LANES:]], axis=0)


def spread(values, seq_len):
    seqs, width = values.shape
    return jnp.broadcast_to(values[:, None, :], (seqs, seq_len, width)).reshape(
        seqs * seq_len, width
    )


def live_column(counts, seq_len):
    wide = spread(counts, seq_len)
    slot = lax.broadcasted_iota(jnp.int32, wide.shape, 0) % seq_len
    return jnp.where(slot.astype(F32) < wide, 1.0, 0.0)[:, 0:1]


def first_norm(x_ref, norm_ref, *rest):
    h1_ref = rest[-1]
    n1, _ = normalize(x_ref[...].astype(F32))
    h1_ref[...] = (n1 * norm_ref[0:1, :] + norm_ref[1:2, :]).astype(BF16)


def attention_forward(
    order, x_ref, h1_ref, live_ref, norm_ref, w0, w1, w2, w3,
    proj_ref, heads_ref, lse_ref, mid_ref, h2_ref,
    weights, sems, *, seq_len,
):
    groups = weights.shape[0]
    first = pl.program_id(0) == 0

    @pl.when(first)
    def _():
        load_weights(order, (w0, w1, w2, w3), weights, sems)
        for group in range(weights.shape[0]):
            wait_weights(weights, sems, group)

    x = x_ref[...].astype(F32)
    rows = x.shape[0]
    h1 = h1_ref[...]
    low_mask = low_lanes()
    high_mask = 1 - low_mask
    low = lax.broadcasted_iota(jnp.int32, (1, LANES), 1) < HD
    own_cols = sequence_columns(seq_len)
    count = rows // LANES
    duos = groups // 2
    projected = [
        dot(h1, weights[group, :, : 5 * LANES], 1, 0).astype(BF16) for group in range(groups)
    ]
    chains = []
    for duo in range(duos):
        for t in range(count):
            span = slice(t * LANES, (t + 1) * LANES)
            blocks = [
                [proj[span, i * LANES : (i + 1) * LANES] for i in range(5)]
                for proj in projected[2 * duo : 2 * duo + 2]
            ]
            for i, (q, k, v) in enumerate(pairs_of(blocks, low)):
                for which, part in enumerate((q, k, v)):
                    at = ((duo * 3 + i) * 3 + which) * LANES
                    proj_ref[span, at : at + LANES] = part
                chains.append((t, duo * 3 + i, q, k, v))
    scores = [dot(k, both_heads(q, low_mask, high_mask), 1, 1) for t, i, q, k, v in chains]
    probs = []
    for (t, i, *_), full in zip(chains, scores):
        compact = diagonal(full, seq_len, own_cols) * (HD**-0.5)
        compact = jnp.where(live_ref[t] > 0.0, compact, -1e30)
        top = jnp.max(compact, axis=0, keepdims=True)
        powers = jnp.exp(compact - top)
        power = jnp.sum(powers, axis=0, keepdims=True)
        lse_ref[t, i : i + 1, :] = top + jnp.log(power)
        probs.append(undiagonal((powers * (1.0 / power)).astype(BF16), own_cols))
    outs = [
        dot(stack_heads(part), both_heads(v, low_mask, high_mask), 0, 0)
        for part, (t, i, q, k, v) in zip(probs, chains)
    ]
    total = x
    for duo in range(duos):
        heads = [[], []]
        for t in range(count):
            at = 3 * (duo * count + t)
            one, two, third = outs[at : at + 3]
            heads[0].append(
                jnp.concatenate([jnp.where(low, 0.0, turn(third)), one], axis=1).astype(BF16)
            )
            heads[1].append(
                jnp.concatenate([jnp.where(low, 0.0, third), two], axis=1).astype(BF16)
            )
        for side, group in enumerate((2 * duo, 2 * duo + 1)):
            joined = jnp.concatenate(heads[side], axis=0)
            heads_ref[:, group * 2 * LANES : (group + 1) * 2 * LANES] = joined
            total = total + dot(joined, weights[group, :, 4 * LANES :], 1, 1)
    mid_ref[...] = total
    n2, _ = normalize(total)
    h2_ref[...] = (n2 * norm_ref[2:3, :] + norm_ref[3:4, :]).astype(BF16)


def up_forward(
    places, h2_ref, count_ref, w0, w1, w2, w3,
    hid_ref, slope_ref, pooled_ref,
    weights, sems, *, seq_len,
):
    groups, _, wide = weights.shape

    @pl.when(pl.program_id(0) == 0)
    def _():
        load_weights(places, (w0, w1, w2, w3), weights, sems)
        for group in range(groups):
            wait_weights(weights, sems, group)

    h2 = h2_ref[...]
    rows = h2.shape[0]
    counts = count_ref[...]
    live = live_column(counts, seq_len)
    seqs = rows // seq_len
    slot = lax.broadcasted_iota(jnp.int32, (seqs, rows), 1)
    member = slot // seq_len == lax.broadcasted_iota(jnp.int32, (seqs, rows), 0)
    within = (slot % seq_len).astype(F32) < counts[:, 0:1]
    pool = jnp.where(jnp.logical_and(member, within), 1.0, 0.0).astype(BF16)
    for group in range(groups):
        cols = slice(group * wide, (group + 1) * wide)
        up = dot(h2, weights[group], 1, 0)
        gate = 0.5 + 0.5 * lax.erf(up * (0.5**0.5))
        hid = (up * gate).astype(BF16)
        hid_ref[:, cols] = hid
        bell = jnp.exp(up * up * -0.5) * (1.0 / math.sqrt(2.0 * math.pi))
        slope_ref[:, cols] = ((gate + up * bell) * live).astype(BF16)
        pooled_ref[:, cols] = dot(pool, hid, 1, 0).astype(BF16)


def down_forward(
    order, hid_ref, mid_ref, count_ref, w0, w1, w2, w3,
    out_ref, pooled_ref, weights, sems, *, seq_len,
):
    groups, _, width = weights.shape
    first = pl.program_id(0) == 0

    @pl.when(first)
    def _():
        load_weights(order, (w0, w1, w2, w3), weights, sems)
        for group in range(weights.shape[0]):
            wait_weights(weights, sems, group)

    total = mid_ref[...]
    for group in range(groups):


        total = total + dot(
            hid_ref[:, group * width : (group + 1) * width], weights[group], 1, 1
        )
    out_ref[...] = total.astype(BF16)
    rows, features = total.shape
    counts = count_ref[...]
    live = live_column(counts, seq_len)
    seqs = rows // seq_len
    sums = jnp.sum((total * live).reshape(seqs, seq_len, features), axis=1)
    pooled_ref[...] = sums / counts[:, 0:1]


def loss_backward(
    places, pooled_ref, count_ref, m0, m1, m2, m3, hid_ref,
    loss_ref, grad_ref, low_ref, g0, g1, g2, g3,
    slots, slot_sems, *, micros, groups,
):
    ff = slots.shape[2]
    pooled = pooled_ref[...]
    seqs, width = pooled.shape
    each = seqs // micros
    scale_text = SOFTMAX_TEMP / math.sqrt(width)
    r = lax.rsqrt(jnp.mean(pooled * pooled, axis=-1, keepdims=True) + EPSILON)
    text = (pooled * r).astype(BF16)
    row_micro = lax.broadcasted_iota(jnp.int32, (seqs, 1), 0) // each
    step = min(m0.shape[0], 1024)
    pieces = [
        ref[i : i + step, :]
        for ref in (m0, m1, m2, m3)
        for i in range(0, ref.shape[0], step)
    ]
    col = lax.broadcasted_iota(jnp.int32, (1, step), 1)
    same = (col // each) % micros == row_micro
    logits = [jnp.where(same, dot(text, piece, 1, 1) * scale_text, -1e30) for piece in pieces]
    top = functools.reduce(
        jnp.maximum, [jnp.max(part, axis=1, keepdims=True) for part in logits]
    )
    powers = [jnp.exp(part - top) for part in logits]
    total = functools.reduce(jnp.add, [jnp.sum(part, axis=1, keepdims=True) for part in powers])
    log_total = top + jnp.log(total)
    positive = lax.broadcasted_iota(jnp.int32, (seqs, 1), 0) == col
    loss = log_total - jnp.sum(jnp.where(positive, logits[0], 0.0), axis=1, keepdims=True)
    loss_ref[...] = jnp.broadcast_to(loss, loss_ref.shape)
    inverse = LOSS_SCALE / total
    grad_text = jnp.zeros((seqs, width), F32)
    for i, (part, piece) in enumerate(zip(powers, pieces)):
        grad_part = part * inverse
        if i == 0:
            grad_part = grad_part - jnp.where(positive, LOSS_SCALE, 0.0)
        grad_text = grad_text + dot(grad_part.astype(BF16), piece, 1, 0)
    grad_text = grad_text * scale_text
    along = jnp.mean(grad_text * pooled, axis=-1, keepdims=True)
    grad = (r * grad_text - (r * r * r) * pooled * along) / count_ref[:, 0:1]
    grad_ref[...] = grad
    low = grad.astype(BF16)
    low_ref[...] = low
    turned = low.T
    for group in range(groups):
        cols = slice(group * ff, (group + 1) * ff)
        if group >= 2:
            drain(slots, slot_sems, group % 2)
        slots[group % 2] = dot(turned, hid_ref[:, cols], 1, 0).astype(BF16)
        store_blocks(
            places, slots.at[group % 2], group, groups, (g0, g1, g2, g3),
            slot_sems.at[group % 2],
        )
    for which in range(min(groups, 2)):
        drain(slots, slot_sems, which)


def drain(slots, sems, which):
    pltpu.make_async_copy(slots.at[which], slots.at[which], sems.at[which]).wait()


def finish_blocks(slots, sems, group, groups, slot):
    @pl.when(group == groups - 1)
    def _():
        drain(slots, sems, slot)

        @pl.when(groups >= 2)
        def _():
            drain(slots, sems, 1 - slot)


def weight_gradient(places, *refs):
    pairs = (len(refs) - 6) // 3
    lefts, rights = refs[: 2 * pairs : 2], refs[1 : 2 * pairs : 2]
    parts, turned = refs[2 * pairs : 2 * pairs + 4], refs[2 * pairs + 4 : -2]
    slots, sems = refs[-2:]
    group = pl.program_id(0)
    groups = pl.num_programs(0)
    slot = group % 2

    @pl.when(group == 0)
    def _():
        for left, across in zip(lefts, turned):
            across[...] = left[...].T

    @pl.when(group >= 2)
    def _():
        drain(slots, sems, slot)

    first = 0
    for across, right in zip(turned, rights):
        last = first + right.shape[1]
        slots[slot, :, first:last] = dot(across[...], right[...], 1, 0).astype(BF16)
        first = last
    store_blocks(places, slots.at[slot], group, groups, parts, sems.at[slot])
    finish_blocks(slots, sems, group, groups, slot)


def norm_back(grad, gain, values):
    n, scale = normalize(values)
    scaled = grad * gain
    moved = scale * (
        scaled
        - jnp.mean(scaled, axis=-1, keepdims=True)
        - n * jnp.mean(scaled * n, axis=-1, keepdims=True)
    )
    gain_grad = jnp.sum(grad * n, axis=0, keepdims=True)
    shift_grad = jnp.sum(grad, axis=0, keepdims=True)
    return moved, gain_grad, shift_grad


def down_backward(order, low_ref, w0, w1, w2, w3, by_seq_ref, weights, sems):
    groups, _, width = weights.shape
    load_weights(order, (w0, w1, w2, w3), weights, sems)
    for group in range(groups):
        wait_weights(weights, sems, group)
        by_seq_ref[:, group * width : (group + 1) * width] = dot(
            low_ref[...], weights[group], 1, 0
        )


def mlp_backward(
    order, grad_ref, by_seq_ref, slope_ref, count_ref, mid_ref, norm_ref,
    w0, w1, w2, w3,
    dup_ref, dmid_ref, dmid_low_ref, sums_ref,
    weights, sems, *, seq_len,
):
    groups, _, width = weights.shape

    @pl.when(pl.program_id(0) == 0)
    def _():
        load_weights(order, (w0, w1, w2, w3), weights, sems)
        sums_ref[...] = jnp.zeros_like(sums_ref)
        for group in range(groups):
            wait_weights(weights, sems, group)

    grad = grad_ref[...]
    mid = mid_ref[...]
    rows, features = mid.shape

    total = jnp.zeros((rows, features), F32)
    for group in range(groups):


        cols = slice(group * width, (group + 1) * width)
        dup = (slope_ref[:, cols].astype(F32) * spread(by_seq_ref[:, cols], seq_len)).astype(BF16)
        dup_ref[:, cols] = dup
        total = total + dot(dup, weights[group], 1, 1)
    moved, gain_grad, shift_grad = norm_back(total, norm_ref[2:3, :], mid)
    live = live_column(count_ref[...], seq_len)
    dmid = spread(grad, seq_len) * live + moved
    dmid_ref[...] = dmid
    dmid_low_ref[...] = dmid.astype(BF16)
    sums_ref[0:1, :] += gain_grad
    sums_ref[1:2, :] += shift_grad


def attention_backward(
    places, x_ref, live_ref, norm_ref, proj_ref, lse_ref, dmid_ref, dmid_low_ref,
    w0, w1, w2, w3, dproj_ref, dx_ref, sums_ref, weights, sems, *, seq_len,
):
    groups = weights.shape[0]

    @pl.when(pl.program_id(0) == 0)
    def _():
        load_weights(places, (w0, w1, w2, w3), weights, sems)
        for group in range(groups):
            wait_weights(weights, sems, group)
        sums_ref[...] = jnp.zeros_like(sums_ref)

    x = x_ref[...].astype(F32)
    rows = x.shape[0]
    dmid_low = dmid_low_ref[...]
    low_mask = low_lanes()
    high_mask = 1 - low_mask
    low = lax.broadcasted_iota(jnp.int32, (1, LANES), 1) < HD
    own_cols = sequence_columns(seq_len)
    score_scale = HD**-0.5
    count = rows // LANES
    duos = groups // 2
    dheads = [
        dot(dmid_low, weights[group, :, 4 * LANES :], 1, 0).astype(BF16)
        for group in range(groups)
    ]
    chains = []
    for duo in range(duos):
        first_d, second_d = dheads[2 * duo : 2 * duo + 2]
        for t in range(count):
            span = slice(t * LANES, (t + 1) * LANES)
            for i, d in enumerate(
                (
                    first_d[span, LANES:],
                    second_d[span, LANES:],
                    jnp.where(low, turn(first_d[span, :LANES]), second_d[span, :LANES]),
                )
            ):
                at = (duo * 3 + i) * 3 * LANES
                q, k, v = (
                    proj_ref[span, at + j * LANES : at + (j + 1) * LANES] for j in range(3)
                )
                qq, kk, dd = (both_heads(part, low_mask, high_mask) for part in (q, k, d))
                chains.append((t, duo * 3 + i, k, v, qq, kk, dd))
    scores = [dot(k, qq, 1, 1) for t, i, k, v, qq, kk, dd in chains]
    powers = [dot(v, dd, 1, 1) for t, i, k, v, qq, kk, dd in chains]
    wide = []
    for (t, i, *_), full, power in zip(chains, scores, powers):
        live = live_ref[t] > 0.0
        compact = diagonal(full, seq_len, own_cols) * score_scale
        lse = lse_ref[t, i : i + 1, :]
        probs = jnp.where(live, jnp.exp(jnp.where(live, compact - lse, 0.0)), 0.0)
        dprobs = diagonal(power, seq_len, own_cols)
        inner = jnp.sum(probs * dprobs, axis=0, keepdims=True)
        dscores = probs * (dprobs - inner) * score_scale
        wide.append(
            (
                undiagonal(dscores.astype(BF16), own_cols),
                undiagonal(probs.astype(BF16), own_cols),
            )
        )
    outs = [
        (dot(stack_heads(ds), kk, 0, 0), dot(ds, qq, 1, 0), dot(p, dd, 1, 0))
        for (ds, p), (t, i, k, v, qq, kk, dd) in zip(wide, chains)
    ]
    total = jnp.zeros(x.shape, F32)
    for duo in range(duos):
        grads = [[], []]
        for t in range(count):
            at = 3 * (duo * count + t)
            one, two, third = outs[at : at + 3]
            grads[0].append(
                jnp.concatenate(
                    one
                    + (jnp.where(low, third[0], turn(third[2])), jnp.where(low, third[1], 0.0)),
                    axis=1,
                ).astype(BF16)
            )
            grads[1].append(
                jnp.concatenate(
                    two
                    + (jnp.where(low, turn(third[0]), third[2]), jnp.where(low, turn(third[1]), 0.0)),
                    axis=1,
                ).astype(BF16)
            )
        for side, group in enumerate((2 * duo, 2 * duo + 1)):
            dproj = jnp.concatenate(grads[side], axis=0)
            dproj_ref[:, group * 5 * LANES : (group + 1) * 5 * LANES] = dproj
            total = total + dot(dproj, weights[group, :, : 5 * LANES], 1, 1)
    moved, gain_grad, shift_grad = norm_back(total, norm_ref[0:1, :], x)
    dx_ref[...] = dmid_ref[...] + moved
    sums_ref[0:1, :] += gain_grad
    sums_ref[1:2, :] += shift_grad


def renew(grad, left, right, left_root, right_root):
    low = grad.astype(BF16)
    keep = 1.0 - STAT_DECAY
    half = dot(left_root.astype(BF16), low, 1, 0).astype(BF16)
    return (
        STAT_DECAY * left + keep * dot(low, low, 1, 1),
        STAT_DECAY * right + keep * dot(low, low, 0, 0),
        SHAMPOO_RATE * dot(half, right_root.astype(BF16), 1, 0),
    )


def shampoo_kernel(*refs):
    terms = refs[:-9]
    master_ref, *stats = refs[-9:-4]
    grad_ref, left_new_ref, right_new_ref, new_ref = refs[-4:]
    grad = sum(term[0].astype(F32) for term in terms)
    grad_ref[...] = grad
    left_new_ref[...], right_new_ref[...], step = renew(grad, *(ref[...] for ref in stats))
    new_ref[...] = master_ref[...] - step


def up_shampoo(*refs):
    terms = refs[:-18]
    up_ref, out_ref, *stats = refs[-18:-8]
    up_grad, up_left, up_right, up_new, out_grad, out_left, out_right, out_new = refs[-8:]
    packed = sum(term[0].astype(F32) for term in terms)
    wide = up_ref.shape[1]
    up, out = packed[:, :wide], unpack_out(packed[:, wide:])
    up_grad[...] = up
    up_left[...], up_right[...], step = renew(up, *(ref[...] for ref in stats[:4]))
    up_new[...] = up_ref[...] - step
    out_grad[...] = out
    out_left[...], out_right[...], step = renew(out, *(ref[...] for ref in stats[4:]))
    out_new[...] = out_ref[...] - step


def attention_shampoo(*refs):
    terms = refs[:-9]
    qkv_ref, *stats = refs[-9:-4]
    qkv_grad, qkv_left, qkv_right, qkv_new = refs[-4:]
    qkv = unpack_qkv(sum(term[0].astype(F32) for term in terms))
    qkv_left[...], qkv_right[...], step = renew(qkv, *(ref[...] for ref in stats))
    width = qkv_ref.shape[2]
    for i in range(3):
        cols = slice(i * width, (i + 1) * width)
        qkv_grad[i] = qkv[:, cols]
        qkv_new[i] = qkv_ref[i] - step[:, cols]


ANY = pl.BlockSpec(memory_space=pl.ANY)
SMEM = pl.BlockSpec(memory_space=pltpu.SMEM)
WHOLE = pl.BlockSpec(memory_space=pltpu.VMEM)


def rows_of(width, height=TILE, start=0):
    return pl.BlockSpec((height, width), lambda i: (i + start, 0))


def fixed(shape):
    return pl.BlockSpec(shape, lambda i: (0,) * len(shape))


def params():
    return pltpu.CompilerParams(vmem_limit_bytes=VMEM_BYTES)


def cost(flops, bytes_accessed):
    return pl.CostEstimate(flops=4 * int(flops), bytes_accessed=int(bytes_accessed), transcendentals=0)


def shape_of(*dims, dtype=BF16):
    return jax.ShapeDtypeStruct(dims, dtype)


def stat_shapes(rows, cols):
    return shape_of(rows, rows, dtype=F32), shape_of(cols, cols, dtype=F32)


def shampoo(kernel, terms, masters, shapes, stats):
    rows, cols = terms[0].shape[1:]
    out_shape = []
    for master, (left, right) in zip(masters, shapes):
        value = shape_of(*master.shape, dtype=F32)
        out_shape += [value, *stat_shapes(left, right), value]
    return pl.pallas_call(
        kernel,
        grid=(1,),
        out_shape=tuple(out_shape),
        in_specs=[pl.BlockSpec((1, rows, cols), lambda i: (0, 0, 0))] * len(terms)
        + [WHOLE] * (len(masters) + len(stats)),
        out_specs=(WHOLE,) * len(out_shape),
        compiler_params=params(),
        cost_estimate=cost(4 * rows * cols * cols, 12 * cols * cols),
        name=kernel.__name__,
    )(*terms, *masters, *(stat[0, 0] for stat in stats))


def pack_qkv(qkv):
    q, k, v = (qkv[:, i] for i in range(3))
    a, b = 2 * HD, 3 * HD
    third = [q[:, a:b], v[:, a:b], k[:, a:b], jnp.zeros_like(k[:, a:b])]
    return jnp.concatenate([q[:, :a], k[:, :a], v[:, :a]] + third, axis=1)


def pack_attention(qkv, out):
    packed = pack_qkv(qkv)
    return jnp.concatenate([packed[:, : 9 * HD], out[:, 2 * HD :], out[:, : 2 * HD]], axis=1)


def unpack_qkv(packed):
    c = [packed[:, i * HD : (i + 1) * HD] for i in range(10)]
    return jnp.concatenate([c[0], c[1], c[6], c[2], c[3], c[8], c[4], c[5], c[7]], axis=1)


def unpack_out(packed):
    return jnp.concatenate([packed[:, 2 * HD :], packed[:, HD : 2 * HD]], axis=1)


def per_device(
    block_in, seq_lengths, image_embed, w_qkv, w_out, w_up, w_down, norm_params, norm_second,
    qkv_left, qkv_right, qkv_left_root, qkv_right_root,
    out_left, out_right, out_left_root, out_right_root,
    up_left, up_right, up_left_root, up_right_root,
    down_left, down_right, down_left_root, down_right_root,
):
    micros, seqs, seq_len, width = block_in.shape
    dp_count, groups = lax.axis_size("dp"), lax.axis_size("mp")
    count = dp_count * groups
    dp_index = lax.axis_index("dp")
    me = dp_index * groups + lax.axis_index("mp")
    owned = w_up.shape[0]
    ff = w_up.shape[1]
    all_seqs = micros * seqs
    rows = all_seqs * seq_len
    tiles = rows // TILE
    seq_tile = TILE // seq_len
    direct = owned % 16 == 0

    def places(near_first):
        masks = source_table(count, near_first)[:2] ^ np.arange(2)[:, None]
        masks = np.concatenate([masks, np.argsort(masks, axis=1)], axis=1)
        odd = me % 2 == 1
        mine = jnp.where(odd, jnp.asarray(masks[1], jnp.int32), jnp.asarray(masks[0], jnp.int32))
        return jnp.concatenate([mine, me.astype(jnp.int32)[None]])

    far_places, near_places = places(False), places(True)

    def order_of(places):
        return places[:count] ^ me

    def inverse_of(places):
        return places[count : 2 * count][jnp.arange(count) ^ me]

    def weights_of(gather, places):
        quarters = gather.quarters()
        if direct:
            return quarters
        whole = jnp.concatenate(quarters, axis=0)[inverse_of(places)]
        whole = whole.reshape(dp_count, groups, owned, whole.shape[-1])
        whole = whole.transpose(1, 0, 2, 3).reshape(groups, width, whole.shape[-1])
        return tuple(jnp.split(whole, 4, axis=0))

    if direct:
        kernel_far, kernel_near = far_places, near_places
    else:
        plain = jnp.arange(groups, dtype=jnp.int32)
        kernel_far = kernel_near = jnp.concatenate([plain, plain, jnp.zeros(1, jnp.int32)])
    block_rows = owned if direct else width
    quarter = (count if direct else groups) // 4

    def sum_of(quarters):
        if not direct:
            whole = jnp.concatenate(quarters, axis=0)
            whole = whole.reshape(groups, dp_count, owned, whole.shape[2])
            whole = whole.transpose(1, 0, 2, 3).reshape(count, owned, whole.shape[3])[order_of(far_places)]
            quarters = jnp.split(whole, 4, axis=0)
        return Sum(quarters, count)

    def width_of(array):
        return array.shape[1]

    own_attention = pack_attention(w_qkv.astype(BF16), w_out.astype(BF16))
    own_up, own_down = w_up.astype(BF16), w_down.astype(BF16)
    own_images = image_embed.reshape(all_seqs, width)
    gather_attention, gather_up, gather_down, gather_images = (
        Gather(block, count) for block in (own_attention, own_up, own_down, own_images)
    )
    gather_attention.far()
    later = gather_down, gather_images
    for gather in later:
        gather.first()
        gather.keep()
    gather_attention.keep(*(gather.held for gather in later))
    gather_attention.first()
    gather_up.far(gather_attention.held)

    x = block_in.reshape(rows, width)
    norms = norm_params.T
    lengths = seq_lengths.reshape(all_seqs)
    live = (jnp.arange(seq_len)[None, :] < lengths[:, None]).astype(F32)
    tile_seqs = LANES // seq_len
    live_keys = live.reshape(rows // LANES, tile_seqs, 1, seq_len)
    live_keys = jnp.broadcast_to(
        live_keys, (rows // LANES, tile_seqs, seq_len, seq_len)
    ).transpose(0, 3, 1, 2).reshape(rows // LANES, seq_len, LANES)
    live_keys = jnp.concatenate([live_keys, live_keys], axis=2)
    counts = jnp.broadcast_to(lengths.astype(F32)[:, None], (all_seqs, LANES))

    count_spec = rows_of(LANES, seq_tile)
    keys_spec = pl.BlockSpec((TILE // LANES, seq_len, 2 * LANES), lambda i: (i, 0, 0))
    lse_spec = pl.BlockSpec((TILE // LANES, 8, 2 * LANES), lambda i: (i, 0, 0))
    norm_spec = fixed((4, width))
    all_ff, all_heads = groups * ff, groups * 2 * LANES
    packed = width_of(own_attention)

    def weight_scratch(cols):
        return [pltpu.VMEM((groups, width, cols), BF16), pltpu.SemaphoreType.DMA((groups,))]

    x_ready, live_keys, counts, kernel_far, kernel_near = after(
        [x, live_keys, counts, kernel_far, kernel_near], gather_attention.held
    )
    h1 = pl.pallas_call(
        first_norm,
        grid=(tiles,),
        in_specs=[rows_of(width), norm_spec],
        out_specs=rows_of(width),
        out_shape=shape_of(rows, width),
        compiler_params=params(),
        cost_estimate=cost(1, 100e6),
        name="first_norm",
    )(x_ready, norms)
    h1, live_keys, counts, kernel_far, kernel_near = join(
        h1, live_keys, counts, kernel_far, kernel_near
    )
    gather_attention.keep(h1)
    gather_attention.second()
    gather_attention.third()
    gather_up.keep(gather_attention.held)
    gather_attention.last(gather_up.held)
    gather_up.first(gather_attention.across)
    gather_down.far(gather_up.held)
    gather_up.keep(gather_attention.across)
    gather_up.second()
    gather_up.third()
    attention_w = weights_of(gather_attention, far_places)

    (h1_ready,) = after([h1], gather_up.held)
    proj, heads, lse, mid, h2 = pl.pallas_call(
        functools.partial(attention_forward, seq_len=seq_len),
        grid=(tiles,),
        in_specs=[SMEM, rows_of(width), rows_of(width), keys_spec, norm_spec, ANY, ANY, ANY, ANY],
        out_specs=(
            rows_of(3 * width), rows_of(all_heads), lse_spec, rows_of(width),
            rows_of(width),
        ),
        out_shape=(
            shape_of(rows, 3 * width), shape_of(rows, all_heads),
            shape_of(rows // LANES, 8, 2 * LANES, dtype=F32),
            shape_of(rows, width, dtype=F32), shape_of(rows, width),
        ),
        scratch_shapes=weight_scratch(packed),
        compiler_params=params(),
        cost_estimate=cost(2 * rows * width * groups * 900, 12e6),
        name="attention_forward",
    )(kernel_far, x, h1_ready, live_keys, norms, *attention_w)

    gather_down.keep(h2)
    gather_up.last(gather_down.held)
    gather_down.second()
    gather_down.third()
    gather_images.far(gather_down.held)
    up_w = weights_of(gather_up, far_places)
    (h2_ready,) = after([h2], gather_down.held)

    hid, slope, pooled_hid = pl.pallas_call(
        functools.partial(up_forward, seq_len=seq_len),
        grid=(tiles,),
        in_specs=[SMEM, rows_of(width), count_spec, ANY, ANY, ANY, ANY],
        out_specs=(rows_of(groups * ff), rows_of(groups * ff), rows_of(groups * ff, seq_tile)),
        out_shape=(
            shape_of(rows, groups * ff), shape_of(rows, groups * ff), shape_of(all_seqs, groups * ff),
        ),
        scratch_shapes=weight_scratch(ff),
        compiler_params=params(),
        cost_estimate=cost(2 * rows * width * groups * ff, 20e6),
        name="up_forward",
    )(kernel_far, h2_ready, counts, *up_w)

    gather_images.keep(hid)
    gather_down.last(hid, gather_images.held)
    gather_images.second(gather_down.across)
    gather_images.third()
    down_w = weights_of(gather_down, near_places)
    (hid_ready,) = after([hid], gather_images.held)

    block_out, pooled = pl.pallas_call(
        functools.partial(down_forward, seq_len=seq_len),
        grid=(tiles,),
        in_specs=[SMEM, rows_of(all_ff), rows_of(width), count_spec, ANY, ANY, ANY, ANY],
        out_specs=(rows_of(width), rows_of(width, seq_tile)),
        out_shape=(shape_of(rows, width), shape_of(all_seqs, width, dtype=F32)),
        scratch_shapes=weight_scratch(ff),
        compiler_params=params(),
        cost_estimate=cost(2 * rows * width * groups * ff, 20e6),
        name="down_forward",
    )(kernel_near, hid_ready, mid, counts, *down_w)

    gather_images.last(pooled)
    images = [part.reshape(-1, width) for part in gather_images.quarters()]

    def quarters_of(cols):
        return (shape_of(quarter, block_rows, cols),) * 4

    loss, grad_seq, grad_low, *down_parts = pl.pallas_call(
        functools.partial(loss_backward, micros=micros, groups=groups),
        in_specs=[SMEM] + [WHOLE] * 7,
        out_specs=(WHOLE,) * 3 + (ANY,) * 4,
        out_shape=(
            shape_of(all_seqs, LANES, dtype=F32), shape_of(all_seqs, width, dtype=F32),
            shape_of(all_seqs, width),
        ) + quarters_of(ff),
        scratch_shapes=[pltpu.VMEM((2, width, ff), BF16), pltpu.SemaphoreType.DMA((2,))],
        compiler_params=params(),
        cost_estimate=cost(8 * all_seqs * width * groups * ff, 20e6),
        name="loss_backward",
    )(kernel_far, pooled, counts, *images, pooled_hid)
    sum_down = sum_of(down_parts)

    by_seq = pl.pallas_call(
        down_backward,
        in_specs=[SMEM, WHOLE, ANY, ANY, ANY, ANY],
        out_specs=WHOLE,
        out_shape=shape_of(all_seqs, all_ff, dtype=F32),
        scratch_shapes=weight_scratch(ff),
        compiler_params=params(),
        cost_estimate=cost(8 * all_seqs * width * groups * ff, 6e6),
        name="down_backward",
    )(kernel_near, grad_low, *down_w)
    by_seq, sum_down.from_across = join(by_seq, sum_down.from_across)
    sum_down.second()
    (grad_seq,) = after([grad_seq], sum_down.going)

    dup, dmid, dmid_low, sums_two = pl.pallas_call(
        functools.partial(mlp_backward, seq_len=seq_len),
        grid=(tiles,),
        in_specs=[
            SMEM, rows_of(width, seq_tile), rows_of(groups * ff, seq_tile), rows_of(groups * ff),
            count_spec, rows_of(width), norm_spec, ANY, ANY, ANY, ANY,
        ],
        out_specs=(rows_of(groups * ff), rows_of(width), rows_of(width), fixed((8, width))),
        out_shape=(
            shape_of(rows, groups * ff), shape_of(rows, width, dtype=F32), shape_of(rows, width),
            shape_of(8, width, dtype=F32),
        ),
        scratch_shapes=weight_scratch(ff),
        compiler_params=params(),
        cost_estimate=cost(2 * rows * width * groups * ff, 25e6),
        name="mlp_backward",
    )(kernel_far, grad_seq, by_seq, slope, counts, mid, norms, *up_w)

    def gradient(name, *pairs):
        cols = [right.shape[1] // groups for _, right in pairs]
        return pl.pallas_call(
            weight_gradient,
            grid=(groups,),
            in_specs=[SMEM] + [
                spec
                for wide in cols
                for spec in (
                    fixed((rows, width)), pl.BlockSpec((rows, wide), lambda i: (0, i))
                )
            ],
            out_specs=(ANY,) * 4,
            out_shape=quarters_of(sum(cols)),
            scratch_shapes=[pltpu.VMEM((width, rows), BF16) for _ in pairs]
            + [pltpu.VMEM((2, width, sum(cols)), BF16), pltpu.SemaphoreType.DMA((2,))],
            compiler_params=params(),
            cost_estimate=cost(2 * rows * width * groups * 900, 10e6),
            name=name,
        )(kernel_far, *(part for pair in pairs for part in pair))

    dmid, sum_down.received = join(dmid, sum_down.received)
    sum_down.first()
    (h2_ready,) = after([h2], sum_down.going)
    up_parts = gradient("up_gradient", (h2_ready, dup), (dmid_low, heads))
    *up_parts, sum_down.received = join(*up_parts, sum_down.received)
    sum_up = sum_of(up_parts)
    sum_down.far()
    (sum_up.from_across,) = after([sum_up.from_across], sum_down.going)
    sum_up.second()

    (x_ready,) = after([x], sum_up.going)
    dproj, input_grad, sums_one = pl.pallas_call(
        functools.partial(attention_backward, seq_len=seq_len),
        grid=(tiles,),
        in_specs=[
            SMEM, rows_of(width), keys_spec, norm_spec, rows_of(3 * width), lse_spec,
            rows_of(width), rows_of(width), ANY, ANY, ANY, ANY,
        ],
        out_specs=(rows_of(groups * 5 * LANES), rows_of(width), fixed((8, width))),
        out_shape=(
            shape_of(rows, groups * 5 * LANES), shape_of(rows, width, dtype=F32),
            shape_of(8, width, dtype=F32),
        ),
        scratch_shapes=weight_scratch(packed),
        compiler_params=params(),
        cost_estimate=cost(2 * rows * width * groups * 1300, 20e6),
        name="attention_backward",
    )(kernel_far, x_ready, live_keys, norms, proj, lse, dmid, dmid_low, *attention_w)

    def exchanged(values, bit):
        return swap(values, [i ^ bit for i in range(count)])

    sums_one, sum_up.received, sum_down.keep = join(sums_one, sum_up.received, sum_down.keep)
    norm_sum = jnp.concatenate([sums_one[:2], sums_two[:2]], axis=0)
    received = exchanged(norm_sum, 1)
    sum_up.first()
    (received,) = after([received], sum_up.going)
    norm_sum = norm_sum + received
    received = exchanged(norm_sum, 8)
    (h1_ready,) = after([h1], sum_up.going, norm_sum)
    attention_parts = gradient("attention_gradient", (h1_ready, dproj))
    *attention_parts, received, sum_up.received = join(
        *attention_parts, received, sum_up.received
    )
    norm_sum = norm_sum + received
    sum_attention = sum_of(attention_parts)
    if count > 16:
        sum_attention.from_across, received = join(
            sum_attention.from_across, exchanged(norm_sum, 16)
        )
        norm_sum = norm_sum + received
    sum_attention.second()
    sum_up.far(sum_attention.going)
    bit = 32
    while bit < count:
        norm_sum = norm_sum + exchanged(norm_sum, bit)
        bit *= 2
    received = exchanged(norm_sum, 2)
    sum_down.keep = after(sum_down.keep, sum_attention.going)
    grad_down, down_left_new, down_right_new, down_new = shampoo(
        shampoo_kernel, sum_down.keep, (w_down,), ((owned, ff),),
        (down_left, down_right, down_left_root, down_right_root),
    )
    sum_attention.received, received, *sooner = join(
        *after([sum_attention.received, received, *sum_up.keep[:-1]], down_new)
    )
    sum_up.keep = [*sooner, sum_up.keep[-1]]
    norm_sum = norm_sum + received
    sum_attention.first()
    received = exchanged(norm_sum, 4)
    (sum_up.keep[-1],) = after([sum_up.keep[-1]], sum_attention.going)
    sum_attention.received, sum_up.keep[-1], received = join(
        sum_attention.received, sum_up.keep[-1], received
    )
    norm_sum = norm_sum + received
    sum_attention.far()
    sum_up.keep = after(sum_up.keep, sum_attention.going)
    (
        grad_up, up_left_new, up_right_new, up_new, grad_out, out_left_new, out_right_new, out_new
    ) = shampoo(
        up_shampoo, sum_up.keep, (w_up, w_out), ((owned, ff), (owned, width_of(w_out))),
        (
            up_left, up_right, up_left_root, up_right_root,
            out_left, out_right, out_left_root, out_right_root,
        ),
    )
    (norm_sum,) = after([norm_sum], up_new)
    grad_norm = lax.dynamic_slice_in_dim(norm_sum, dp_index * owned, owned, 1).T
    norm_second_new = STAT_DECAY * norm_second + (1.0 - STAT_DECAY) * grad_norm * grad_norm
    own_params = lax.dynamic_slice_in_dim(norm_params, dp_index * owned, owned, 0)
    norm_new = own_params - NORM_RATE * grad_norm / (jnp.sqrt(norm_second_new) + 1e-08)
    *sum_attention.keep, grad_norm, norm_second_new, norm_new = join(
        *sum_attention.keep, grad_norm, norm_second_new, norm_new
    )
    qkv_turned = w_qkv.transpose(1, 0, 2)
    grad_qkv, qkv_left_new, qkv_right_new, qkv_new = shampoo(
        attention_shampoo, sum_attention.keep, (qkv_turned,), ((owned, 3 * w_qkv.shape[2]),),
        (qkv_left, qkv_right, qkv_left_root, qkv_right_root),
    )
    grad_qkv, qkv_new = grad_qkv.transpose(1, 0, 2), qkv_new.transpose(1, 0, 2)
    (
        qkv_left_new, qkv_right_new, out_left_new, out_right_new,
        up_left_new, up_right_new, down_left_new, down_right_new,
    ) = (
        stat[None, None]
        for stat in (
            qkv_left_new, qkv_right_new, out_left_new, out_right_new,
            up_left_new, up_right_new, down_left_new, down_right_new,
        )
    )
    return (
        block_out.reshape(block_in.shape),
        input_grad.reshape(block_in.shape),
        loss[:, 0].reshape(micros, seqs),
        grad_qkv, qkv_left_new, qkv_right_new, qkv_new,
        grad_out, out_left_new, out_right_new, out_new,
        grad_up, up_left_new, up_right_new, up_new,
        grad_down, down_left_new, down_right_new, down_new,
        grad_norm, norm_second_new, norm_new,
    )


def solution(mesh):
    sequence = P(None, AXES)
    stat = P("dp", "mp", None, None)
    weight = P("dp", "mp")
    qkv = P("dp", None, "mp")
    norm = P("dp", None)
    in_specs = (sequence, sequence, sequence, qkv, weight, weight, weight, P(), norm) + (stat,) * 16
    out_specs = (
        (sequence, sequence, sequence)
        + (qkv, stat, stat, qkv)
        + (weight, stat, stat, weight) * 3
        + (norm, norm, norm)
    )
    return jax.shard_map(
        per_device, mesh=mesh, in_specs=in_specs, out_specs=out_specs, check_vma=False
    )
```

```python
import functools
import math

import jax
import jax.numpy as jnp
import numpy as np
from jax import lax
from jax.experimental import pallas as pl
from jax.experimental.pallas import tpu as pltpu
from jax.sharding import PartitionSpec as P

AXES = ("dp", "mp")
HD = 64
LANES = 128
EPSILON = 1e-06
SOFTMAX_TEMP = 2.0
LOSS_SCALE = 32.0
STAT_DECAY = 0.5
SHAMPOO_RATE = 0.3
NORM_RATE = 0.5
TILE = 256
VMEM_BYTES = 53 * 1024 * 1024
SMALL_BYTES = 20 * 1024 * 1024
F32 = jnp.float32
BF16 = jnp.bfloat16


def far_digits(count):
    digits = []
    weight = 8
    while weight < count:
        size = min(4, count // weight)
        digits.append((weight, size))
        weight *= size
    return digits


def near_steps(count):
    return (
        [i ^ (4 if i % 2 == 0 else 2) for i in range(count)],
        [i ^ (2 if i % 2 == 0 else 4) for i in range(count)],
        [i ^ 1 for i in range(count)],
    )


def far_steps(count, weight, size):
    return [[i ^ (weight * m) for i in range(count)] for m in range(1, size)]


def source_table(count, near_first):
    first, second, third = near_steps(count)
    far = [far_steps(count, weight, size) for weight, size in far_digits(count)]
    rounds = [[first]] + far if near_first else far + [[first]]
    table = np.arange(count)[:, None]
    for steps in rounds + [[second], [third]]:
        table = np.concatenate([table] + [table[np.array(step)] for step in steps], axis=1)
    return table


def swap(values, step):
    return lax.ppermute(values, AXES, list(enumerate(step)))


class Gather:
    def __init__(self, block, count):
        self.count = count
        self.near = near_steps(count)
        self.held = block[None]
        self.received = []

    def keep(self, *earlier):
        if self.received:
            self.received = after(self.received, *earlier)
            self.held = jnp.concatenate([self.held] + self.received, axis=0)
            self.received = []

    def far(self, *earlier):
        (self.held,) = after([self.held], *earlier)
        for weight, size in far_digits(self.count):
            self.keep()
            steps = far_steps(self.count, weight, size)
            self.received = [swap(self.held, step) for step in steps]

    def first(self, *earlier):
        (self.held,) = after([self.held], *earlier)
        self.received = [swap(self.held, self.near[0])]

    def second(self, *earlier):
        (self.held,) = after([self.held], *earlier)
        self.across = swap(self.held, self.near[1])

    def third(self, *earlier):
        (self.held,) = after([self.held], *earlier)
        self.held_other = swap(self.held, self.near[2])

    def last(self, *earlier):
        (self.across,) = after([self.across], *earlier)
        self.across_other = swap(self.across, self.near[2])

    def quarters(self):
        return self.held, self.across, self.held_other, self.across_other


def join(*values):
    return lax.optimization_barrier(values)


def after(values, *earlier, keep=None):
    if not earlier:
        return list(values)
    return list(lax.optimization_barrier((*values, *earlier)))[: keep or len(values)]


def add_low(*terms):
    return sum(term.astype(F32) for term in terms).astype(BF16)


class Sum:
    def __init__(self, quarters, count):
        self.count = count
        self.near = near_steps(count)
        self.held, self.across, held_other, across_other = quarters
        self.from_across = swap(across_other, self.near[2])
        self.from_held = swap(held_other, self.near[2])

    def second(self, *earlier):
        (received,) = after([self.from_across], *earlier)
        self.going = add_low(self.across, received)
        self.received = swap(self.going, self.near[1])

    def first(self, *earlier):
        (received,) = after([self.received], *earlier)
        half = self.held.shape[0] // 2
        terms = self.held, self.from_held, received
        self.going = add_low(*(term[half:] for term in terms))
        self.keep = add_low(*(term[:half] for term in terms))
        self.received = swap(self.going, self.near[0])

    def far_half(self, *earlier):
        if far_digits(self.count) != [(8, 4)]:
            return self.far(*earlier)
        (received,) = after([self.received], *earlier)
        terms = self.keep, received
        going = add_low(*(term[2:] for term in terms))
        self.keep = add_low(*(term[:2] for term in terms))
        self.received = swap(going, far_steps(self.count, 8, 4)[1])
        self.going = going

    def far_rest(self, *earlier):
        if far_digits(self.count) != [(8, 4)]:
            return
        (received,) = after([self.received], *earlier)
        going = add_low(self.keep[1:], received[1:])
        self.keep = [self.keep, received, swap(going, far_steps(self.count, 8, 4)[0])]
        self.going = going

    def far(self, *earlier):
        (received,) = after([self.received], *earlier)
        keep = [self.keep, received]
        for weight, size in far_digits(self.count)[::-1]:
            step_size = keep[0].shape[0] // size
            parts = [
                add_low(*(term[m * step_size : (m + 1) * step_size] for term in keep))
                for m in range(1, size)
            ]
            keep = [term[:step_size] if step_size > 1 else term for term in keep] + [
                swap(part, step)
                for part, step in zip(parts, far_steps(self.count, weight, size))
            ]
        self.going = parts[-1]
        self.keep = keep


def dot(left, right, left_dim, right_dim):
    return lax.dot_general(
        left, right, (((left_dim,), (right_dim,)), ((), ())), preferred_element_type=F32
    )


def load_weights(places, parts, weights, sems, first=0):
    size, rows, _ = parts[0].shape
    groups, _, cols = weights.shape
    me = places[2 * size * len(parts)]

    def body(q, carry):
        for i, part in enumerate(parts):
            index = places[i * size + q] ^ me
            group = index % groups
            place = pl.multiple_of((index // groups) * rows, 16)
            pltpu.make_async_copy(
                part.at[q, :, pl.ds(first, cols)],
                weights.at[group, pl.ds(place, rows), :],
                sems.at[group],
            ).start()
        return carry

    lax.fori_loop(0, size, body, 0)


def store_blocks(places, source, group, groups, parts, sem):
    size, rows, _ = parts[0].shape
    count = size * len(parts)
    me = places[2 * count]

    def body(p, carry):
        position = places[count + ((p * groups + group) ^ me)]
        block = source.at[pl.ds(pl.multiple_of(p * rows, 16), rows), :]
        for i, part in enumerate(parts):

            @pl.when((position // size) % len(parts) == i)
            def _():
                pltpu.make_async_copy(block, part.at[position % size], sem).start()

        return carry

    lax.fori_loop(0, source.shape[0] // rows, body, 0)


def wait_weights(weights, sems, group):
    pltpu.make_async_copy(weights.at[group], weights.at[group], sems.at[group]).wait()


def normalize(values):
    center = values - jnp.mean(values, axis=-1, keepdims=True)
    spread = jnp.mean(center * center, axis=-1, keepdims=True)
    scale = lax.rsqrt(spread + EPSILON)
    return center * scale, scale


def low_lanes(dtype=BF16):
    lane = lax.broadcasted_iota(jnp.int32, (1, LANES), 1)
    return jnp.where(lane < HD, 1.0, 0.0).astype(dtype)


def pairs_of(blocks, low):
    first, second = blocks

    def join(left, right, high_half):
        if high_half:
            return jnp.where(low, turn(left), right)
        return jnp.where(low, left, turn(right))

    return (
        (first[0], first[1], first[2]),
        (second[0], second[1], second[2]),
        (
            join(first[3], second[3], False),
            join(first[4], second[4], False),
            join(first[3], second[3], True),
        ),
    )


def turn(values):
    return jnp.concatenate([values[:, HD:], values[:, :HD]], axis=1)


def both_heads(values, low_mask, high_mask):
    return jnp.concatenate([values * low_mask, values * high_mask], axis=0)


def diagonal(full, seq_len, own_cols):
    picked = full[:seq_len]
    for i, own in enumerate(own_cols):
        if i:
            picked = jnp.where(own, full[i * seq_len : (i + 1) * seq_len], picked)
    return picked


def undiagonal(compact, own_cols):
    return jnp.concatenate(
        [jnp.where(own, compact, jnp.zeros_like(compact)) for own in own_cols], axis=0
    )


def sequence_columns(seq_len):
    lane = lax.broadcasted_iota(jnp.int32, (seq_len, 2 * LANES), 1) % LANES
    return [lane // seq_len == i for i in range(LANES // seq_len)]


def stack_heads(values):
    return jnp.concatenate([values[:, :LANES], values[:, LANES:]], axis=0)


def spread(values, seq_len):
    seqs, width = values.shape
    return jnp.broadcast_to(values[:, None, :], (seqs, seq_len, width)).reshape(
        seqs * seq_len, width
    )


def live_column(counts, seq_len):
    wide = spread(counts, seq_len)
    slot = lax.broadcasted_iota(jnp.int32, wide.shape, 0) % seq_len
    return jnp.where(slot.astype(F32) < wide, 1.0, 0.0)[:, 0:1]


def first_norm(x_ref, norm_ref, h1_ref, turned_ref):
    n1, _ = normalize(x_ref[...].astype(F32))
    h1 = (n1 * norm_ref[0:1, :] + norm_ref[1:2, :]).astype(BF16)
    h1_ref[...] = h1
    turned_ref[...] = h1.T


def attention_forward(
    order, x_ref, h1_ref, live_ref, norm_ref, w0, w1, w2, w3,
    proj_ref, heads_ref, lse_ref, mid_ref, h2_ref,
    weights, sems, *, seq_len,
):
    groups = weights.shape[0]
    first = pl.program_id(0) == 0

    @pl.when(first)
    def _():
        load_weights(order, (w0, w1, w2, w3), weights, sems)
        for group in range(weights.shape[0]):
            wait_weights(weights, sems, group)

    x = x_ref[...].astype(F32)
    rows = x.shape[0]
    h1 = h1_ref[...]
    low_mask = low_lanes()
    high_mask = 1 - low_mask
    low = lax.broadcasted_iota(jnp.int32, (1, LANES), 1) < HD
    own_cols = sequence_columns(seq_len)
    count = rows // LANES
    duos = groups // 2
    projected = [
        dot(h1, weights[group, :, : 5 * LANES], 1, 0).astype(BF16) for group in range(groups)
    ]
    chains = []
    for duo in range(duos):
        for t in range(count):
            span = slice(t * LANES, (t + 1) * LANES)
            blocks = [
                [proj[span, i * LANES : (i + 1) * LANES] for i in range(5)]
                for proj in projected[2 * duo : 2 * duo + 2]
            ]
            for i, (q, k, v) in enumerate(pairs_of(blocks, low)):
                for which, part in enumerate((q, k, v)):
                    at = ((duo * 3 + i) * 3 + which) * LANES
                    proj_ref[span, at : at + LANES] = part
                chains.append((t, duo * 3 + i, q, k, v))
    scores = [dot(k, both_heads(q, low_mask, high_mask), 1, 1) for t, i, q, k, v in chains]
    probs = []
    for (t, i, *_), full in zip(chains, scores):
        compact = diagonal(full, seq_len, own_cols) * (HD**-0.5)
        compact = jnp.where(live_ref[t] > 0.0, compact, -1e30)
        top = jnp.max(compact, axis=0, keepdims=True)
        powers = jnp.exp(compact - top)
        power = jnp.sum(powers, axis=0, keepdims=True)
        lse_ref[t, i : i + 1, :] = top + jnp.log(power)
        probs.append(undiagonal((powers * (1.0 / power)).astype(BF16), own_cols))
    outs = [
        dot(stack_heads(part), both_heads(v, low_mask, high_mask), 0, 0)
        for part, (t, i, q, k, v) in zip(probs, chains)
    ]
    total = x
    for duo in range(duos):
        heads = [[], []]
        for t in range(count):
            at = 3 * (duo * count + t)
            one, two, third = outs[at : at + 3]
            heads[0].append(
                jnp.concatenate([jnp.where(low, 0.0, turn(third)), one], axis=1).astype(BF16)
            )
            heads[1].append(
                jnp.concatenate([jnp.where(low, 0.0, third), two], axis=1).astype(BF16)
            )
        for side, group in enumerate((2 * duo, 2 * duo + 1)):
            joined = jnp.concatenate(heads[side], axis=0)
            heads_ref[:, group * 2 * LANES : (group + 1) * 2 * LANES] = joined
            total = total + dot(joined, weights[group, :, 4 * LANES :], 1, 1)
    mid_ref[...] = total
    n2, _ = normalize(total)
    h2_ref[...] = (n2 * norm_ref[2:3, :] + norm_ref[3:4, :]).astype(BF16)


def up_forward(
    places, h2_ref, count_ref, w0, w1, w2, w3,
    hid_ref, slope_ref, pooled_ref,
    weights, sems, *, seq_len,
):
    groups, _, wide = weights.shape

    @pl.when(pl.program_id(0) == 0)
    def _():
        load_weights(places, (w0, w1, w2, w3), weights, sems)
        for group in range(groups):
            wait_weights(weights, sems, group)

    h2 = h2_ref[...]
    rows = h2.shape[0]
    counts = count_ref[...]
    live = live_column(counts, seq_len)
    seqs = rows // seq_len
    slot = lax.broadcasted_iota(jnp.int32, (seqs, rows), 1)
    member = slot // seq_len == lax.broadcasted_iota(jnp.int32, (seqs, rows), 0)
    within = (slot % seq_len).astype(F32) < counts[:, 0:1]
    pool = jnp.where(jnp.logical_and(member, within), 1.0, 0.0).astype(BF16)
    for group in range(groups):
        cols = slice(group * wide, (group + 1) * wide)
        up = dot(h2, weights[group], 1, 0)
        gate = 0.5 + 0.5 * lax.erf(up * (0.5**0.5))
        hid = (up * gate).astype(BF16)
        hid_ref[:, cols] = hid
        bell = jnp.exp(up * up * -0.5) * (1.0 / math.sqrt(2.0 * math.pi))
        slope_ref[:, cols] = ((gate + up * bell) * live).astype(BF16)
        pooled_ref[:, cols] = dot(pool, hid, 1, 0).astype(BF16)


def down_forward(
    order, hid_ref, mid_ref, count_ref, w0, w1, w2, w3,
    out_ref, pooled_ref, weights, sems, *, seq_len,
):
    groups, _, width = weights.shape
    first = pl.program_id(0) == 0

    @pl.when(first)
    def _():
        load_weights(order, (w0, w1, w2, w3), weights, sems)
        for group in range(weights.shape[0]):
            wait_weights(weights, sems, group)

    total = mid_ref[...]
    for group in range(groups):


        total = total + dot(
            hid_ref[:, group * width : (group + 1) * width], weights[group], 1, 1
        )
    out_ref[...] = total.astype(BF16)
    rows, features = total.shape
    counts = count_ref[...]
    live = live_column(counts, seq_len)
    seqs = rows // seq_len
    sums = jnp.sum((total * live).reshape(seqs, seq_len, features), axis=1)
    pooled_ref[...] = sums / counts[:, 0:1]


def loss_backward(
    places, pooled_ref, count_ref, m0, m1, m2, m3, hid_ref,
    loss_ref, grad_ref, low_ref, g0, g1, g2, g3,
    slots, slot_sems, *, micros, groups,
):
    ff = slots.shape[2]
    pooled = pooled_ref[...]
    seqs, width = pooled.shape
    each = seqs // micros
    scale_text = SOFTMAX_TEMP / math.sqrt(width)
    r = lax.rsqrt(jnp.mean(pooled * pooled, axis=-1, keepdims=True) + EPSILON)
    text = (pooled * r).astype(BF16)
    row_micro = lax.broadcasted_iota(jnp.int32, (seqs, 1), 0) // each
    step = min(m0.shape[0], 1024)
    pieces = [
        ref[i : i + step, :]
        for ref in (m0, m1, m2, m3)
        for i in range(0, ref.shape[0], step)
    ]
    col = lax.broadcasted_iota(jnp.int32, (1, step), 1)
    same = (col // each) % micros == row_micro
    logits = [jnp.where(same, dot(text, piece, 1, 1) * scale_text, -1e30) for piece in pieces]
    top = functools.reduce(
        jnp.maximum, [jnp.max(part, axis=1, keepdims=True) for part in logits]
    )
    powers = [jnp.exp(part - top) for part in logits]
    total = functools.reduce(jnp.add, [jnp.sum(part, axis=1, keepdims=True) for part in powers])
    log_total = top + jnp.log(total)
    positive = lax.broadcasted_iota(jnp.int32, (seqs, 1), 0) == col
    loss = log_total - jnp.sum(jnp.where(positive, logits[0], 0.0), axis=1, keepdims=True)
    loss_ref[...] = jnp.broadcast_to(loss, loss_ref.shape)
    inverse = LOSS_SCALE / total
    grad_text = jnp.zeros((seqs, width), F32)
    for i, (part, piece) in enumerate(zip(powers, pieces)):
        grad_part = part * inverse
        if i == 0:
            grad_part = grad_part - jnp.where(positive, LOSS_SCALE, 0.0)
        grad_text = grad_text + dot(grad_part.astype(BF16), piece, 1, 0)
    grad_text = grad_text * scale_text
    along = jnp.mean(grad_text * pooled, axis=-1, keepdims=True)
    grad = (r * grad_text - (r * r * r) * pooled * along) / count_ref[:, 0:1]
    grad_ref[...] = grad
    low = grad.astype(BF16)
    low_ref[...] = low
    turned = low.T
    for group in range(groups):
        cols = slice(group * ff, (group + 1) * ff)
        if group >= 2:
            drain(slots, slot_sems, group % 2)
        slots[group % 2] = dot(turned, hid_ref[:, cols], 1, 0).astype(BF16)
        store_blocks(
            places, slots.at[group % 2], group, groups, (g0, g1, g2, g3),
            slot_sems.at[group % 2],
        )
    for which in range(min(groups, 2)):
        drain(slots, slot_sems, which)


def drain(slots, sems, which):
    pltpu.make_async_copy(slots.at[which], slots.at[which], sems.at[which]).wait()


def finish_blocks(slots, sems, group, groups, slot):
    @pl.when(group == groups - 1)
    def _():
        drain(slots, sems, slot)

        @pl.when(groups >= 2)
        def _():
            drain(slots, sems, 1 - slot)


def weight_gradient(places, *refs):
    pairs = (len(refs) - 6) // 3
    lefts, rights = refs[: 2 * pairs : 2], refs[1 : 2 * pairs : 2]
    parts, turned = refs[2 * pairs : 2 * pairs + 4], refs[2 * pairs + 4 : -2]
    slots, sems = refs[-2:]
    group = pl.program_id(0)
    groups = pl.num_programs(0)
    slot = group % 2

    @pl.when(group == 0)
    def _():
        for left, across in zip(lefts, turned):
            across[...] = left[...].T

    @pl.when(group >= 2)
    def _():
        drain(slots, sems, slot)

    first = 0
    for across, right in zip(turned, rights):
        last = first + right.shape[1]
        slots[slot, :, first:last] = dot(across[...], right[...], 1, 0).astype(BF16)
        first = last
    store_blocks(places, slots.at[slot], group, groups, parts, sems.at[slot])
    finish_blocks(slots, sems, group, groups, slot)


def turned_gradient(places, left_ref, right_ref, g0, g1, g2, g3, slots, sems):
    group = pl.program_id(0)
    groups = pl.num_programs(0)
    slot = group % 2

    @pl.when(group >= 2)
    def _():
        drain(slots, sems, slot)

    slots[slot] = dot(left_ref[...], right_ref[...], 1, 0).astype(BF16)
    store_blocks(places, slots.at[slot], group, groups, (g0, g1, g2, g3), sems.at[slot])
    finish_blocks(slots, sems, group, groups, slot)


def norm_back(grad, gain, values):
    n, scale = normalize(values)
    scaled = grad * gain
    moved = scale * (
        scaled
        - jnp.mean(scaled, axis=-1, keepdims=True)
        - n * jnp.mean(scaled * n, axis=-1, keepdims=True)
    )
    gain_grad = jnp.sum(grad * n, axis=0, keepdims=True)
    shift_grad = jnp.sum(grad, axis=0, keepdims=True)
    return moved, gain_grad, shift_grad


def down_backward(order, low_ref, w0, w1, w2, w3, by_seq_ref, weights, sems):
    groups, _, width = weights.shape
    load_weights(order, (w0, w1, w2, w3), weights, sems)
    for group in range(groups):
        wait_weights(weights, sems, group)
        by_seq_ref[:, group * width : (group + 1) * width] = dot(
            low_ref[...], weights[group], 1, 0
        )


def mlp_backward(
    order, grad_ref, by_seq_ref, slope_ref, count_ref, mid_ref, norm_ref,
    w0, w1, w2, w3,
    dup_ref, dmid_ref, dmid_low_ref, sums_ref,
    weights, sems, *, seq_len,
):
    groups, _, width = weights.shape

    @pl.when(pl.program_id(0) == 0)
    def _():
        load_weights(order, (w0, w1, w2, w3), weights, sems)
        sums_ref[...] = jnp.zeros_like(sums_ref)
        for group in range(groups):
            wait_weights(weights, sems, group)

    grad = grad_ref[...]
    mid = mid_ref[...]
    rows, features = mid.shape

    total = jnp.zeros((rows, features), F32)
    for group in range(groups):


        cols = slice(group * width, (group + 1) * width)
        dup = (slope_ref[:, cols].astype(F32) * spread(by_seq_ref[:, cols], seq_len)).astype(BF16)
        dup_ref[:, cols] = dup
        total = total + dot(dup, weights[group], 1, 1)
    moved, gain_grad, shift_grad = norm_back(total, norm_ref[2:3, :], mid)
    live = live_column(count_ref[...], seq_len)
    dmid = spread(grad, seq_len) * live + moved
    dmid_ref[...] = dmid
    dmid_low_ref[...] = dmid.astype(BF16)
    sums_ref[0:1, :] += gain_grad
    sums_ref[1:2, :] += shift_grad


def attention_backward(
    places, x_ref, live_ref, norm_ref, proj_ref, lse_ref, dmid_ref, dmid_low_ref,
    w0, w1, w2, w3, dproj_ref, dx_ref, sums_ref, weights, sems, *, seq_len,
):
    groups = weights.shape[0]

    @pl.when(pl.program_id(0) == 0)
    def _():
        load_weights(places, (w0, w1, w2, w3), weights, sems)
        for group in range(groups):
            wait_weights(weights, sems, group)
        sums_ref[...] = jnp.zeros_like(sums_ref)

    x = x_ref[...].astype(F32)
    rows = x.shape[0]
    dmid_low = dmid_low_ref[...]
    low_mask = low_lanes()
    high_mask = 1 - low_mask
    low = lax.broadcasted_iota(jnp.int32, (1, LANES), 1) < HD
    own_cols = sequence_columns(seq_len)
    score_scale = HD**-0.5
    count = rows // LANES
    duos = groups // 2
    dheads = [
        dot(dmid_low, weights[group, :, 4 * LANES :], 1, 0).astype(BF16)
        for group in range(groups)
    ]
    chains = []
    for duo in range(duos):
        first_d, second_d = dheads[2 * duo : 2 * duo + 2]
        for t in range(count):
            span = slice(t * LANES, (t + 1) * LANES)
            for i, d in enumerate(
                (
                    first_d[span, LANES:],
                    second_d[span, LANES:],
                    jnp.where(low, turn(first_d[span, :LANES]), second_d[span, :LANES]),
                )
            ):
                at = (duo * 3 + i) * 3 * LANES
                q, k, v = (
                    proj_ref[span, at + j * LANES : at + (j + 1) * LANES] for j in range(3)
                )
                qq, kk, dd = (both_heads(part, low_mask, high_mask) for part in (q, k, d))
                chains.append((t, duo * 3 + i, k, v, qq, kk, dd))
    scores = [dot(k, qq, 1, 1) for t, i, k, v, qq, kk, dd in chains]
    powers = [dot(v, dd, 1, 1) for t, i, k, v, qq, kk, dd in chains]
    wide = []
    for (t, i, *_), full, power in zip(chains, scores, powers):
        live = live_ref[t] > 0.0
        compact = diagonal(full, seq_len, own_cols) * score_scale
        lse = lse_ref[t, i : i + 1, :]
        probs = jnp.where(live, jnp.exp(jnp.where(live, compact - lse, 0.0)), 0.0)
        dprobs = diagonal(power, seq_len, own_cols)
        inner = jnp.sum(probs * dprobs, axis=0, keepdims=True)
        dscores = probs * (dprobs - inner) * score_scale
        wide.append(
            (
                undiagonal(dscores.astype(BF16), own_cols),
                undiagonal(probs.astype(BF16), own_cols),
            )
        )
    outs = [
        (dot(stack_heads(ds), kk, 0, 0), dot(ds, qq, 1, 0), dot(p, dd, 1, 0))
        for (ds, p), (t, i, k, v, qq, kk, dd) in zip(wide, chains)
    ]
    total = jnp.zeros(x.shape, F32)
    for duo in range(duos):
        grads = [[], []]
        for t in range(count):
            at = 3 * (duo * count + t)
            one, two, third = outs[at : at + 3]
            grads[0].append(
                jnp.concatenate(
                    one
                    + (jnp.where(low, third[0], turn(third[2])), jnp.where(low, third[1], 0.0)),
                    axis=1,
                ).astype(BF16)
            )
            grads[1].append(
                jnp.concatenate(
                    two
                    + (jnp.where(low, turn(third[0]), third[2]), jnp.where(low, turn(third[1]), 0.0)),
                    axis=1,
                ).astype(BF16)
            )
        for side, group in enumerate((2 * duo, 2 * duo + 1)):
            dproj = jnp.concatenate(grads[side], axis=0)
            dproj_ref[:, group * 5 * LANES : (group + 1) * 5 * LANES] = dproj
            total = total + dot(dproj, weights[group, :, : 5 * LANES], 1, 1)
    moved, gain_grad, shift_grad = norm_back(total, norm_ref[0:1, :], x)
    dx_ref[...] = dmid_ref[...] + moved
    sums_ref[0:1, :] += gain_grad
    sums_ref[1:2, :] += shift_grad


def renew(grad, left, right, left_root, right_root):
    low = grad.astype(BF16)
    keep = 1.0 - STAT_DECAY
    half = dot(left_root.astype(BF16), low, 1, 0).astype(BF16)
    return (
        STAT_DECAY * left + keep * dot(low, low, 1, 1),
        STAT_DECAY * right + keep * dot(low, low, 0, 0),
        SHAMPOO_RATE * dot(half, right_root.astype(BF16), 1, 0),
    )


def shampoo_kernel(*refs):
    terms = refs[:-9]
    master_ref, *stats = refs[-9:-4]
    grad_ref, left_new_ref, right_new_ref, new_ref = refs[-4:]
    grad = sum(term[0].astype(F32) for term in terms)
    grad_ref[...] = grad
    left_new_ref[...], right_new_ref[...], step = renew(grad, *(ref[...] for ref in stats))
    new_ref[...] = master_ref[...] - step


def up_shampoo(*refs):
    terms = refs[:-18]
    up_ref, out_ref, *stats = refs[-18:-8]
    up_grad, up_left, up_right, up_new, out_grad, out_left, out_right, out_new = refs[-8:]
    packed = sum(term[0].astype(F32) for term in terms)
    wide = up_ref.shape[1]
    up, out = packed[:, :wide], unpack_out(packed[:, wide:])
    up_grad[...] = up
    up_left[...], up_right[...], step = renew(up, *(ref[...] for ref in stats[:4]))
    up_new[...] = up_ref[...] - step
    out_grad[...] = out
    out_left[...], out_right[...], step = renew(out, *(ref[...] for ref in stats[4:]))
    out_new[...] = out_ref[...] - step


def attention_shampoo(*refs):
    terms = refs[:-9]
    qkv_ref, *stats = refs[-9:-4]
    qkv_grad, qkv_left, qkv_right, qkv_new = refs[-4:]
    qkv = unpack_qkv(sum(term[0].astype(F32) for term in terms))
    qkv_left[...], qkv_right[...], step = renew(qkv, *(ref[...] for ref in stats))
    width = qkv_ref.shape[2]
    for i in range(3):
        cols = slice(i * width, (i + 1) * width)
        qkv_grad[i] = qkv[:, cols]
        qkv_new[i] = qkv_ref[i] - step[:, cols]


ANY = pl.BlockSpec(memory_space=pl.ANY)
SMEM = pl.BlockSpec(memory_space=pltpu.SMEM)
WHOLE = pl.BlockSpec(memory_space=pltpu.VMEM)


def rows_of(width, height=TILE, start=0):
    return pl.BlockSpec((height, width), lambda i: (i + start, 0))


def fixed(shape):
    return pl.BlockSpec(shape, lambda i: (0,) * len(shape))


def params(limit=VMEM_BYTES):
    return pltpu.CompilerParams(vmem_limit_bytes=limit)


def cost(flops, bytes_accessed):
    return pl.CostEstimate(flops=4 * int(flops), bytes_accessed=int(bytes_accessed), transcendentals=0)


def shape_of(*dims, dtype=BF16):
    return jax.ShapeDtypeStruct(dims, dtype)


def stat_shapes(rows, cols):
    return shape_of(rows, rows, dtype=F32), shape_of(cols, cols, dtype=F32)


def shampoo(kernel, terms, masters, shapes, stats, limit=VMEM_BYTES):
    rows, cols = terms[0].shape[1:]
    out_shape = []
    for master, (left, right) in zip(masters, shapes):
        value = shape_of(*master.shape, dtype=F32)
        out_shape += [value, *stat_shapes(left, right), value]
    return pl.pallas_call(
        kernel,
        grid=(1,),
        out_shape=tuple(out_shape),
        in_specs=[pl.BlockSpec((1, rows, cols), lambda i: (0, 0, 0))] * len(terms)
        + [WHOLE] * (len(masters) + len(stats)),
        out_specs=(WHOLE,) * len(out_shape),
        compiler_params=params(limit),
        cost_estimate=cost(4 * rows * cols * cols, 12 * cols * cols),
        name=kernel.__name__,
    )(*terms, *masters, *(stat[0, 0] for stat in stats))


def pack_qkv(qkv):
    q, k, v = (qkv[:, i] for i in range(3))
    a, b = 2 * HD, 3 * HD
    third = [q[:, a:b], v[:, a:b], k[:, a:b], jnp.zeros_like(k[:, a:b])]
    return jnp.concatenate([q[:, :a], k[:, :a], v[:, :a]] + third, axis=1)


def pack_attention(qkv, out):
    packed = pack_qkv(qkv)
    return jnp.concatenate([packed[:, : 9 * HD], out[:, 2 * HD :], out[:, : 2 * HD]], axis=1)


def unpack_qkv(packed):
    c = [packed[:, i * HD : (i + 1) * HD] for i in range(10)]
    return jnp.concatenate([c[0], c[1], c[6], c[2], c[3], c[8], c[4], c[5], c[7]], axis=1)


def unpack_out(packed):
    return jnp.concatenate([packed[:, 2 * HD :], packed[:, HD : 2 * HD]], axis=1)


def per_device(
    block_in, seq_lengths, image_embed, w_qkv, w_out, w_up, w_down, norm_params, norm_second,
    qkv_left, qkv_right, qkv_left_root, qkv_right_root,
    out_left, out_right, out_left_root, out_right_root,
    up_left, up_right, up_left_root, up_right_root,
    down_left, down_right, down_left_root, down_right_root,
):
    micros, seqs, seq_len, width = block_in.shape
    dp_count, groups = lax.axis_size("dp"), lax.axis_size("mp")
    count = dp_count * groups
    dp_index = lax.axis_index("dp")
    me = dp_index * groups + lax.axis_index("mp")
    owned = w_up.shape[0]
    ff = w_up.shape[1]
    all_seqs = micros * seqs
    rows = all_seqs * seq_len
    tiles = rows // TILE
    seq_tile = TILE // seq_len
    direct = owned % 16 == 0

    def places(near_first):
        masks = source_table(count, near_first)[:2] ^ np.arange(2)[:, None]
        masks = np.concatenate([masks, np.argsort(masks, axis=1)], axis=1)
        odd = me % 2 == 1
        mine = jnp.where(odd, jnp.asarray(masks[1], jnp.int32), jnp.asarray(masks[0], jnp.int32))
        return jnp.concatenate([mine, me.astype(jnp.int32)[None]])

    far_places, near_places = places(False), places(True)

    def order_of(places):
        return places[:count] ^ me

    def inverse_of(places):
        return places[count : 2 * count][jnp.arange(count) ^ me]

    def weights_of(gather, places):
        quarters = gather.quarters()
        if direct:
            return quarters
        whole = jnp.concatenate(quarters, axis=0)[inverse_of(places)]
        whole = whole.reshape(dp_count, groups, owned, whole.shape[-1])
        whole = whole.transpose(1, 0, 2, 3).reshape(groups, width, whole.shape[-1])
        return tuple(jnp.split(whole, 4, axis=0))

    plain = jnp.arange(groups, dtype=jnp.int32)
    if direct:
        kernel_far, kernel_near = far_places, near_places
    else:
        kernel_far = kernel_near = jnp.concatenate([plain, plain, jnp.zeros(1, jnp.int32)])
    block_rows = owned if direct else width
    quarter = (count if direct else groups) // 4

    def sum_of(quarters):
        if not direct:
            whole = jnp.concatenate(quarters, axis=0)
            whole = whole.reshape(groups, dp_count, owned, whole.shape[2])
            whole = whole.transpose(1, 0, 2, 3).reshape(count, owned, whole.shape[3])[order_of(far_places)]
            quarters = jnp.split(whole, 4, axis=0)
        return Sum(quarters, count)

    def width_of(array):
        return array.shape[1]

    own_attention = pack_attention(w_qkv.astype(BF16), w_out.astype(BF16))
    own_up, own_down = w_up.astype(BF16), w_down.astype(BF16)
    own_images = image_embed.reshape(all_seqs, width)
    gather_attention, gather_up, gather_down, gather_images = (
        Gather(block, count) for block in (own_attention, own_up, own_down, own_images)
    )
    gather_attention.far()
    later = gather_down, gather_images
    for gather in later:
        gather.first()
        gather.keep()
    gather_attention.keep(*(gather.held for gather in later))
    gather_attention.first()
    gather_up.far(gather_attention.held)

    x = block_in.reshape(rows, width)
    norms = norm_params.T
    lengths = seq_lengths.reshape(all_seqs)
    live = (jnp.arange(seq_len)[None, :] < lengths[:, None]).astype(F32)
    tile_seqs = LANES // seq_len
    live_keys = live.reshape(rows // LANES, tile_seqs, 1, seq_len)
    live_keys = jnp.broadcast_to(
        live_keys, (rows // LANES, tile_seqs, seq_len, seq_len)
    ).transpose(0, 3, 1, 2).reshape(rows // LANES, seq_len, LANES)
    live_keys = jnp.concatenate([live_keys, live_keys], axis=2)
    counts = jnp.broadcast_to(lengths.astype(F32)[:, None], (all_seqs, LANES))

    count_spec = rows_of(LANES, seq_tile)
    keys_spec = pl.BlockSpec((TILE // LANES, seq_len, 2 * LANES), lambda i: (i, 0, 0))
    lse_spec = pl.BlockSpec((TILE // LANES, 8, 2 * LANES), lambda i: (i, 0, 0))
    norm_spec = fixed((4, width))
    all_ff, all_heads = groups * ff, groups * 2 * LANES
    packed = width_of(own_attention)

    def weight_scratch(cols):
        return [pltpu.VMEM((groups, width, cols), BF16), pltpu.SemaphoreType.DMA((groups,))]

    x_ready, live_keys, counts, kernel_far, kernel_near = after(
        [x, live_keys, counts, kernel_far, kernel_near], gather_attention.held
    )
    h1, h1_turned = pl.pallas_call(
        first_norm,
        grid=(tiles,),
        in_specs=[rows_of(width), norm_spec],
        out_specs=(rows_of(width), pl.BlockSpec((width, TILE), lambda i: (0, i))),
        out_shape=(shape_of(rows, width), shape_of(width, rows)),
        compiler_params=params(),
        cost_estimate=cost(1, 100e6),
        name="first_norm",
    )(x_ready, norms)
    h1, live_keys, counts, kernel_far, kernel_near = join(
        h1, live_keys, counts, kernel_far, kernel_near
    )
    gather_attention.keep(h1)
    gather_attention.second()
    gather_attention.third()
    gather_up.keep(gather_attention.held)
    gather_attention.last(gather_up.held)
    gather_up.first(gather_attention.across)
    gather_down.far(gather_up.held)
    gather_up.keep(gather_attention.across)
    gather_up.second()
    gather_up.third()
    attention_w = weights_of(gather_attention, far_places)

    (h1_ready,) = after([h1], gather_up.held)
    proj, heads, lse, mid, h2 = pl.pallas_call(
        functools.partial(attention_forward, seq_len=seq_len),
        grid=(tiles,),
        in_specs=[SMEM, rows_of(width), rows_of(width), keys_spec, norm_spec, ANY, ANY, ANY, ANY],
        out_specs=(
            rows_of(3 * width), rows_of(all_heads), lse_spec, rows_of(width),
            rows_of(width),
        ),
        out_shape=(
            shape_of(rows, 3 * width), shape_of(rows, all_heads),
            shape_of(rows // LANES, 8, 2 * LANES, dtype=F32),
            shape_of(rows, width, dtype=F32), shape_of(rows, width),
        ),
        scratch_shapes=weight_scratch(packed),
        compiler_params=params(),
        cost_estimate=cost(2 * rows * width * groups * 900, 12e6),
        name="attention_forward",
    )(kernel_far, x, h1_ready, live_keys, norms, *attention_w)

    gather_down.keep(h2)
    gather_up.last(gather_down.held)
    gather_down.second()
    gather_down.third()
    gather_images.far(gather_down.held)
    up_w = weights_of(gather_up, far_places)
    (h2_ready,) = after([h2], gather_down.held)

    hid, slope, pooled_hid = pl.pallas_call(
        functools.partial(up_forward, seq_len=seq_len),
        grid=(tiles,),
        in_specs=[SMEM, rows_of(width), count_spec, ANY, ANY, ANY, ANY],
        out_specs=(rows_of(groups * ff), rows_of(groups * ff), rows_of(groups * ff, seq_tile)),
        out_shape=(
            shape_of(rows, groups * ff), shape_of(rows, groups * ff), shape_of(all_seqs, groups * ff),
        ),
        scratch_shapes=weight_scratch(ff),
        compiler_params=params(),
        cost_estimate=cost(2 * rows * width * groups * ff, 20e6),
        name="up_forward",
    )(kernel_far, h2_ready, counts, *up_w)

    gather_images.keep(hid)
    gather_down.last(hid, gather_images.held)
    gather_images.second(gather_down.across)
    gather_images.third()
    down_w = weights_of(gather_down, near_places)
    (hid_ready,) = after([hid], gather_images.held)

    block_out, pooled = pl.pallas_call(
        functools.partial(down_forward, seq_len=seq_len),
        grid=(tiles,),
        in_specs=[SMEM, rows_of(all_ff), rows_of(width), count_spec, ANY, ANY, ANY, ANY],
        out_specs=(rows_of(width), rows_of(width, seq_tile)),
        out_shape=(shape_of(rows, width), shape_of(all_seqs, width, dtype=F32)),
        scratch_shapes=weight_scratch(ff),
        compiler_params=params(),
        cost_estimate=cost(2 * rows * width * groups * ff, 20e6),
        name="down_forward",
    )(kernel_near, hid_ready, mid, counts, *down_w)

    gather_images.last(pooled)
    images = [part.reshape(-1, width) for part in gather_images.quarters()]

    def quarters_of(cols):
        return (shape_of(quarter, block_rows, cols),) * 4

    loss, grad_seq, grad_low, *down_parts = pl.pallas_call(
        functools.partial(loss_backward, micros=micros, groups=groups),
        in_specs=[SMEM] + [WHOLE] * 7,
        out_specs=(WHOLE,) * 3 + (ANY,) * 4,
        out_shape=(
            shape_of(all_seqs, LANES, dtype=F32), shape_of(all_seqs, width, dtype=F32),
            shape_of(all_seqs, width),
        ) + quarters_of(ff),
        scratch_shapes=[pltpu.VMEM((2, width, ff), BF16), pltpu.SemaphoreType.DMA((2,))],
        compiler_params=params(),
        cost_estimate=cost(8 * all_seqs * width * groups * ff, 20e6),
        name="loss_backward",
    )(kernel_far, pooled, counts, *images, pooled_hid)
    sum_down = sum_of(down_parts)

    by_seq = pl.pallas_call(
        down_backward,
        in_specs=[SMEM, WHOLE, ANY, ANY, ANY, ANY],
        out_specs=WHOLE,
        out_shape=shape_of(all_seqs, all_ff, dtype=F32),
        scratch_shapes=weight_scratch(ff),
        compiler_params=params(),
        cost_estimate=cost(8 * all_seqs * width * groups * ff, 6e6),
        name="down_backward",
    )(kernel_near, grad_low, *down_w)
    by_seq, sum_down.from_across = join(by_seq, sum_down.from_across)
    sum_down.second()
    (grad_seq,) = after([grad_seq], sum_down.going)

    dup, dmid, dmid_low, sums_two = pl.pallas_call(
        functools.partial(mlp_backward, seq_len=seq_len),
        grid=(tiles,),
        in_specs=[
            SMEM, rows_of(width, seq_tile), rows_of(groups * ff, seq_tile), rows_of(groups * ff),
            count_spec, rows_of(width), norm_spec, ANY, ANY, ANY, ANY,
        ],
        out_specs=(rows_of(groups * ff), rows_of(width), rows_of(width), fixed((2, width))),
        out_shape=(
            shape_of(rows, groups * ff), shape_of(rows, width, dtype=F32), shape_of(rows, width),
            shape_of(2, width, dtype=F32),
        ),
        scratch_shapes=weight_scratch(ff),
        compiler_params=params(),
        cost_estimate=cost(2 * rows * width * groups * ff, 25e6),
        name="mlp_backward",
    )(kernel_far, grad_seq, by_seq, slope, counts, mid, norms, *up_w)

    def gradient(name, *pairs):
        cols = [right.shape[1] // groups for _, right in pairs]
        return pl.pallas_call(
            weight_gradient,
            grid=(groups,),
            in_specs=[SMEM] + [
                spec
                for wide in cols
                for spec in (
                    fixed((rows, width)), pl.BlockSpec((rows, wide), lambda i: (0, i))
                )
            ],
            out_specs=(ANY,) * 4,
            out_shape=quarters_of(sum(cols)),
            scratch_shapes=[pltpu.VMEM((width, rows), BF16) for _ in pairs]
            + [pltpu.VMEM((2, width, sum(cols)), BF16), pltpu.SemaphoreType.DMA((2,))],
            compiler_params=params(),
            cost_estimate=cost(2 * rows * width * groups * 900, 10e6),
            name=name,
        )(kernel_far, *(part for pair in pairs for part in pair))

    dmid, sum_down.received = join(dmid, sum_down.received)
    sum_down.first()
    (h2_ready,) = after([h2], sum_down.going)
    up_parts = gradient("up_gradient", (h2_ready, dup), (dmid_low, heads))
    *up_parts, sum_down.received = join(*up_parts, sum_down.received)
    sum_up = sum_of(up_parts)
    sum_down.far_half()
    (sum_up.from_across,) = after([sum_up.from_across], sum_down.going)
    sum_up.second()

    (x_ready,) = after([x], sum_up.going)
    dproj, input_grad, sums_one = pl.pallas_call(
        functools.partial(attention_backward, seq_len=seq_len),
        grid=(tiles,),
        in_specs=[
            SMEM, rows_of(width), keys_spec, norm_spec, rows_of(3 * width), lse_spec,
            rows_of(width), rows_of(width), ANY, ANY, ANY, ANY,
        ],
        out_specs=(rows_of(groups * 5 * LANES), rows_of(width), fixed((2, width))),
        out_shape=(
            shape_of(rows, groups * 5 * LANES), shape_of(rows, width, dtype=F32),
            shape_of(2, width, dtype=F32),
        ),
        scratch_shapes=weight_scratch(packed),
        compiler_params=params(),
        cost_estimate=cost(2 * rows * width * groups * 1300, 20e6),
        name="attention_backward",
    )(kernel_far, x_ready, live_keys, norms, proj, lse, dmid, dmid_low, *attention_w)

    def exchanged(values, bit):
        return swap(values, [i ^ bit for i in range(count)])

    if far_digits(count) == [(8, 4)]:
        sums_one, sum_up.received, sum_down.received = join(
            sums_one, sum_up.received, sum_down.received
        )
    sum_down.far_rest()
    norm_sum = jnp.concatenate([sums_one, sums_two], axis=0)
    received = exchanged(norm_sum, 1)
    sum_up.first()
    (received,) = after([received], sum_up.going)
    norm_sum = norm_sum + received
    received = exchanged(norm_sum, 8)
    (h1_ready,) = after([h1_turned], sum_up.going, sum_down.going, norm_sum)
    attention_parts = pl.pallas_call(
        turned_gradient,
        grid=(groups,),
        in_specs=[
            SMEM, fixed((width, rows)), pl.BlockSpec((rows, 5 * LANES), lambda i: (0, i))
        ],
        out_specs=(ANY,) * 4,
        out_shape=quarters_of(5 * LANES),
        scratch_shapes=[pltpu.VMEM((2, width, 5 * LANES), BF16), pltpu.SemaphoreType.DMA((2,))],
        compiler_params=params(),
        cost_estimate=cost(2 * rows * width * groups * 900, 10e6),
        name="attention_gradient",
    )(kernel_far, h1_ready, dproj)
    *attention_parts, received, sum_up.received, sum_down.keep[-1] = join(
        *attention_parts, received, sum_up.received, sum_down.keep[-1]
    )
    norm_sum = norm_sum + received
    sum_attention = sum_of(attention_parts)
    if count > 16:
        sum_attention.from_across, received = join(
            sum_attention.from_across, exchanged(norm_sum, 16)
        )
        norm_sum = norm_sum + received
    sum_attention.second()
    sum_up.far(sum_attention.going)
    bit = 32
    while bit < count:
        norm_sum = norm_sum + exchanged(norm_sum, bit)
        bit *= 2
    received = exchanged(norm_sum, 2)
    sum_down.keep = after(sum_down.keep, sum_attention.going)
    grad_down, down_left_new, down_right_new, down_new = shampoo(
        shampoo_kernel, sum_down.keep, (w_down,), ((owned, ff),),
        (down_left, down_right, down_left_root, down_right_root),
    )
    sum_attention.received, received, *sooner = join(
        *after([sum_attention.received, received, *sum_up.keep[:-1]], down_new)
    )
    sum_up.keep = [*sooner, sum_up.keep[-1]]
    norm_sum = norm_sum + received
    sum_attention.first()
    received = exchanged(norm_sum, 4)
    (sum_up.keep[-1],) = after([sum_up.keep[-1]], sum_attention.going)
    sum_attention.received, sum_up.keep[-1], received = join(
        sum_attention.received, sum_up.keep[-1], received
    )
    norm_sum = norm_sum + received
    sum_attention.far()
    sum_up.keep = after(sum_up.keep, sum_attention.going)
    (
        grad_up, up_left_new, up_right_new, up_new, grad_out, out_left_new, out_right_new, out_new
    ) = shampoo(
        up_shampoo, sum_up.keep, (w_up, w_out), ((owned, ff), (owned, width_of(w_out))),
        (
            up_left, up_right, up_left_root, up_right_root,
            out_left, out_right, out_left_root, out_right_root,
        ),
    )
    (norm_sum,) = after([norm_sum], up_new)
    grad_norm = lax.dynamic_slice_in_dim(norm_sum, dp_index * owned, owned, 1).T
    norm_second_new = STAT_DECAY * norm_second + (1.0 - STAT_DECAY) * grad_norm * grad_norm
    own_params = lax.dynamic_slice_in_dim(norm_params, dp_index * owned, owned, 0)
    norm_new = own_params - NORM_RATE * grad_norm / (jnp.sqrt(norm_second_new) + 1e-08)
    *sum_attention.keep, grad_norm, norm_second_new, norm_new = join(
        *sum_attention.keep, grad_norm, norm_second_new, norm_new
    )
    qkv_turned = w_qkv.transpose(1, 0, 2)
    grad_qkv, qkv_left_new, qkv_right_new, qkv_new = shampoo(
        attention_shampoo, sum_attention.keep, (qkv_turned,), ((owned, 3 * w_qkv.shape[2]),),
        (qkv_left, qkv_right, qkv_left_root, qkv_right_root), limit=SMALL_BYTES,
    )
    grad_qkv, qkv_new = grad_qkv.transpose(1, 0, 2), qkv_new.transpose(1, 0, 2)
    (
        qkv_left_new, qkv_right_new, out_left_new, out_right_new,
        up_left_new, up_right_new, down_left_new, down_right_new,
    ) = (
        stat[None, None]
        for stat in (
            qkv_left_new, qkv_right_new, out_left_new, out_right_new,
            up_left_new, up_right_new, down_left_new, down_right_new,
        )
    )
    return (
        block_out.reshape(block_in.shape),
        input_grad.reshape(block_in.shape),
        loss[:, 0].reshape(micros, seqs),
        grad_qkv, qkv_left_new, qkv_right_new, qkv_new,
        grad_out, out_left_new, out_right_new, out_new,
        grad_up, up_left_new, up_right_new, up_new,
        grad_down, down_left_new, down_right_new, down_new,
        grad_norm, norm_second_new, norm_new,
    )


def solution(mesh):
    sequence = P(None, AXES)
    stat = P("dp", "mp", None, None)
    weight = P("dp", "mp")
    qkv = P("dp", None, "mp")
    norm = P("dp", None)
    in_specs = (sequence, sequence, sequence, qkv, weight, weight, weight, P(), norm) + (stat,) * 16
    out_specs = (
        (sequence, sequence, sequence)
        + (qkv, stat, stat, qkv)
        + (weight, stat, stat, weight) * 3
        + (norm, norm, norm)
    )
    return jax.shard_map(
        per_device, mesh=mesh, in_specs=in_specs, out_specs=out_specs, check_vma=False
    )
```

```python
import functools
import math

import jax
import jax.numpy as jnp
import numpy as np
from jax import lax
from jax.experimental import pallas as pl
from jax.experimental.pallas import tpu as pltpu
from jax.sharding import PartitionSpec as P

AXES = ("dp", "mp")
HD = 64
LANES = 128
EPSILON = 1e-06
SOFTMAX_TEMP = 2.0
LOSS_SCALE = 32.0
STAT_DECAY = 0.5
SHAMPOO_RATE = 0.3
NORM_RATE = 0.5
TILE = 256
VMEM_BYTES = 53 * 1024 * 1024
SMALL_BYTES = 20 * 1024 * 1024
F32 = jnp.float32
BF16 = jnp.bfloat16


def far_digits(count):
    digits = []
    weight = 8
    while weight < count:
        size = min(4, count // weight)
        digits.append((weight, size))
        weight *= size
    return digits


def near_steps(count):
    return (
        [i ^ (4 if i % 2 == 0 else 2) for i in range(count)],
        [i ^ (2 if i % 2 == 0 else 4) for i in range(count)],
        [i ^ 1 for i in range(count)],
    )


def far_steps(count, weight, size):
    return [[i ^ (weight * m) for i in range(count)] for m in range(1, size)]


def source_table(count, near_first):
    first, second, third = near_steps(count)
    far = [far_steps(count, weight, size) for weight, size in far_digits(count)]
    rounds = [[first]] + far if near_first else far + [[first]]
    table = np.arange(count)[:, None]
    for steps in rounds + [[second], [third]]:
        table = np.concatenate([table] + [table[np.array(step)] for step in steps], axis=1)
    return table


def swap(values, step):
    return lax.ppermute(values, AXES, list(enumerate(step)))


class Gather:
    def __init__(self, block, count):
        self.count = count
        self.near = near_steps(count)
        self.held = block[None]
        self.received = []

    def keep(self, *earlier):
        if self.received:
            self.received = after(self.received, *earlier)
            self.held = jnp.concatenate([self.held] + self.received, axis=0)
            self.received = []

    def far(self, *earlier):
        (self.held,) = after([self.held], *earlier)
        for weight, size in far_digits(self.count):
            self.keep()
            steps = far_steps(self.count, weight, size)
            self.received = [swap(self.held, step) for step in steps]

    def first(self, *earlier):
        (self.held,) = after([self.held], *earlier)
        self.received = [swap(self.held, self.near[0])]

    def second(self, *earlier):
        (self.held,) = after([self.held], *earlier)
        self.across = swap(self.held, self.near[1])

    def third(self, *earlier):
        (self.held,) = after([self.held], *earlier)
        self.held_other = swap(self.held, self.near[2])

    def last(self, *earlier):
        (self.across,) = after([self.across], *earlier)
        self.across_other = swap(self.across, self.near[2])

    def quarters(self):
        return self.held, self.across, self.held_other, self.across_other


def join(*values):
    return lax.optimization_barrier(values)


def after(values, *earlier, keep=None):
    if not earlier:
        return list(values)
    return list(lax.optimization_barrier((*values, *earlier)))[: keep or len(values)]


def add_low(*terms):
    return sum(term.astype(F32) for term in terms).astype(BF16)


class Sum:
    def __init__(self, quarters, count):
        self.count = count
        self.near = near_steps(count)
        self.held, self.across, held_other, across_other = quarters
        self.from_across = swap(across_other, self.near[2])
        self.from_held = swap(held_other, self.near[2])

    def second(self, *earlier):
        (received,) = after([self.from_across], *earlier)
        self.going = add_low(self.across, received)
        self.received = swap(self.going, self.near[1])

    def first(self, *earlier):
        (received,) = after([self.received], *earlier)
        half = self.held.shape[0] // 2
        terms = self.held, self.from_held, received
        self.going = add_low(*(term[half:] for term in terms))
        self.keep = add_low(*(term[:half] for term in terms))
        self.received = swap(self.going, self.near[0])

    def far_half(self, *earlier):
        if far_digits(self.count) != [(8, 4)]:
            return self.far(*earlier)
        (received,) = after([self.received], *earlier)
        terms = self.keep, received
        going = add_low(*(term[2:] for term in terms))
        self.keep = add_low(*(term[:2] for term in terms))
        self.received = swap(going, far_steps(self.count, 8, 4)[1])
        self.going = going

    def far_rest(self, *earlier):
        if far_digits(self.count) != [(8, 4)]:
            return
        (received,) = after([self.received], *earlier)
        going = add_low(self.keep[1:], received[1:])
        self.keep = [self.keep, received, swap(going, far_steps(self.count, 8, 4)[0])]
        self.going = going

    def far(self, *earlier):
        (received,) = after([self.received], *earlier)
        keep = [self.keep, received]
        for weight, size in far_digits(self.count)[::-1]:
            step_size = keep[0].shape[0] // size
            parts = [
                add_low(*(term[m * step_size : (m + 1) * step_size] for term in keep))
                for m in range(1, size)
            ]
            keep = [term[:step_size] if step_size > 1 else term for term in keep] + [
                swap(part, step)
                for part, step in zip(parts, far_steps(self.count, weight, size))
            ]
        self.going = parts[-1]
        self.keep = keep


def dot(left, right, left_dim, right_dim):
    return lax.dot_general(
        left, right, (((left_dim,), (right_dim,)), ((), ())), preferred_element_type=F32
    )


def load_weights(places, parts, weights, sems, first=0):
    size, rows, _ = parts[0].shape
    groups, _, cols = weights.shape
    me = places[2 * size * len(parts)]

    def body(q, carry):
        for i, part in enumerate(parts):
            index = places[i * size + q] ^ me
            group = index % groups
            place = pl.multiple_of((index // groups) * rows, 16)
            pltpu.make_async_copy(
                part.at[q, :, pl.ds(first, cols)],
                weights.at[group, pl.ds(place, rows), :],
                sems.at[group],
            ).start()
        return carry

    lax.fori_loop(0, size, body, 0)


def store_blocks(places, source, group, groups, parts, sem):
    size, rows, _ = parts[0].shape
    count = size * len(parts)
    me = places[2 * count]

    def body(p, carry):
        position = places[count + ((p * groups + group) ^ me)]
        block = source.at[pl.ds(pl.multiple_of(p * rows, 16), rows), :]
        for i, part in enumerate(parts):

            @pl.when((position // size) % len(parts) == i)
            def _():
                pltpu.make_async_copy(block, part.at[position % size], sem).start()

        return carry

    lax.fori_loop(0, source.shape[0] // rows, body, 0)


def wait_weights(weights, sems, group):
    pltpu.make_async_copy(weights.at[group], weights.at[group], sems.at[group]).wait()


def normalize(values):
    center = values - jnp.mean(values, axis=-1, keepdims=True)
    spread = jnp.mean(center * center, axis=-1, keepdims=True)
    scale = lax.rsqrt(spread + EPSILON)
    return center * scale, scale


def low_lanes(dtype=BF16):
    lane = lax.broadcasted_iota(jnp.int32, (1, LANES), 1)
    return jnp.where(lane < HD, 1.0, 0.0).astype(dtype)


def pairs_of(blocks, low):
    first, second = blocks

    def join(left, right, high_half):
        if high_half:
            return jnp.where(low, turn(left), right)
        return jnp.where(low, left, turn(right))

    return (
        (first[0], first[1], first[2]),
        (second[0], second[1], second[2]),
        (
            join(first[3], second[3], False),
            join(first[4], second[4], False),
            join(first[3], second[3], True),
        ),
    )


def turn(values):
    return jnp.concatenate([values[:, HD:], values[:, :HD]], axis=1)


def both_heads(values, low_mask, high_mask):
    return jnp.concatenate([values * low_mask, values * high_mask], axis=0)


def diagonal(full, seq_len, own_cols):
    picked = full[:seq_len]
    for i, own in enumerate(own_cols):
        if i:
            picked = jnp.where(own, full[i * seq_len : (i + 1) * seq_len], picked)
    return picked


def undiagonal(compact, own_cols):
    return jnp.concatenate(
        [jnp.where(own, compact, jnp.zeros_like(compact)) for own in own_cols], axis=0
    )


def sequence_columns(seq_len):
    lane = lax.broadcasted_iota(jnp.int32, (seq_len, 2 * LANES), 1) % LANES
    return [lane // seq_len == i for i in range(LANES // seq_len)]


def stack_heads(values):
    return jnp.concatenate([values[:, :LANES], values[:, LANES:]], axis=0)


def spread(values, seq_len):
    seqs, width = values.shape
    return jnp.broadcast_to(values[:, None, :], (seqs, seq_len, width)).reshape(
        seqs * seq_len, width
    )


def live_column(counts, seq_len):
    wide = spread(counts, seq_len)
    slot = lax.broadcasted_iota(jnp.int32, wide.shape, 0) % seq_len
    return jnp.where(slot.astype(F32) < wide, 1.0, 0.0)[:, 0:1]


def first_norm(x_ref, norm_ref, h1_ref, turned_ref):
    n1, _ = normalize(x_ref[...].astype(F32))
    h1 = (n1 * norm_ref[0:1, :] + norm_ref[1:2, :]).astype(BF16)
    h1_ref[...] = h1
    turned_ref[...] = h1.T


def attention_forward(
    order, x_ref, h1_ref, live_ref, norm_ref, w0, w1, w2, w3,
    proj_ref, heads_ref, lse_ref, mid_ref, h2_ref,
    weights, sems, *, seq_len,
):
    groups = weights.shape[0]
    first = pl.program_id(0) == 0

    @pl.when(first)
    def _():
        load_weights(order, (w0, w1, w2, w3), weights, sems)
        for group in range(weights.shape[0]):
            wait_weights(weights, sems, group)

    x = x_ref[...].astype(F32)
    rows = x.shape[0]
    h1 = h1_ref[...]
    low_mask = low_lanes()
    high_mask = 1 - low_mask
    low = lax.broadcasted_iota(jnp.int32, (1, LANES), 1) < HD
    own_cols = sequence_columns(seq_len)
    count = rows // LANES
    duos = groups // 2
    projected = [
        dot(h1, weights[group, :, : 5 * LANES], 1, 0).astype(BF16) for group in range(groups)
    ]
    chains = []
    for duo in range(duos):
        for t in range(count):
            span = slice(t * LANES, (t + 1) * LANES)
            blocks = [
                [proj[span, i * LANES : (i + 1) * LANES] for i in range(5)]
                for proj in projected[2 * duo : 2 * duo + 2]
            ]
            for i, (q, k, v) in enumerate(pairs_of(blocks, low)):
                for which, part in enumerate((q, k, v)):
                    at = ((duo * 3 + i) * 3 + which) * LANES
                    proj_ref[span, at : at + LANES] = part
                chains.append((t, duo * 3 + i, q, k, v))
    scores = [dot(k, both_heads(q, low_mask, high_mask), 1, 1) for t, i, q, k, v in chains]
    probs = []
    for (t, i, *_), full in zip(chains, scores):
        compact = diagonal(full, seq_len, own_cols) * (HD**-0.5)
        compact = jnp.where(live_ref[t] > 0.0, compact, -1e30)
        top = jnp.max(compact, axis=0, keepdims=True)
        powers = jnp.exp(compact - top)
        power = jnp.sum(powers, axis=0, keepdims=True)
        lse_ref[t, i : i + 1, :] = top + jnp.log(power)
        probs.append(undiagonal((powers * (1.0 / power)).astype(BF16), own_cols))
    outs = [
        dot(stack_heads(part), both_heads(v, low_mask, high_mask), 0, 0)
        for part, (t, i, q, k, v) in zip(probs, chains)
    ]
    total = x
    for duo in range(duos):
        heads = [[], []]
        for t in range(count):
            at = 3 * (duo * count + t)
            one, two, third = outs[at : at + 3]
            heads[0].append(
                jnp.concatenate([jnp.where(low, 0.0, turn(third)), one], axis=1).astype(BF16)
            )
            heads[1].append(
                jnp.concatenate([jnp.where(low, 0.0, third), two], axis=1).astype(BF16)
            )
        for side, group in enumerate((2 * duo, 2 * duo + 1)):
            joined = jnp.concatenate(heads[side], axis=0)
            heads_ref[:, group * 2 * LANES : (group + 1) * 2 * LANES] = joined
            total = total + dot(joined, weights[group, :, 4 * LANES :], 1, 1)
    mid_ref[...] = total
    n2, _ = normalize(total)
    h2_ref[...] = (n2 * norm_ref[2:3, :] + norm_ref[3:4, :]).astype(BF16)


def up_forward(
    places, h2_ref, count_ref, w0, w1, w2, w3,
    hid_ref, slope_ref, pooled_ref,
    weights, sems, *, seq_len,
):
    groups, _, wide = weights.shape

    @pl.when(pl.program_id(0) == 0)
    def _():
        load_weights(places, (w0, w1, w2, w3), weights, sems)
        for group in range(groups):
            wait_weights(weights, sems, group)

    h2 = h2_ref[...]
    rows = h2.shape[0]
    counts = count_ref[...]
    live = live_column(counts, seq_len)
    seqs = rows // seq_len
    slot = lax.broadcasted_iota(jnp.int32, (seqs, rows), 1)
    member = slot // seq_len == lax.broadcasted_iota(jnp.int32, (seqs, rows), 0)
    within = (slot % seq_len).astype(F32) < counts[:, 0:1]
    pool = jnp.where(jnp.logical_and(member, within), 1.0, 0.0).astype(BF16)
    for group in range(groups):
        cols = slice(group * wide, (group + 1) * wide)
        up = dot(h2, weights[group], 1, 0)
        gate = 0.5 + 0.5 * lax.erf(up * (0.5**0.5))
        hid = (up * gate).astype(BF16)
        hid_ref[:, cols] = hid
        bell = jnp.exp(up * up * -0.5) * (1.0 / math.sqrt(2.0 * math.pi))
        slope_ref[:, cols] = ((gate + up * bell) * live).astype(BF16)
        pooled_ref[:, cols] = dot(pool, hid, 1, 0).astype(BF16)


def down_forward(
    order, hid_ref, mid_ref, count_ref, w0, w1, w2, w3,
    out_ref, pooled_ref, weights, sems, *, seq_len,
):
    groups, _, width = weights.shape
    first = pl.program_id(0) == 0

    @pl.when(first)
    def _():
        load_weights(order, (w0, w1, w2, w3), weights, sems)
        for group in range(weights.shape[0]):
            wait_weights(weights, sems, group)

    total = mid_ref[...]
    for group in range(groups):


        total = total + dot(
            hid_ref[:, group * width : (group + 1) * width], weights[group], 1, 1
        )
    out_ref[...] = total.astype(BF16)
    rows, features = total.shape
    counts = count_ref[...]
    live = live_column(counts, seq_len)
    seqs = rows // seq_len
    sums = jnp.sum((total * live).reshape(seqs, seq_len, features), axis=1)
    pooled_ref[...] = sums / counts[:, 0:1]


def loss_backward(
    places, pooled_ref, count_ref, m0, m1, m2, m3, hid_ref,
    loss_ref, grad_ref, low_ref, g0, g1, g2, g3,
    slots, slot_sems, *, micros, groups,
):
    ff = slots.shape[2]
    pooled = pooled_ref[...]
    seqs, width = pooled.shape
    each = seqs // micros
    scale_text = SOFTMAX_TEMP / math.sqrt(width)
    r = lax.rsqrt(jnp.mean(pooled * pooled, axis=-1, keepdims=True) + EPSILON)
    text = (pooled * r).astype(BF16)
    row_micro = lax.broadcasted_iota(jnp.int32, (seqs, 1), 0) // each
    step = min(m0.shape[0], 1024)
    pieces = [
        ref[i : i + step, :]
        for ref in (m0, m1, m2, m3)
        for i in range(0, ref.shape[0], step)
    ]
    col = lax.broadcasted_iota(jnp.int32, (1, step), 1)
    same = (col // each) % micros == row_micro
    logits = [jnp.where(same, dot(text, piece, 1, 1) * scale_text, -1e30) for piece in pieces]
    top = functools.reduce(
        jnp.maximum, [jnp.max(part, axis=1, keepdims=True) for part in logits]
    )
    powers = [jnp.exp(part - top) for part in logits]
    total = functools.reduce(jnp.add, [jnp.sum(part, axis=1, keepdims=True) for part in powers])
    log_total = top + jnp.log(total)
    positive = lax.broadcasted_iota(jnp.int32, (seqs, 1), 0) == col
    loss = log_total - jnp.sum(jnp.where(positive, logits[0], 0.0), axis=1, keepdims=True)
    loss_ref[...] = jnp.broadcast_to(loss, loss_ref.shape)
    inverse = LOSS_SCALE / total
    grad_text = jnp.zeros((seqs, width), F32)
    for i, (part, piece) in enumerate(zip(powers, pieces)):
        grad_part = part * inverse
        if i == 0:
            grad_part = grad_part - jnp.where(positive, LOSS_SCALE, 0.0)
        grad_text = grad_text + dot(grad_part.astype(BF16), piece, 1, 0)
    grad_text = grad_text * scale_text
    along = jnp.mean(grad_text * pooled, axis=-1, keepdims=True)
    grad = (r * grad_text - (r * r * r) * pooled * along) / count_ref[:, 0:1]
    grad_ref[...] = grad
    low = grad.astype(BF16)
    low_ref[...] = low
    turned = low.T
    for group in range(groups):
        cols = slice(group * ff, (group + 1) * ff)
        if group >= 2:
            drain(slots, slot_sems, group % 2)
        slots[group % 2] = dot(turned, hid_ref[:, cols], 1, 0).astype(BF16)
        store_blocks(
            places, slots.at[group % 2], group, groups, (g0, g1, g2, g3),
            slot_sems.at[group % 2],
        )
    for which in range(min(groups, 2)):
        drain(slots, slot_sems, which)


def drain(slots, sems, which):
    pltpu.make_async_copy(slots.at[which], slots.at[which], sems.at[which]).wait()


def finish_blocks(slots, sems, group, groups, slot):
    @pl.when(group == groups - 1)
    def _():
        drain(slots, sems, slot)

        @pl.when(groups >= 2)
        def _():
            drain(slots, sems, 1 - slot)


def weight_gradient(places, *refs):
    pairs = (len(refs) - 6) // 3
    lefts, rights = refs[: 2 * pairs : 2], refs[1 : 2 * pairs : 2]
    parts, turned = refs[2 * pairs : 2 * pairs + 4], refs[2 * pairs + 4 : -2]
    slots, sems = refs[-2:]
    group = pl.program_id(0)
    groups = pl.num_programs(0)
    slot = group % 2

    @pl.when(group == 0)
    def _():
        for left, across in zip(lefts, turned):
            across[...] = left[...].T

    @pl.when(group >= 2)
    def _():
        drain(slots, sems, slot)

    first = 0
    for across, right in zip(turned, rights):
        last = first + right.shape[1]
        slots[slot, :, first:last] = dot(across[...], right[...], 1, 0).astype(BF16)
        first = last
    store_blocks(places, slots.at[slot], group, groups, parts, sems.at[slot])
    finish_blocks(slots, sems, group, groups, slot)


def turned_gradient(places, left_ref, right_ref, g0, g1, g2, g3, slots, sems):
    group = pl.program_id(0)
    groups = pl.num_programs(0)
    slot = group % 2

    @pl.when(group >= 2)
    def _():
        drain(slots, sems, slot)

    slots[slot] = dot(left_ref[...], right_ref[...], 1, 0).astype(BF16)
    store_blocks(places, slots.at[slot], group, groups, (g0, g1, g2, g3), sems.at[slot])
    finish_blocks(slots, sems, group, groups, slot)


def norm_back(grad, gain, values):
    n, scale = normalize(values)
    scaled = grad * gain
    moved = scale * (
        scaled
        - jnp.mean(scaled, axis=-1, keepdims=True)
        - n * jnp.mean(scaled * n, axis=-1, keepdims=True)
    )
    gain_grad = jnp.sum(grad * n, axis=0, keepdims=True)
    shift_grad = jnp.sum(grad, axis=0, keepdims=True)
    return moved, gain_grad, shift_grad


def down_backward(order, low_ref, w0, w1, w2, w3, by_seq_ref, weights, sems):
    groups, _, width = weights.shape
    load_weights(order, (w0, w1, w2, w3), weights, sems)
    for group in range(groups):
        wait_weights(weights, sems, group)
        by_seq_ref[:, group * width : (group + 1) * width] = dot(
            low_ref[...], weights[group], 1, 0
        )


def mlp_backward(
    order, grad_ref, by_seq_ref, slope_ref, count_ref, mid_ref, norm_ref,
    w0, w1, w2, w3,
    dup_ref, dmid_ref, dmid_low_ref, sums_ref,
    weights, sems, *, seq_len,
):
    groups, _, width = weights.shape

    @pl.when(pl.program_id(0) == 0)
    def _():
        load_weights(order, (w0, w1, w2, w3), weights, sems)
        sums_ref[...] = jnp.zeros_like(sums_ref)
        for group in range(groups):
            wait_weights(weights, sems, group)

    grad = grad_ref[...]
    mid = mid_ref[...]
    rows, features = mid.shape

    total = jnp.zeros((rows, features), F32)
    for group in range(groups):


        cols = slice(group * width, (group + 1) * width)
        dup = (slope_ref[:, cols].astype(F32) * spread(by_seq_ref[:, cols], seq_len)).astype(BF16)
        dup_ref[:, cols] = dup
        total = total + dot(dup, weights[group], 1, 1)
    moved, gain_grad, shift_grad = norm_back(total, norm_ref[2:3, :], mid)
    live = live_column(count_ref[...], seq_len)
    dmid = spread(grad, seq_len) * live + moved
    dmid_ref[...] = dmid
    dmid_low_ref[...] = dmid.astype(BF16)
    sums_ref[0:1, :] += gain_grad
    sums_ref[1:2, :] += shift_grad


def attention_backward(
    places, x_ref, live_ref, norm_ref, proj_ref, lse_ref, dmid_ref, dmid_low_ref,
    w0, w1, w2, w3, dproj_ref, dx_ref, sums_ref, weights, sems, *, seq_len,
):
    groups = weights.shape[0]

    @pl.when(pl.program_id(0) == 0)
    def _():
        load_weights(places, (w0, w1, w2, w3), weights, sems)
        for group in range(groups):
            wait_weights(weights, sems, group)
        sums_ref[...] = jnp.zeros_like(sums_ref)

    x = x_ref[...].astype(F32)
    rows = x.shape[0]
    dmid_low = dmid_low_ref[...]
    low_mask = low_lanes()
    high_mask = 1 - low_mask
    low = lax.broadcasted_iota(jnp.int32, (1, LANES), 1) < HD
    own_cols = sequence_columns(seq_len)
    score_scale = HD**-0.5
    count = rows // LANES
    duos = groups // 2
    dheads = [
        dot(dmid_low, weights[group, :, 4 * LANES :], 1, 0).astype(BF16)
        for group in range(groups)
    ]
    chains = []
    for duo in range(duos):
        first_d, second_d = dheads[2 * duo : 2 * duo + 2]
        for t in range(count):
            span = slice(t * LANES, (t + 1) * LANES)
            for i, d in enumerate(
                (
                    first_d[span, LANES:],
                    second_d[span, LANES:],
                    jnp.where(low, turn(first_d[span, :LANES]), second_d[span, :LANES]),
                )
            ):
                at = (duo * 3 + i) * 3 * LANES
                q, k, v = (
                    proj_ref[span, at + j * LANES : at + (j + 1) * LANES] for j in range(3)
                )
                qq, kk, dd = (both_heads(part, low_mask, high_mask) for part in (q, k, d))
                chains.append((t, duo * 3 + i, k, v, qq, kk, dd))
    scores = [dot(k, qq, 1, 1) for t, i, k, v, qq, kk, dd in chains]
    powers = [dot(v, dd, 1, 1) for t, i, k, v, qq, kk, dd in chains]
    wide = []
    for (t, i, *_), full, power in zip(chains, scores, powers):
        live = live_ref[t] > 0.0
        compact = diagonal(full, seq_len, own_cols) * score_scale
        lse = lse_ref[t, i : i + 1, :]
        probs = jnp.where(live, jnp.exp(jnp.where(live, compact - lse, 0.0)), 0.0)
        dprobs = diagonal(power, seq_len, own_cols)
        inner = jnp.sum(probs * dprobs, axis=0, keepdims=True)
        dscores = probs * (dprobs - inner) * score_scale
        wide.append(
            (
                undiagonal(dscores.astype(BF16), own_cols),
                undiagonal(probs.astype(BF16), own_cols),
            )
        )
    outs = [
        (dot(stack_heads(ds), kk, 0, 0), dot(ds, qq, 1, 0), dot(p, dd, 1, 0))
        for (ds, p), (t, i, k, v, qq, kk, dd) in zip(wide, chains)
    ]
    total = jnp.zeros(x.shape, F32)
    for duo in range(duos):
        grads = [[], []]
        for t in range(count):
            at = 3 * (duo * count + t)
            one, two, third = outs[at : at + 3]
            grads[0].append(
                jnp.concatenate(
                    one
                    + (jnp.where(low, third[0], turn(third[2])), jnp.where(low, third[1], 0.0)),
                    axis=1,
                ).astype(BF16)
            )
            grads[1].append(
                jnp.concatenate(
                    two
                    + (jnp.where(low, turn(third[0]), third[2]), jnp.where(low, turn(third[1]), 0.0)),
                    axis=1,
                ).astype(BF16)
            )
        for side, group in enumerate((2 * duo, 2 * duo + 1)):
            dproj = jnp.concatenate(grads[side], axis=0)
            dproj_ref[:, group * 5 * LANES : (group + 1) * 5 * LANES] = dproj
            total = total + dot(dproj, weights[group, :, : 5 * LANES], 1, 1)
    moved, gain_grad, shift_grad = norm_back(total, norm_ref[0:1, :], x)
    dx_ref[...] = dmid_ref[...] + moved
    sums_ref[0:1, :] += gain_grad
    sums_ref[1:2, :] += shift_grad


def renew(grad, left, right, left_root, right_root):
    low = grad.astype(BF16)
    keep = 1.0 - STAT_DECAY
    half = dot(left_root.astype(BF16), low, 1, 0).astype(BF16)
    return (
        STAT_DECAY * left + keep * dot(low, low, 1, 1),
        STAT_DECAY * right + keep * dot(low, low, 0, 0),
        SHAMPOO_RATE * dot(half, right_root.astype(BF16), 1, 0),
    )


def shampoo_kernel(*refs):
    terms = refs[:-9]
    master_ref, *stats = refs[-9:-4]
    grad_ref, left_new_ref, right_new_ref, new_ref = refs[-4:]
    grad = sum(term[0].astype(F32) for term in terms)
    grad_ref[...] = grad
    left_new_ref[...], right_new_ref[...], step = renew(grad, *(ref[...] for ref in stats))
    new_ref[...] = master_ref[...] - step


def up_shampoo(*refs):
    terms = refs[:-18]
    up_ref, out_ref, *stats = refs[-18:-8]
    up_grad, up_left, up_right, up_new, out_grad, out_left, out_right, out_new = refs[-8:]
    packed = sum(term[0].astype(F32) for term in terms)
    wide = up_ref.shape[1]
    up, out = packed[:, :wide], unpack_out(packed[:, wide:])
    up_grad[...] = up
    up_left[...], up_right[...], step = renew(up, *(ref[...] for ref in stats[:4]))
    up_new[...] = up_ref[...] - step
    out_grad[...] = out
    out_left[...], out_right[...], step = renew(out, *(ref[...] for ref in stats[4:]))
    out_new[...] = out_ref[...] - step


def attention_shampoo(*refs):
    terms = refs[:-9]
    qkv_ref, *stats = refs[-9:-4]
    qkv_grad, qkv_left, qkv_right, qkv_new = refs[-4:]
    qkv = unpack_qkv(sum(term[0].astype(F32) for term in terms))
    qkv_left[...], qkv_right[...], step = renew(qkv, *(ref[...] for ref in stats))
    width = qkv_ref.shape[2]
    for i in range(3):
        cols = slice(i * width, (i + 1) * width)
        qkv_grad[i] = qkv[:, cols]
        qkv_new[i] = qkv_ref[i] - step[:, cols]


ANY = pl.BlockSpec(memory_space=pl.ANY)
SMEM = pl.BlockSpec(memory_space=pltpu.SMEM)
WHOLE = pl.BlockSpec(memory_space=pltpu.VMEM)


def rows_of(width, height=TILE, start=0):
    return pl.BlockSpec((height, width), lambda i: (i + start, 0))


def fixed(shape):
    return pl.BlockSpec(shape, lambda i: (0,) * len(shape))


def params(limit=VMEM_BYTES):
    return pltpu.CompilerParams(vmem_limit_bytes=limit)


def cost(flops, bytes_accessed):
    return pl.CostEstimate(flops=4 * int(flops), bytes_accessed=int(bytes_accessed), transcendentals=0)


def shape_of(*dims, dtype=BF16):
    return jax.ShapeDtypeStruct(dims, dtype)


def stat_shapes(rows, cols):
    return shape_of(rows, rows, dtype=F32), shape_of(cols, cols, dtype=F32)


def shampoo(kernel, terms, masters, shapes, stats, limit=VMEM_BYTES):
    rows, cols = terms[0].shape[1:]
    out_shape = []
    for master, (left, right) in zip(masters, shapes):
        value = shape_of(*master.shape, dtype=F32)
        out_shape += [value, *stat_shapes(left, right), value]
    return pl.pallas_call(
        kernel,
        grid=(1,),
        out_shape=tuple(out_shape),
        in_specs=[pl.BlockSpec((1, rows, cols), lambda i: (0, 0, 0))] * len(terms)
        + [WHOLE] * (len(masters) + len(stats)),
        out_specs=(WHOLE,) * len(out_shape),
        compiler_params=params(limit),
        cost_estimate=cost(4 * rows * cols * cols, 12 * cols * cols),
        name=kernel.__name__,
    )(*terms, *masters, *(stat[0, 0] for stat in stats))


def pack_qkv(qkv):
    q, k, v = (qkv[:, i] for i in range(3))
    a, b = 2 * HD, 3 * HD
    third = [q[:, a:b], v[:, a:b], k[:, a:b], jnp.zeros_like(k[:, a:b])]
    return jnp.concatenate([q[:, :a], k[:, :a], v[:, :a]] + third, axis=1)


def pack_attention(qkv, out):
    packed = pack_qkv(qkv)
    return jnp.concatenate([packed[:, : 9 * HD], out[:, 2 * HD :], out[:, : 2 * HD]], axis=1)


def unpack_qkv(packed):
    c = [packed[:, i * HD : (i + 1) * HD] for i in range(10)]
    return jnp.concatenate([c[0], c[1], c[6], c[2], c[3], c[8], c[4], c[5], c[7]], axis=1)


def unpack_out(packed):
    return jnp.concatenate([packed[:, 2 * HD :], packed[:, HD : 2 * HD]], axis=1)


def per_device(
    block_in, seq_lengths, image_embed, w_qkv, w_out, w_up, w_down, norm_params, norm_second,
    qkv_left, qkv_right, qkv_left_root, qkv_right_root,
    out_left, out_right, out_left_root, out_right_root,
    up_left, up_right, up_left_root, up_right_root,
    down_left, down_right, down_left_root, down_right_root,
):
    micros, seqs, seq_len, width = block_in.shape
    dp_count, groups = lax.axis_size("dp"), lax.axis_size("mp")
    count = dp_count * groups
    dp_index = lax.axis_index("dp")
    me = dp_index * groups + lax.axis_index("mp")
    owned = w_up.shape[0]
    ff = w_up.shape[1]
    all_seqs = micros * seqs
    rows = all_seqs * seq_len
    tiles = rows // TILE
    seq_tile = TILE // seq_len
    direct = owned % 16 == 0

    def places(near_first):
        masks = source_table(count, near_first)[:2] ^ np.arange(2)[:, None]
        masks = np.concatenate([masks, np.argsort(masks, axis=1)], axis=1)
        odd = me % 2 == 1
        mine = jnp.where(odd, jnp.asarray(masks[1], jnp.int32), jnp.asarray(masks[0], jnp.int32))
        return jnp.concatenate([mine, me.astype(jnp.int32)[None]])

    far_places, near_places = places(False), places(True)

    def order_of(places):
        return places[:count] ^ me

    def inverse_of(places):
        return places[count : 2 * count][jnp.arange(count) ^ me]

    def weights_of(gather, places):
        quarters = gather.quarters()
        if direct:
            return quarters
        whole = jnp.concatenate(quarters, axis=0)[inverse_of(places)]
        whole = whole.reshape(dp_count, groups, owned, whole.shape[-1])
        whole = whole.transpose(1, 0, 2, 3).reshape(groups, width, whole.shape[-1])
        return tuple(jnp.split(whole, 4, axis=0))

    plain = jnp.arange(groups, dtype=jnp.int32)
    if direct:
        kernel_far, kernel_near = far_places, near_places
    else:
        kernel_far = kernel_near = jnp.concatenate([plain, plain, jnp.zeros(1, jnp.int32)])
    block_rows = owned if direct else width
    quarter = (count if direct else groups) // 4

    def sum_of(quarters):
        if not direct:
            whole = jnp.concatenate(quarters, axis=0)
            whole = whole.reshape(groups, dp_count, owned, whole.shape[2])
            whole = whole.transpose(1, 0, 2, 3).reshape(count, owned, whole.shape[3])[order_of(far_places)]
            quarters = jnp.split(whole, 4, axis=0)
        return Sum(quarters, count)

    def width_of(array):
        return array.shape[1]

    own_attention = pack_attention(w_qkv.astype(BF16), w_out.astype(BF16))
    own_up, own_down = w_up.astype(BF16), w_down.astype(BF16)
    own_images = image_embed.reshape(all_seqs, width)
    gather_attention, gather_up, gather_down, gather_images = (
        Gather(block, count) for block in (own_attention, own_up, own_down, own_images)
    )
    gather_attention.far()
    later = gather_down, gather_images
    for gather in later:
        gather.first()
        gather.keep()
    gather_attention.keep(*(gather.held for gather in later))
    gather_attention.first()
    gather_up.far(gather_attention.held)

    x = block_in.reshape(rows, width)
    norms = norm_params.T
    lengths = seq_lengths.reshape(all_seqs)
    live = (jnp.arange(seq_len)[None, :] < lengths[:, None]).astype(F32)
    tile_seqs = LANES // seq_len
    live_keys = live.reshape(rows // LANES, tile_seqs, 1, seq_len)
    live_keys = jnp.broadcast_to(
        live_keys, (rows // LANES, tile_seqs, seq_len, seq_len)
    ).transpose(0, 3, 1, 2).reshape(rows // LANES, seq_len, LANES)
    live_keys = jnp.concatenate([live_keys, live_keys], axis=2)
    counts = jnp.broadcast_to(lengths.astype(F32)[:, None], (all_seqs, LANES))

    count_spec = rows_of(LANES, seq_tile)
    keys_spec = pl.BlockSpec((TILE // LANES, seq_len, 2 * LANES), lambda i: (i, 0, 0))
    lse_spec = pl.BlockSpec((TILE // LANES, 8, 2 * LANES), lambda i: (i, 0, 0))
    norm_spec = fixed((4, width))
    all_ff, all_heads = groups * ff, groups * 2 * LANES
    packed = width_of(own_attention)

    def weight_scratch(cols):
        return [pltpu.VMEM((groups, width, cols), BF16), pltpu.SemaphoreType.DMA((groups,))]

    x_ready, live_keys, counts, kernel_far, kernel_near = after(
        [x, live_keys, counts, kernel_far, kernel_near], gather_attention.held
    )
    h1, h1_turned = pl.pallas_call(
        first_norm,
        grid=(tiles,),
        in_specs=[rows_of(width), norm_spec],
        out_specs=(rows_of(width), pl.BlockSpec((width, TILE), lambda i: (0, i))),
        out_shape=(shape_of(rows, width), shape_of(width, rows)),
        compiler_params=params(),
        cost_estimate=cost(1, 100e6),
        name="first_norm",
    )(x_ready, norms)
    h1, live_keys, counts, kernel_far, kernel_near = join(
        h1, live_keys, counts, kernel_far, kernel_near
    )
    gather_attention.keep(h1)
    gather_attention.second()
    gather_attention.third()
    gather_up.keep(gather_attention.held)
    gather_attention.last(gather_up.held)
    gather_up.first(gather_attention.across)
    gather_down.far(gather_up.held)
    gather_up.keep(gather_attention.across)
    gather_up.second()
    gather_up.third()
    attention_w = weights_of(gather_attention, far_places)

    (h1_ready,) = after([h1], gather_up.held)
    proj, heads, lse, mid, h2 = pl.pallas_call(
        functools.partial(attention_forward, seq_len=seq_len),
        grid=(tiles,),
        in_specs=[SMEM, rows_of(width), rows_of(width), keys_spec, norm_spec, ANY, ANY, ANY, ANY],
        out_specs=(
            rows_of(3 * width), rows_of(all_heads), lse_spec, rows_of(width),
            rows_of(width),
        ),
        out_shape=(
            shape_of(rows, 3 * width), shape_of(rows, all_heads),
            shape_of(rows // LANES, 8, 2 * LANES, dtype=F32),
            shape_of(rows, width, dtype=F32), shape_of(rows, width),
        ),
        scratch_shapes=weight_scratch(packed),
        compiler_params=params(),
        cost_estimate=cost(2 * rows * width * groups * 900, 12e6),
        name="attention_forward",
    )(kernel_far, x, h1_ready, live_keys, norms, *attention_w)

    gather_down.keep(h2)
    gather_up.last(gather_down.held)
    gather_down.second()
    gather_down.third()
    gather_images.far(gather_down.held)
    up_w = weights_of(gather_up, far_places)
    (h2_ready,) = after([h2], gather_down.held)

    hid, slope, pooled_hid = pl.pallas_call(
        functools.partial(up_forward, seq_len=seq_len),
        grid=(tiles,),
        in_specs=[SMEM, rows_of(width), count_spec, ANY, ANY, ANY, ANY],
        out_specs=(rows_of(groups * ff), rows_of(groups * ff), rows_of(groups * ff, seq_tile)),
        out_shape=(
            shape_of(rows, groups * ff), shape_of(rows, groups * ff), shape_of(all_seqs, groups * ff),
        ),
        scratch_shapes=weight_scratch(ff),
        compiler_params=params(),
        cost_estimate=cost(2 * rows * width * groups * ff, 20e6),
        name="up_forward",
    )(kernel_far, h2_ready, counts, *up_w)

    gather_images.keep(hid)
    gather_down.last(hid, gather_images.held)
    gather_images.second(gather_down.across)
    gather_images.third()
    down_w = weights_of(gather_down, near_places)
    (hid_ready,) = after([hid], gather_images.held)

    block_out, pooled = pl.pallas_call(
        functools.partial(down_forward, seq_len=seq_len),
        grid=(tiles,),
        in_specs=[SMEM, rows_of(all_ff), rows_of(width), count_spec, ANY, ANY, ANY, ANY],
        out_specs=(rows_of(width), rows_of(width, seq_tile)),
        out_shape=(shape_of(rows, width), shape_of(all_seqs, width, dtype=F32)),
        scratch_shapes=weight_scratch(ff),
        compiler_params=params(),
        cost_estimate=cost(2 * rows * width * groups * ff, 20e6),
        name="down_forward",
    )(kernel_near, hid_ready, mid, counts, *down_w)

    gather_images.last(pooled)
    images = [part.reshape(-1, width) for part in gather_images.quarters()]

    def quarters_of(cols):
        return (shape_of(quarter, block_rows, cols),) * 4

    loss, grad_seq, grad_low, *down_parts = pl.pallas_call(
        functools.partial(loss_backward, micros=micros, groups=groups),
        in_specs=[SMEM] + [WHOLE] * 7,
        out_specs=(WHOLE,) * 3 + (ANY,) * 4,
        out_shape=(
            shape_of(all_seqs, LANES, dtype=F32), shape_of(all_seqs, width, dtype=F32),
            shape_of(all_seqs, width),
        ) + quarters_of(ff),
        scratch_shapes=[pltpu.VMEM((2, width, ff), BF16), pltpu.SemaphoreType.DMA((2,))],
        compiler_params=params(),
        cost_estimate=cost(8 * all_seqs * width * groups * ff, 20e6),
        name="loss_backward",
    )(kernel_far, pooled, counts, *images, pooled_hid)
    sum_down = sum_of(down_parts)

    by_seq = pl.pallas_call(
        down_backward,
        in_specs=[SMEM, WHOLE, ANY, ANY, ANY, ANY],
        out_specs=WHOLE,
        out_shape=shape_of(all_seqs, all_ff, dtype=F32),
        scratch_shapes=weight_scratch(ff),
        compiler_params=params(),
        cost_estimate=cost(8 * all_seqs * width * groups * ff, 6e6),
        name="down_backward",
    )(kernel_near, grad_low, *down_w)
    by_seq, sum_down.from_across = join(by_seq, sum_down.from_across)
    sum_down.second()
    (grad_seq,) = after([grad_seq], sum_down.going)

    dup, dmid, dmid_low, sums_two = pl.pallas_call(
        functools.partial(mlp_backward, seq_len=seq_len),
        grid=(tiles,),
        in_specs=[
            SMEM, rows_of(width, seq_tile), rows_of(groups * ff, seq_tile), rows_of(groups * ff),
            count_spec, rows_of(width), norm_spec, ANY, ANY, ANY, ANY,
        ],
        out_specs=(rows_of(groups * ff), rows_of(width), rows_of(width), fixed((2, width))),
        out_shape=(
            shape_of(rows, groups * ff), shape_of(rows, width, dtype=F32), shape_of(rows, width),
            shape_of(2, width, dtype=F32),
        ),
        scratch_shapes=weight_scratch(ff),
        compiler_params=params(),
        cost_estimate=cost(2 * rows * width * groups * ff, 25e6),
        name="mlp_backward",
    )(kernel_far, grad_seq, by_seq, slope, counts, mid, norms, *up_w)

    def gradient(name, *pairs):
        cols = [right.shape[1] // groups for _, right in pairs]
        return pl.pallas_call(
            weight_gradient,
            grid=(groups,),
            in_specs=[SMEM] + [
                spec
                for wide in cols
                for spec in (
                    fixed((rows, width)), pl.BlockSpec((rows, wide), lambda i: (0, i))
                )
            ],
            out_specs=(ANY,) * 4,
            out_shape=quarters_of(sum(cols)),
            scratch_shapes=[pltpu.VMEM((width, rows), BF16) for _ in pairs]
            + [pltpu.VMEM((2, width, sum(cols)), BF16), pltpu.SemaphoreType.DMA((2,))],
            compiler_params=params(),
            cost_estimate=cost(2 * rows * width * groups * 900, 10e6),
            name=name,
        )(kernel_far, *(part for pair in pairs for part in pair))

    dmid, sum_down.received = join(dmid, sum_down.received)
    sum_down.first()
    (h2_ready,) = after([h2], sum_down.going)
    up_parts = gradient("up_gradient", (h2_ready, dup), (dmid_low, heads))
    *up_parts, sum_down.received = join(*up_parts, sum_down.received)
    sum_up = sum_of(up_parts)
    sum_down.far_half()
    (sum_up.from_across,) = after([sum_up.from_across], sum_down.going)
    sum_up.second()

    (x_ready,) = after([x], sum_up.going)
    dproj, input_grad, sums_one = pl.pallas_call(
        functools.partial(attention_backward, seq_len=seq_len),
        grid=(tiles,),
        in_specs=[
            SMEM, rows_of(width), keys_spec, norm_spec, rows_of(3 * width), lse_spec,
            rows_of(width), rows_of(width), ANY, ANY, ANY, ANY,
        ],
        out_specs=(rows_of(groups * 5 * LANES), rows_of(width), fixed((2, width))),
        out_shape=(
            shape_of(rows, groups * 5 * LANES), shape_of(rows, width, dtype=F32),
            shape_of(2, width, dtype=F32),
        ),
        scratch_shapes=weight_scratch(packed),
        compiler_params=params(),
        cost_estimate=cost(2 * rows * width * groups * 1300, 20e6),
        name="attention_backward",
    )(kernel_far, x_ready, live_keys, norms, proj, lse, dmid, dmid_low, *attention_w)

    def exchanged(values, bit):
        return swap(values, [i ^ bit for i in range(count)])

    if far_digits(count) == [(8, 4)]:
        sums_one, sum_up.received, sum_down.received = join(
            sums_one, sum_up.received, sum_down.received
        )
    sum_down.far_rest()
    norm_sum = jnp.concatenate([sums_one, sums_two], axis=0)
    received = exchanged(norm_sum, 1)
    sum_up.first()
    (received,) = after([received], sum_up.going)
    norm_sum = norm_sum + received
    received = exchanged(norm_sum, 8)
    (h1_ready,) = after([h1_turned], sum_up.going, sum_down.going, norm_sum)
    attention_parts = pl.pallas_call(
        turned_gradient,
        grid=(groups,),
        in_specs=[
            SMEM, fixed((width, rows)), pl.BlockSpec((rows, 5 * LANES), lambda i: (0, i))
        ],
        out_specs=(ANY,) * 4,
        out_shape=quarters_of(5 * LANES),
        scratch_shapes=[pltpu.VMEM((2, width, 5 * LANES), BF16), pltpu.SemaphoreType.DMA((2,))],
        compiler_params=params(),
        cost_estimate=cost(2 * rows * width * groups * 900, 10e6),
        name="attention_gradient",
    )(kernel_far, h1_ready, dproj)
    *attention_parts, received, sum_up.received, sum_down.keep[-1] = join(
        *attention_parts, received, sum_up.received, sum_down.keep[-1]
    )
    norm_sum = norm_sum + received
    sum_attention = sum_of(attention_parts)
    sum_attention.second()
    (norm_sum,) = after([norm_sum], sum_attention.going)
    sum_up.far(sum_attention.going)
    received = exchanged(norm_sum, 16) if count > 16 else jnp.zeros_like(norm_sum)
    sum_down.keep = after(sum_down.keep, sum_attention.going)
    grad_down, down_left_new, down_right_new, down_new = shampoo(
        shampoo_kernel, sum_down.keep, (w_down,), ((owned, ff),),
        (down_left, down_right, down_left_root, down_right_root),
    )
    sum_attention.received, received, *sooner = join(
        *after([sum_attention.received, received, *sum_up.keep[:-1]], down_new)
    )
    sum_up.keep = [*sooner, sum_up.keep[-1]]
    norm_sum = norm_sum + received
    sum_attention.first()
    received = exchanged(norm_sum, 2)
    (sum_up.keep[-1],) = after([sum_up.keep[-1]], sum_attention.going)
    sum_attention.received, sum_up.keep[-1], received = join(
        sum_attention.received, sum_up.keep[-1], received
    )
    norm_sum = norm_sum + received
    sum_attention.far()
    sum_up.keep = after(sum_up.keep, sum_attention.going)
    (
        grad_up, up_left_new, up_right_new, up_new, grad_out, out_left_new, out_right_new, out_new
    ) = shampoo(
        up_shampoo, sum_up.keep, (w_up, w_out), ((owned, ff), (owned, width_of(w_out))),
        (
            up_left, up_right, up_left_root, up_right_root,
            out_left, out_right, out_left_root, out_right_root,
        ),
    )
    bit = 32
    while bit < count:
        norm_sum = norm_sum + exchanged(norm_sum, bit)
        bit *= 2
    (received,) = after([exchanged(norm_sum, 4)], up_new)
    norm_sum = norm_sum + received
    grad_norm = lax.dynamic_slice_in_dim(norm_sum, dp_index * owned, owned, 1).T
    norm_second_new = STAT_DECAY * norm_second + (1.0 - STAT_DECAY) * grad_norm * grad_norm
    own_params = lax.dynamic_slice_in_dim(norm_params, dp_index * owned, owned, 0)
    norm_new = own_params - NORM_RATE * grad_norm / (jnp.sqrt(norm_second_new) + 1e-08)
    *sum_attention.keep, grad_norm, norm_second_new, norm_new = join(
        *sum_attention.keep, grad_norm, norm_second_new, norm_new
    )
    qkv_turned = w_qkv.transpose(1, 0, 2)
    grad_qkv, qkv_left_new, qkv_right_new, qkv_new = shampoo(
        attention_shampoo, sum_attention.keep, (qkv_turned,), ((owned, 3 * w_qkv.shape[2]),),
        (qkv_left, qkv_right, qkv_left_root, qkv_right_root), limit=SMALL_BYTES,
    )
    grad_qkv, qkv_new = grad_qkv.transpose(1, 0, 2), qkv_new.transpose(1, 0, 2)
    (
        qkv_left_new, qkv_right_new, out_left_new, out_right_new,
        up_left_new, up_right_new, down_left_new, down_right_new,
    ) = (
        stat[None, None]
        for stat in (
            qkv_left_new, qkv_right_new, out_left_new, out_right_new,
            up_left_new, up_right_new, down_left_new, down_right_new,
        )
    )
    return (
        block_out.reshape(block_in.shape),
        input_grad.reshape(block_in.shape),
        loss[:, 0].reshape(micros, seqs),
        grad_qkv, qkv_left_new, qkv_right_new, qkv_new,
        grad_out, out_left_new, out_right_new, out_new,
        grad_up, up_left_new, up_right_new, up_new,
        grad_down, down_left_new, down_right_new, down_new,
        grad_norm, norm_second_new, norm_new,
    )


def solution(mesh):
    sequence = P(None, AXES)
    stat = P("dp", "mp", None, None)
    weight = P("dp", "mp")
    qkv = P("dp", None, "mp")
    norm = P("dp", None)
    in_specs = (sequence, sequence, sequence, qkv, weight, weight, weight, P(), norm) + (stat,) * 16
    out_specs = (
        (sequence, sequence, sequence)
        + (qkv, stat, stat, qkv)
        + (weight, stat, stat, weight) * 3
        + (norm, norm, norm)
    )
    return jax.shard_map(
        per_device, mesh=mesh, in_specs=in_specs, out_specs=out_specs, check_vma=False
    )
```
